32 devices in a mesh: fsdp: 8 (over z, y), seq: 4 (over x, core).
Axes of the slice: x: 2, y: 2, z: 4, core: 2. Of those that a mesh axis runs over, the one named last changes fastest.
Arguments:
- images: bfloat16 [16, 1376, 1024], P('fsdp', 'seq'), may hold values from -6 to 6
- cotangent: bfloat16 [16, 1376, 1024], P('fsdp', 'seq'), may hold values from -6 to 6
- valid_count: int32 [16], P('fsdp'), may hold values from 1370 to 1373
- first_gain: bfloat16 [1024], P('fsdp'), may hold values from 0.25 to 1.75
- first_shift: bfloat16 [1024], P('fsdp'), may hold values from -3 to 3
- triple_weight: bfloat16 [1024, 3072], P('fsdp'), may hold values from -0.25 to 0.25
- query_bias: bfloat16 [1024], P('fsdp'), may hold values from -3 to 3
- value_bias: bfloat16 [1024], P('fsdp'), may hold values from -3 to 3
- output_weight: bfloat16 [1024, 1024], P('fsdp'), may hold values from -0.75 to 0.75
- output_bias: bfloat16 [1024], P('fsdp'), may hold values from -3 to 3
- attend_scale: bfloat16 [1024], P('fsdp'), may hold values from 0.5 to 1.5
- second_gain: bfloat16 [1024], P('fsdp'), may hold values from 0.25 to 1.75
- second_shift: bfloat16 [1024], P('fsdp'), may hold values from -3 to 3
- expand_weight: bfloat16 [1024, 4096], P('fsdp'), may hold values from -0.1875 to 0.1875
- expand_bias: bfloat16 [4096], P('fsdp'), may hold values from -3 to 3
- reduce_weight: bfloat16 [4096, 1024], P('fsdp'), may hold values from -0.09375 to 0.09375
- reduce_bias: bfloat16 [1024], P('fsdp'), may hold values from -3 to 3
- feed_scale: bfloat16 [1024], P('fsdp'), may hold values from 0.5 to 1.5
Outputs:
- outputs: bfloat16 [16, 1376, 1024], P('fsdp', 'seq')
- grad_images: float32 [16, 1376, 1024], P('fsdp', 'seq')
- grad_first_gain: float32 [1024], P('fsdp')
- grad_first_shift: float32 [1024], P('fsdp')
- grad_triple_weight: float32 [1024, 3072], P('fsdp')
- grad_query_bias: float32 [1024], P('fsdp')
- grad_value_bias: float32 [1024], P('fsdp')
- grad_output_weight: float32 [1024, 1024], P('fsdp')
- grad_output_bias: float32 [1024], P('fsdp')
- grad_attend_scale: float32 [1024], P('fsdp')
- grad_second_gain: float32 [1024], P('fsdp')
- grad_second_shift: float32 [1024], P('fsdp')
- grad_expand_weight: float32 [1024, 4096], P('fsdp')
- grad_expand_bias: float32 [4096], P('fsdp')
- grad_reduce_weight: float32 [4096, 1024], P('fsdp')
- grad_reduce_bias: float32 [1024], P('fsdp')
- grad_feed_scale: float32 [1024], P('fsdp')
The draws below stay inside these ranges and needn't reach their ends.
Inputs may be any that keep to these rules, and one draw needn't show every extreme that they name: `valid_count`: the number of live tokens of each image; its positions from there to 1376 are padding, masked as keys.
All inputs are finite; a program needn't handle non-finite values.
Results may differ from the reference program's by a relative error of at most 0.018.
Values may be sent and summed in bfloat16 or wider, within the bound.
No kernel may reach another device: no remote copies, remote signals or barrier semaphores. Data moves between devices by JAX's collectives and lax.ppermute only.
A program may use at most 256 MiB of HBM per device.

```python
import jax
import jax.numpy as jnp
from jax import lax

D = 1024
HEADS = 16
HEAD_DIM = 64
FF = 4096
LEN = 1376
IMAGES = 16


def set_ends(values, rng, smallest, largest):
    longest = values.shape.index(max(values.shape))
    spots = []
    for shift in (0, 1):
        where = [jax.random.randint(jax.random.fold_in(rng, axis), (), 0, length) for axis, length in enumerate(values.shape)]
        where[longest] = (where[longest] + shift) % values.shape[longest]
        spots.append(tuple(where))
    return values.at[spots[0]].set(smallest).at[spots[1]].set(largest)


def block_scale(stream_key, dims, pieces, low, high):
    factor_of, own = 1.0, jax.random.fold_in(stream_key, 6)
    for dim, parts in pieces:
        heights = jnp.exp(jax.random.uniform(jax.random.fold_in(own, dim), (parts,), jnp.float32, low / len(pieces), high / len(pieces)))
        factor_of = factor_of * jnp.repeat(heights, dims[dim] // parts).reshape([-1 if axis == dim else 1 for axis in range(len(dims))])
    return factor_of


def centred(rng, extent, spread, limit, cuts=(), kind=jnp.bfloat16):
    drawn = jax.random.normal(rng, extent, jnp.float32) * spread
    if len(cuts) > 0:
        drawn = block_scale(rng, extent, cuts, -0.22, 0.18) * drawn
    return jnp.clip(drawn, min=-limit, max=limit).astype(kind)


def setup_inputs(seed: int = 0) -> dict:
    seeds = jax.random.split(jax.random.key(seed), 19)
    return {
        "images": centred(seeds[0], (IMAGES, LEN, D), 1.0, 6.0, ((0, 8), (1, 4))),
        "cotangent": centred(seeds[1], (IMAGES, LEN, D), 1.0, 6.0, ((0, 8), (1, 4))),
        "valid_count": set_ends(jax.random.randint(seeds[2], (IMAGES,), LEN - 6, LEN - 2), jax.random.fold_in(seeds[2], 1), LEN - 6, (LEN - 2) - 1).astype(jnp.int32),
        "first_gain": jnp.clip(1.0 + 0.15 * jax.random.normal(seeds[3], (D,), jnp.float32), 0.25, 1.75).astype(jnp.bfloat16),
        "first_shift": centred(seeds[4], (D,), 0.3, 3.0, ((0, 8),)),
        "triple_weight": centred(seeds[5], (D, 3 * D), (D // 2) ** -0.5, 0.25, ((0, 8),)),
        "query_bias": centred(seeds[6], (D,), 0.5, 3.0, ((0, 8),)),
        "value_bias": centred(seeds[7], (D,), 0.5, 3.0, ((0, 8),)),
        "output_weight": centred(seeds[8], (D, D), (D // 16) ** -0.5, 0.75, ((0, 8),)),
        "output_bias": centred(seeds[9], (D,), 0.3, 3.0, ((0, 8),)),
        "attend_scale": jnp.clip(0.5 + 1.0 * jax.random.uniform(seeds[10], (D,), jnp.float32) ** block_scale(seeds[10], (D,), ((0, 8),), -0.2, 0.2), 0.5, 1.5).astype(jnp.bfloat16),
        "second_gain": jnp.clip(1.0 + 0.15 * jax.random.normal(seeds[11], (D,), jnp.float32), 0.25, 1.75).astype(jnp.bfloat16),
        "second_shift": centred(seeds[12], (D,), 0.3, 3.0, ((0, 8),)),
        "expand_weight": centred(seeds[13], (D, FF), D ** -0.5, 0.1875, ((0, 8),)),
        "expand_bias": centred(seeds[14], (FF,), 0.5, 3.0, ((0, 8),)),
        "reduce_weight": centred(seeds[15], (FF, D), FF ** -0.5, 0.09375, ((0, 8),)),
        "reduce_bias": centred(seeds[16], (D,), 0.3, 3.0, ((0, 8),)),
        "feed_scale": jnp.clip(0.5 + 1.0 * jax.random.uniform(seeds[17], (D,), jnp.float32) ** block_scale(seeds[17], (D,), ((0, 8),), -0.2, 0.2), 0.5, 1.5).astype(jnp.bfloat16),
    }


@jax.custom_vjp
def low(v):
    return lax.optimization_barrier(v.astype(jnp.bfloat16)).astype(jnp.float32)

@jax.custom_vjp
def low_back(v):
    return v

def low_keep(v):
    return (low(v), None)

def low_pass(kept, grad):
    return (grad,)

def back_keep(v):
    return (v, None)

def back_low(kept, grad):
    return (low(grad),)
low.defvjp(low_keep, low_pass)
low_back.defvjp(back_keep, back_low)
EPSILON = 1e-06

def layer_norm(inputs, gain, shift):
    average = lax.optimization_barrier(jnp.mean(inputs, -1, keepdims=True))
    centered = inputs - average
    variance = lax.optimization_barrier(jnp.mean(centered * centered, -1, keepdims=True))
    return centered * lax.rsqrt(variance + EPSILON) * gain + shift

def matmul(left, right):
    return jnp.dot(left, right, precision=lax.Precision.HIGHEST, preferred_element_type=jnp.float32)

def attend_image(bundle):
    queries, key_rows, value_rows, live_count = bundle
    factor = HEAD_DIM ** (-0.5)
    scores = jnp.einsum('qhd,khd->hqk', queries, key_rows, precision=lax.Precision.HIGHEST) * factor
    scores = low_back(scores)
    live_keys = lax.broadcasted_iota(jnp.int32, (1, 1, LEN), 2) < live_count
    scores = jnp.where(live_keys, scores, -1e+30)
    highest = lax.optimization_barrier(jnp.max(scores, -1, keepdims=True))
    powers = jnp.exp(scores - highest)
    probs = powers / lax.optimization_barrier(jnp.sum(powers, -1, keepdims=True))
    return jnp.einsum('hqk,khd->qhd', low(probs), value_rows, precision=lax.Precision.HIGHEST)

def forward(inputs, first_gain, first_shift, triple_weight, query_bias, value_bias, output_weight, output_bias, attend_scale, second_gain, second_shift, expand_weight, expand_bias, reduce_weight, reduce_bias, feed_scale, valid_count):
    token_rows = inputs.reshape(-1, D)
    first_normed = low(layer_norm(token_rows, first_gain, first_shift))
    joint_bias = jnp.concatenate([query_bias, jnp.zeros_like(query_bias), value_bias])
    triple = low(low_back(matmul(first_normed, triple_weight) + joint_bias))
    triple = triple.reshape(IMAGES, LEN, 3, HEADS, HEAD_DIM)
    attended = lax.map(jax.checkpoint(attend_image), (triple[:, :, 0], triple[:, :, 1], triple[:, :, 2], valid_count))
    attended = low(low_back(attended.reshape(-1, D)))
    branch_attend = low_back(matmul(attended, output_weight) + output_bias)
    residual = token_rows + attend_scale * branch_attend
    second_normed = low(layer_norm(residual, second_gain, second_shift))
    expanded = low_back(matmul(second_normed, expand_weight) + expand_bias)
    activated = low(jax.nn.gelu(expanded, approximate=False))
    branch_feed = low_back(matmul(activated, reduce_weight) + reduce_bias)
    return (residual + feed_scale * branch_feed).reshape(IMAGES, LEN, D)

def reference(images, cotangent, valid_count, first_gain, first_shift, triple_weight, query_bias, value_bias, output_weight, output_bias, attend_scale, second_gain, second_shift, expand_weight, expand_bias, reduce_weight, reduce_bias, feed_scale):
    params = (first_gain, first_shift, triple_weight, query_bias, value_bias, output_weight, output_bias, attend_scale, second_gain, second_shift, expand_weight, expand_bias, reduce_weight, reduce_bias, feed_scale)
    params = tuple((param.astype(jnp.float32) for param in params))
    inputs = images.astype(jnp.float32)

    def layer(inputs, *weights):
        return forward(inputs, *weights, valid_count)
    result, pull = jax.vjp(layer, inputs, *params)
    grads = pull(cotangent.astype(jnp.float32))
    return (result.astype(jnp.bfloat16), grads[0], grads[1], grads[2], grads[3], grads[4], grads[5], grads[6], grads[7], grads[8], grads[9], grads[10], grads[11], grads[12], grads[13], grads[14], grads[15])
```

```python
import functools

import jax
import jax.numpy as jnp
from jax import lax
from jax.experimental import pallas as pl
from jax.experimental.pallas import tpu as pltpu
from jax.sharding import Mesh, PartitionSpec as P

HEAD_DIM = 64
EPSILON = 1e-06
BF = jnp.bfloat16
F32 = jnp.float32
MASKED = -1e30


def dot(left, right):
    return lax.dot_general(left, right, (((1,), (0,)), ((), ())), preferred_element_type=F32)


def dot_left_t(left, right):
    return lax.dot_general(left, right, (((0,), (0,)), ((), ())), preferred_element_type=F32)


def dot_right_t(left, right):
    return lax.dot_general(left, right, (((1,), (1,)), ((), ())), preferred_element_type=F32)


def column_total(array):
    return dot(jnp.ones((8, array.shape[0]), BF), array)[0]


def normalize(rows):
    average = jnp.mean(rows, -1, keepdims=True)
    centered = rows - average
    variance = jnp.mean(centered * centered, -1, keepdims=True)
    factor = lax.rsqrt(variance + EPSILON)
    return centered * factor, factor


def normalize_back(normal, factor, weighted):
    return factor * (
        weighted
        - jnp.mean(weighted, -1, keepdims=True)
        - normal * jnp.mean(weighted * normal, -1, keepdims=True)
    )


def spans(total, step):
    return [(start, min(step, total - start)) for start in range(0, total, step)]


def merge(ref, out):
    pieces, _, rows, _ = ref.shape
    for piece in range(pieces):
        out[pl.ds(piece * rows, rows), :] = ref[piece, 0].astype(F32)


def lane_parts(block, heads, head):
    lane = lax.broadcasted_iota(jnp.int32, (1, block), 1)
    if heads == 1:
        return lane < HEAD_DIM, lane - HEAD_DIM
    if head == 0:
        return lane < HEAD_DIM, lane - HEAD_DIM
    return lane >= HEAD_DIM, lane


def split_three(values):
    high = values.astype(BF).astype(F32)
    rest = values - high
    middle = rest.astype(BF).astype(F32)
    return high, middle, rest - middle


def dead_column(limit_ref, length):
    image = pl.program_id(0)
    row = lax.broadcasted_iota(jnp.int32, (length, 1), 0)
    dead = (row >= limit_ref[image, 0]) & (row < limit_ref[image, 1])
    return jnp.where(dead, MASKED, 0.0)


def attend_forward_kernel(limit_ref, q_ref, k_ref, v_ref, out_ref, log_ref, q_s, k_s, v_s, o_s):
    pieces, _, rows, block = q_ref.shape
    length = pieces * rows
    heads = max(block // HEAD_DIM, 1)
    merge(q_ref, q_s)
    merge(k_ref, k_s)
    merge(v_ref, v_s)
    dead = dead_column(limit_ref, length)
    aug = []
    for head in range(heads):
        own, spare = lane_parts(2 * HEAD_DIM, heads, head)
        q = jnp.where(own, q_s[...] * 0.125, jnp.where(spare == 0, 1.0, 0.0)).astype(BF)
        k = jnp.where(own, k_s[...], jnp.where(spare == 0, dead, 0.0)).astype(BF)
        v = jnp.where(own, v_s[...], jnp.where(spare == 0, 1.0, 0.0)).astype(BF)
        aug.append((q, k, v))
    for start, size in spans(length, 352):
        results = []
        for head in range(heads):
            q, k, v = aug[head]
            scores = dot_right_t(q[start : start + size], k)
            top = jnp.max(scores, -1, keepdims=True)
            powers = jnp.exp(scores - top).astype(BF)
            mixed = dot(powers, v)
            own, spare = lane_parts(2 * HEAD_DIM, heads, head)
            at = HEAD_DIM if head == 0 else 0
            total = mixed[:, at : at + 1]
            results.append((mixed / total, top + jnp.log(total)))
        own, _ = lane_parts(2 * HEAD_DIM, heads, 0)
        if heads == 1:
            o_s[pl.ds(start, size), :] = results[0][0]
            log_ref[0, 0, pl.ds(start, size), :] = jnp.broadcast_to(
                results[0][1], (size, 2 * HEAD_DIM)
            )
        else:
            o_s[pl.ds(start, size), :] = jnp.where(own, results[0][0], results[1][0])
            log_ref[0, 0, pl.ds(start, size), :] = jnp.where(own, results[1][1], results[0][1])
    for piece in range(pieces):
        out_ref[piece, 0] = o_s[pl.ds(piece * rows, rows), :].astype(BF)


def attend_backward_kernel(
    limit_ref, q_ref, k_ref, v_ref, o_ref, g_ref, log_ref, dq_ref, dk_ref, dv_ref,
    q_s, k_s, v_s, o_s, g_s, dq_s, dk_s, dv_s,
):
    pieces, _, rows, block = q_ref.shape
    length = pieces * rows
    heads = max(block // HEAD_DIM, 1)
    merge(q_ref, q_s)
    merge(k_ref, k_s)
    merge(v_ref, v_s)
    merge(o_ref, o_s)
    merge(g_ref, g_s)
    dead = dead_column(limit_ref, length)
    product = o_s[...] * g_s[...]
    for head in range(heads):
        own, spare = lane_parts(2 * HEAD_DIM, heads, head)
        log_parts = split_three(log_ref[0, 0])
        inner = jnp.sum(jnp.where(own, product, 0.0), -1, keepdims=True)
        inner_parts = split_three(inner)
        zero = jnp.zeros((length, 2 * HEAD_DIM), F32)
        q_tail, k_tail, v_tail, g_tail = zero, zero, zero, zero
        for place in range(3):
            q_tail = jnp.where(spare == place, -log_parts[place], q_tail)
            g_tail = jnp.where(spare == place, -inner_parts[place], g_tail)
            k_tail = jnp.where(spare == place, 1.0, k_tail)
            v_tail = jnp.where(spare == place, 1.0, v_tail)
        q_tail = jnp.where(spare == 3, 1.0, q_tail)
        k_tail = jnp.where(spare == 3, dead, k_tail)
        q = jnp.where(own, q_s[...] * 0.125, q_tail).astype(BF)
        k = jnp.where(own, k_s[...], k_tail).astype(BF)
        v = jnp.where(own, v_s[...], v_tail).astype(BF)
        g = jnp.where(own, g_s[...], g_tail).astype(BF)
        k_t = jnp.where(own, k_s[...] * 0.125, 0.0).T.astype(BF)
        dk = dv = None
        for start, size in spans(length, 512):
            q_part, g_part = q[start : start + size], g[start : start + size]
            probs = jnp.exp(dot_right_t(k, q_part))
            slopes = (probs * dot_right_t(v, g_part)).astype(BF)
            probs = probs.astype(BF)
            dv_part = dot(probs, g_part)
            dk_part = dot(slopes, q_part)
            dv = dv_part if dv is None else dv + dv_part
            dk = dk_part if dk is None else dk + dk_part
            dq_part = dot(k_t, slopes).T
            if head == 0:
                dq_s[pl.ds(start, size), :] = dq_part
            else:
                dq_s[pl.ds(start, size), :] += dq_part
        if head == 0:
            dk_s[...] = dk
            dv_s[...] = dv
        else:
            dk_s[...] = jnp.where(own, dk, dk_s[...])
            dv_s[...] = jnp.where(own, dv, dv_s[...])
    for piece in range(pieces):
        part = pl.ds(piece * rows, rows)
        dq_ref[piece, 0] = dq_s[part, :].astype(BF)
        dk_ref[piece, 0] = dk_s[part, :].astype(BF)
        dv_ref[piece, 0] = dv_s[part, :].astype(BF)


def attend_specs(pieces, rows, first):
    def at(limit_index):
        return pl.BlockSpec(
            (pieces, 1, rows, 2 * HEAD_DIM),
            lambda image, pair, limits: (0, image, 0, limit_index + pair),
        )

    return at(first)


def attend_forward(triple, limits):
    pieces, images, rows, columns = triple.shape
    head_width = columns // 3
    length = pieces * rows
    pairs = head_width // (2 * HEAD_DIM)
    wide = pltpu.VMEM((length, 2 * HEAD_DIM), F32)
    spec = functools.partial(attend_specs, pieces, rows)
    heads = images * head_width // HEAD_DIM
    return pl.pallas_call(
        attend_forward_kernel,
        grid_spec=pltpu.PrefetchScalarGridSpec(
            num_scalar_prefetch=1,
            grid=(images, pairs),
            in_specs=[spec(0), spec(pairs), spec(2 * pairs)],
            out_specs=[
                spec(0),
                pl.BlockSpec((1, 1, length, 2 * HEAD_DIM), lambda i, p, limits: (i, p, 0, 0)),
            ],
            scratch_shapes=[wide] * 4,
        ),
        out_shape=[
            jax.ShapeDtypeStruct((pieces, images, rows, head_width), BF),
            jax.ShapeDtypeStruct((images, pairs, length, 2 * HEAD_DIM), F32),
        ],
        compiler_params=pltpu.CompilerParams(vmem_limit_bytes=50 * 2**20),
        cost_estimate=pl.CostEstimate(
            flops=heads * length * length * 1024,
            bytes_accessed=4 * triple.size,
            transcendentals=heads * length * length,
        ),
        name="attend_forward",
    )(limits, triple, triple, triple)


def attend_backward(triple, attended, grad, logs, limits):
    pieces, images, rows, columns = triple.shape
    head_width = columns // 3
    length = pieces * rows
    pairs = head_width // (2 * HEAD_DIM)
    wide = pltpu.VMEM((length, 2 * HEAD_DIM), F32)
    spec = functools.partial(attend_specs, pieces, rows)
    shape = jax.ShapeDtypeStruct((pieces, images, rows, head_width), BF)
    heads = images * head_width // HEAD_DIM
    return pl.pallas_call(
        attend_backward_kernel,
        grid_spec=pltpu.PrefetchScalarGridSpec(
            num_scalar_prefetch=1,
            grid=(images, pairs),
            in_specs=[
                spec(0),
                spec(pairs),
                spec(2 * pairs),
                spec(0),
                spec(0),
                pl.BlockSpec((1, 1, length, 2 * HEAD_DIM), lambda i, p, limits: (i, p, 0, 0)),
            ],
            out_specs=[spec(0)] * 3,
            scratch_shapes=[wide] * 8,
        ),
        out_shape=[shape] * 3,
        compiler_params=pltpu.CompilerParams(vmem_limit_bytes=56 * 2**20),
        cost_estimate=pl.CostEstimate(
            flops=heads * length * length * 2560,
            bytes_accessed=8 * triple.size,
            transcendentals=heads * length * length,
        ),
        name="attend_backward",
    )(limits, triple, triple, triple, attended, grad, logs)


def gelu_parts(values):
    size = jnp.abs(values) * 0.7071067811865476
    bell = jnp.exp(-size * size)
    t = 1.0 / (1.0 + 0.3275911 * size)
    tail = t * (
        0.254829592
        + t * (-0.284496736 + t * (1.421413741 + t * (-1.453152027 + t * 1.061405429)))
    )
    tail = 0.5 * tail * bell
    return jnp.where(values >= 0.0, 1.0 - tail, tail), 0.3989422804014327 * bell


def expand_kernel(rows_ref, weight_ref, bias_ref, active_ref, slope_ref):
    count = rows_ref.shape[0]
    for start, size in spans(count, 352):
        expanded = dot(rows_ref[start : start + size, :], weight_ref[...]) + bias_ref[...]
        below, density = gelu_parts(expanded)
        active_ref[start : start + size, :] = (expanded * below).astype(BF)
        slope_ref[start : start + size, :] = (below + expanded * density).astype(BF)


def expand_rows(rows, weight, bias):
    count, width = rows.shape
    units = weight.shape[1]
    tile = 256
    shape = jax.ShapeDtypeStruct((count, units), BF)
    return pl.pallas_call(
        expand_kernel,
        grid=(units // tile,),
        in_specs=[
            pl.BlockSpec((count, width), lambda i: (0, 0)),
            pl.BlockSpec((width, tile), lambda i: (0, i)),
            pl.BlockSpec((1, tile), lambda i: (0, i)),
        ],
        out_specs=[pl.BlockSpec((count, tile), lambda i: (0, i))] * 2,
        out_shape=[shape] * 2,
        compiler_params=pltpu.CompilerParams(vmem_limit_bytes=48 * 2**20),
        cost_estimate=pl.CostEstimate(
            flops=4 * count * units * width,
            bytes_accessed=2 * (count * width + width * units + 2 * count * units),
            transcendentals=2 * count * units,
        ),
        name="expand_rows",
    )(rows, weight, bias)


def far_send(array, shift):
    count = lax.axis_size("far")
    return lax.ppermute(array, "far", [(i, (i + shift) % count) for i in range(count)])


def far_gather(array):
    count = lax.axis_size("far")
    return [array] + [far_send(array, count - r) for r in range(1, count)]


def far_exchange(slots):
    count = len(slots)
    out = [slots[0]] + [None] * (count - 1)
    for r in range(1, count):
        out[count - r] = far_send(slots[r], r)
    return out


def far_sum(slots):
    arrived = far_exchange(slots)
    return sum(part.astype(F32) for part in arrived)


def other_core(array):
    return lax.ppermute(array, "core", [(0, 1), (1, 0)])


def fsdp_gather(array):
    return lax.all_gather(array, "fsdp", axis=0, tiled=True)


def fsdp_scatter(array):
    return lax.psum_scatter(array, "fsdp", scatter_dimension=0, tiled=True)


def core_join(mine, axis, core):
    other = other_core(mine)
    return jnp.stack(
        [jnp.where(core == 0, mine, other), jnp.where(core == 0, other, mine)], axis
    )


def shards(
    images,
    cotangent,
    valid_count,
    first_gain,
    first_shift,
    triple_weight,
    query_bias,
    value_bias,
    output_weight,
    output_bias,
    attend_scale,
    second_gain,
    second_shift,
    expand_weight,
    expand_bias,
    reduce_weight,
    reduce_bias,
    feed_scale,
):
    image_count, local_len, width = images.shape
    own_rows = image_count * local_len
    far_count, fsdp_count = lax.axis_size("far"), lax.axis_size("fsdp")
    far, core = lax.axis_index("far"), lax.axis_index("core")
    seq_count = 2 * far_count
    shard = width // fsdp_count
    units = expand_weight.shape[1]
    unit_part = units // (2 * fsdp_count)
    near_heads = width // HEAD_DIM // seq_count
    head_width = near_heads * HEAD_DIM

    def my_heads(array, axis):
        shape = array.shape
        array = array.reshape(
            shape[:axis] + (far_count, near_heads, 2, HEAD_DIM) + shape[axis + 1 :]
        )
        array = lax.dynamic_index_in_dim(array, far, axis, False)
        array = lax.dynamic_index_in_dim(array, core, axis + 1, False)
        return array.reshape(shape[:axis] + (head_width,) + shape[axis + 1 :])

    triple_mine = my_heads(triple_weight.reshape(shard, 3, width), 2).reshape(shard, 3 * head_width)
    bias_mine = lax.dynamic_index_in_dim(expand_bias.reshape(2, unit_part), core, 0, False)
    bias_columns = unit_part // shard
    vectors = [
        first_gain, first_shift, query_bias, value_bias, output_bias, attend_scale,
        second_gain, second_shift, reduce_bias, feed_scale,
    ]
    vector_count = len(vectors)
    packed = jnp.concatenate(
        [triple_mine, jnp.stack(vectors, 1), bias_mine.reshape(shard, bias_columns)], 1
    )
    packed = jnp.pad(packed, ((0, 0), (0, -packed.shape[1] % 128)))
    packed = fsdp_gather(packed)
    triple_whole = packed[:, : 3 * head_width]
    small = packed[:, 3 * head_width : 3 * head_width + vector_count + bias_columns]
    small = small.astype(F32).T
    (gain_1, shift_1, bias_q, bias_v, bias_o, scale_a, gain_2, shift_2, bias_r, scale_f) = [
        small[i] for i in range(vector_count)
    ]
    bias_e = (
        small[vector_count:]
        .reshape(bias_columns, fsdp_count, shard)
        .transpose(1, 2, 0)
        .reshape(1, fsdp_count * unit_part)
    )

    split_output = shard % (2 * HEAD_DIM) == 0
    if split_output:
        output_mine = lax.dynamic_index_in_dim(
            output_weight.reshape(shard // (2 * HEAD_DIM), 2, HEAD_DIM, width), core, 1, False
        ).reshape(shard // 2, width)
        output_whole = fsdp_gather(output_mine)
    else:
        output_whole = lax.dynamic_index_in_dim(
            fsdp_gather(output_weight).reshape(-1, 2, HEAD_DIM, width), core, 1, False
        )
    output_whole = output_whole.reshape(far_count, head_width, width)
    output_whole = jnp.roll(output_whole, -far, 0).reshape(width // 2, width)
    expand_mine = lax.dynamic_index_in_dim(
        expand_weight.reshape(shard, fsdp_count, 2, unit_part), core, 2, False
    ).reshape(shard, units // 2)
    expand_whole = fsdp_gather(expand_mine)
    reduce_mine = lax.dynamic_index_in_dim(
        reduce_weight.reshape(2, unit_part, width), core, 0, False
    )
    reduce_whole = fsdp_gather(reduce_mine)

    mine = images.reshape(own_rows, width)
    slots = far_gather(mine)
    tokens = []
    for slot in slots:
        tokens += [slot, other_core(slot)]
    tokens = jnp.stack(tokens, 0).reshape(seq_count * own_rows, width)
    normal_1, factor_1 = normalize(tokens.astype(F32))
    first_normed = (normal_1 * gain_1 + shift_1).astype(BF)
    joint_bias = jnp.concatenate(
        [my_heads(bias_q, 0), jnp.zeros((head_width,), F32), my_heads(bias_v, 0)]
    )
    triple = (dot(first_normed, triple_whole) + joint_bias).astype(BF)

    last_slot = ((far_count - 1 - far) % far_count) * 2 + (1 - core)
    dead_from = last_slot * local_len + valid_count - (seq_count - 1) * local_len
    limits = jnp.stack(
        [dead_from, jnp.broadcast_to((last_slot + 1) * local_len, dead_from.shape)], 1
    ).astype(jnp.int32)

    direct = local_len % 8 == 0 and head_width % (2 * HEAD_DIM) == 0

    def to_kernel(array):
        array = array.reshape(seq_count, image_count, local_len, -1)
        if direct:
            return array
        parts = array.shape[-1] // head_width
        array = array.transpose(1, 0, 2, 3).reshape(
            1, image_count, seq_count * local_len, parts, head_width
        )
        lanes = -head_width % (2 * HEAD_DIM)
        array = jnp.pad(array, ((0, 0),) * 4 + ((0, lanes),))
        return array.reshape(1, image_count, seq_count * local_len, -1)

    def from_kernel(array):
        if direct:
            return array.reshape(seq_count * own_rows, -1)
        array = array[..., :head_width].reshape(image_count, seq_count, local_len, head_width)
        return array.transpose(1, 0, 2, 3).reshape(seq_count * own_rows, head_width)

    triple_in = to_kernel(triple)
    attended_in, logs = attend_forward(triple_in, limits)
    attended = from_kernel(attended_in).reshape(far_count, 2 * own_rows, head_width)
    attended = far_exchange([attended[r] for r in range(far_count)])
    attended_rows = jnp.concatenate(attended, 1)

    branch = dot(attended_rows, output_whole)
    branch_attend = (
        branch[:own_rows] + other_core(branch[own_rows:].astype(BF)).astype(F32) + bias_o
    )
    inputs = mine.astype(F32)
    residual = inputs + scale_a * branch_attend
    normal_2, factor_2 = normalize(residual)
    second_mine = (normal_2 * gain_2 + shift_2).astype(BF)
    second_normed = jnp.concatenate([second_mine, other_core(second_mine)], 0)
    activated, slope = expand_rows(second_normed, expand_whole, bias_e)
    branch = dot(activated, reduce_whole)
    branch_feed = (
        branch[:own_rows] + other_core(branch[own_rows:].astype(BF)).astype(F32) + bias_r
    )
    outputs = residual + scale_f * branch_feed

    cotangent = cotangent.reshape(own_rows, width)
    upstream = cotangent.astype(F32)
    both = jnp.concatenate([cotangent, other_core(cotangent)], 0)
    grad_feed = (scale_f * both.astype(F32)).astype(BF)
    grad_feed_scale = jnp.sum(upstream * branch_feed, 0)
    grad_reduce_bias = column_total(grad_feed[:own_rows])
    grad_reduce_weight = fsdp_scatter(dot_left_t(activated, grad_feed).astype(BF))
    grad_expanded = (dot_right_t(grad_feed, reduce_whole) * slope.astype(F32)).astype(BF)
    grad_expand_bias = column_total(grad_expanded)
    grad_expand_weight = fsdp_scatter(dot_left_t(second_normed, grad_expanded).astype(BF))
    partial = dot_right_t(grad_expanded, expand_whole)
    upper = partial[:own_rows] + other_core(partial[own_rows:].astype(BF)).astype(F32)
    grad_second_gain = jnp.sum(upper * normal_2, 0)
    grad_second_shift = jnp.sum(upper, 0)
    grad_residual = upstream + normalize_back(normal_2, factor_2, upper * gain_2)
    grad_attend_scale = jnp.sum(grad_residual * branch_attend, 0)
    grad_attend = (scale_a * grad_residual).astype(BF)
    grad_output_bias = column_total(grad_attend)
    grad_attend = jnp.concatenate([grad_attend, other_core(grad_attend)], 0)
    grad_attended = dot_right_t(grad_attend, output_whole).astype(BF)
    grad_attended = far_exchange(
        [grad_attended[:, r * head_width : (r + 1) * head_width] for r in range(far_count)]
    )
    grad_attended = to_kernel(jnp.stack(grad_attended, 0))
    grad_output_weight = dot_left_t(attended_rows, grad_attend).astype(BF)
    grad_output_weight = jnp.roll(
        grad_output_weight.reshape(far_count, head_width, width), far, 0
    ).reshape(width // 2, width)

    pieces = attend_backward(triple_in, attended_in, grad_attended, logs, limits)
    grad_triple = jnp.concatenate([from_kernel(piece) for piece in pieces], 1)

    partial = dot_right_t(grad_triple, triple_whole)
    grad_first_gain = jnp.sum(partial * normal_1, 0)
    grad_first_shift = jnp.sum(partial, 0)
    partial = partial.astype(BF).reshape(far_count, 2, own_rows, width)
    partial = partial[:, 0].astype(F32) + other_core(partial[:, 1]).astype(F32)
    partial = partial.astype(BF)
    upper = far_sum([partial[r] for r in range(far_count)])
    normal, factor = normalize(inputs)
    grad_images = grad_residual + normalize_back(normal, factor, upper * gain_1)

    column_sums = column_total(grad_triple)

    def place_heads(vector):
        here = jnp.arange(far_count)[:, None, None, None] == far
        here = here & (jnp.arange(2)[None, None, :, None] == core)
        vector = vector.reshape(1, near_heads, 1, HEAD_DIM)
        return jnp.where(here, vector, 0.0).reshape(width)

    def place_units(vector):
        vector = vector.reshape(fsdp_count, shard, bias_columns)
        vector = vector.transpose(2, 0, 1).reshape(1, bias_columns, width)
        vector = jnp.where(jnp.arange(2)[:, None, None] == core, vector, 0.0)
        return [vector[i, j] for i in range(2) for j in range(bias_columns)]

    sums = [
        grad_first_gain, grad_first_shift,
        place_heads(column_sums[:head_width]), place_heads(column_sums[2 * head_width :]),
        grad_output_bias, grad_attend_scale, grad_second_gain, grad_second_shift,
        grad_reduce_bias, grad_feed_scale,
    ] + place_units(grad_expand_bias)
    sums = jnp.stack(sums, 0).astype(BF).T
    sums = jnp.pad(sums, ((0, 0), (0, -sums.shape[1] % 128)))
    grad_packed = jnp.concatenate([dot_left_t(first_normed, grad_triple).astype(BF), sums], 1)
    grad_packed = fsdp_scatter(grad_packed)
    grad_packed = lax.all_gather(grad_packed, ("far", "core"), axis=0, tiled=False)
    grad_packed = grad_packed.astype(F32)
    grad_triple_weight = (
        grad_packed[:, :, : 3 * head_width]
        .reshape(far_count, 2, shard, 3, near_heads, HEAD_DIM)
        .transpose(2, 3, 0, 4, 1, 5)
        .reshape(shard, 3 * width)
    )
    sums = jnp.sum(grad_packed[:, :, 3 * head_width :], 0).T

    def far_total(array):
        total = array.astype(F32)
        for r in range(1, far_count):
            total = total + far_send(array, r).astype(F32)
        return total

    if split_output:
        grad_output_weight = far_total(fsdp_scatter(grad_output_weight)).astype(BF)
        grad_output_weight = core_join(
            grad_output_weight.reshape(-1, HEAD_DIM, width), 1, core
        ).reshape(shard, width)
    else:
        spread = grad_output_weight.reshape(-1, 1, HEAD_DIM, width)
        spread = jnp.where(jnp.arange(2)[None, :, None, None] == core, spread, 0)
        spread = fsdp_scatter(spread.reshape(width, width))
        grad_output_weight = far_total(spread)
        grad_output_weight = grad_output_weight + other_core(grad_output_weight)
    grad_expand_weight = core_join(
        far_total(grad_expand_weight).astype(BF).reshape(shard, fsdp_count, unit_part), 2, core
    ).reshape(shard, units)
    grad_reduce_weight = core_join(far_total(grad_reduce_weight).astype(BF), 0, core).reshape(
        2 * unit_part, width
    )
    grad_expand_bias = (
        sums[10 : 10 + 2 * bias_columns]
        .reshape(2, bias_columns, shard)
        .transpose(0, 2, 1)
        .reshape(2 * unit_part)
    )
    return (
        outputs.reshape(image_count, local_len, width).astype(BF),
        grad_images.reshape(image_count, local_len, width),
        sums[0],
        sums[1],
        grad_triple_weight,
        sums[2],
        sums[3],
        grad_output_weight.astype(F32),
        sums[4],
        sums[5],
        sums[6],
        sums[7],
        grad_expand_weight.astype(F32),
        grad_expand_bias,
        grad_reduce_weight.astype(F32),
        sums[8],
        sums[9],
    )


def solution(mesh):
    fsdp, seq = mesh.devices.shape
    split = Mesh(mesh.devices.reshape(fsdp, seq // 2, 2), ("fsdp", "far", "core"))
    tokens = P("fsdp", ("far", "core"), None)
    row, matrix = P("fsdp"), P("fsdp", None)
    return jax.shard_map(
        shards,
        mesh=split,
        in_specs=(
            tokens, tokens, row, row, row, matrix, row, row, matrix,
            row, row, row, row, matrix, row, matrix, row, row,
        ),
        out_specs=(
            tokens, tokens, row, row, matrix, row, row, matrix,
            row, row, row, row, matrix, row, matrix, row, row,
        ),
        check_vma=False,
    )
```

```python
import functools

import jax
import jax.numpy as jnp
from jax import lax
from jax.experimental import pallas as pl
from jax.experimental.pallas import tpu as pltpu
from jax.sharding import Mesh, PartitionSpec as P

HEAD_DIM = 64
EPSILON = 1e-06
BF = jnp.bfloat16
F32 = jnp.float32
MASKED = -1e30


def dot(left, right):
    return lax.dot_general(left, right, (((1,), (0,)), ((), ())), preferred_element_type=F32)


def dot_left_t(left, right):
    return lax.dot_general(left, right, (((0,), (0,)), ((), ())), preferred_element_type=F32)


def dot_right_t(left, right):
    return lax.dot_general(left, right, (((1,), (1,)), ((), ())), preferred_element_type=F32)


def column_total(array):
    return dot(jnp.ones((8, array.shape[0]), BF), array)[0]


def normalize(rows):
    average = jnp.mean(rows, -1, keepdims=True)
    centered = rows - average
    variance = jnp.mean(centered * centered, -1, keepdims=True)
    factor = lax.rsqrt(variance + EPSILON)
    return centered * factor, factor


def normalize_back(normal, factor, weighted):
    return factor * (
        weighted
        - jnp.mean(weighted, -1, keepdims=True)
        - normal * jnp.mean(weighted * normal, -1, keepdims=True)
    )


def spans(total, step):
    return [(start, min(step, total - start)) for start in range(0, total, step)]


def merge(ref, out):
    pieces, _, rows, _ = ref.shape
    for piece in range(pieces):
        out[pl.ds(piece * rows, rows), :] = ref[piece, 0].astype(F32)


def lane_parts(block, heads, head):
    lane = lax.broadcasted_iota(jnp.int32, (1, block), 1)
    if heads == 1:
        return lane < HEAD_DIM, lane - HEAD_DIM
    if head == 0:
        return lane < HEAD_DIM, lane - HEAD_DIM
    return lane >= HEAD_DIM, lane


def split_three(values):
    high = values.astype(BF).astype(F32)
    rest = values - high
    middle = rest.astype(BF).astype(F32)
    return high, middle, rest - middle


def dead_column(limit_ref, length):
    image = pl.program_id(0)
    row = lax.broadcasted_iota(jnp.int32, (length, 1), 0)
    dead = (row >= limit_ref[image, 0]) & (row < limit_ref[image, 1])
    return jnp.where(dead, MASKED, 0.0)


def attend_forward_kernel(limit_ref, q_ref, k_ref, v_ref, out_ref, log_ref, q_s, k_s, v_s, o_s):
    pieces, _, rows, block = q_ref.shape
    length = pieces * rows
    heads = max(block // HEAD_DIM, 1)
    merge(q_ref, q_s)
    merge(k_ref, k_s)
    merge(v_ref, v_s)
    dead = dead_column(limit_ref, length)
    aug = []
    for head in range(heads):
        own, spare = lane_parts(2 * HEAD_DIM, heads, head)
        q = jnp.where(own, q_s[...] * 0.125, jnp.where(spare == 0, 1.0, 0.0)).astype(BF)
        k = jnp.where(own, k_s[...], jnp.where(spare == 0, dead, 0.0)).astype(BF)
        v = jnp.where(own, v_s[...], jnp.where(spare == 0, 1.0, 0.0)).astype(BF)
        aug.append((q, k, v))
    for start, size in spans(length, 352):
        results = []
        for head in range(heads):
            q, k, v = aug[head]
            scores = dot_right_t(q[start : start + size], k)
            top = jnp.max(scores, -1, keepdims=True)
            powers = jnp.exp(scores - top).astype(BF)
            mixed = dot(powers, v)
            own, spare = lane_parts(2 * HEAD_DIM, heads, head)
            at = HEAD_DIM if head == 0 else 0
            total = mixed[:, at : at + 1]
            results.append((mixed / total, top + jnp.log(total)))
        own, _ = lane_parts(2 * HEAD_DIM, heads, 0)
        if heads == 1:
            o_s[pl.ds(start, size), :] = results[0][0]
            log_ref[0, 0, pl.ds(start, size), :] = jnp.broadcast_to(
                results[0][1], (size, 2 * HEAD_DIM)
            )
        else:
            o_s[pl.ds(start, size), :] = jnp.where(own, results[0][0], results[1][0])
            log_ref[0, 0, pl.ds(start, size), :] = jnp.where(own, results[1][1], results[0][1])
    for piece in range(pieces):
        out_ref[piece, 0] = o_s[pl.ds(piece * rows, rows), :].astype(BF)


def attend_backward_kernel(
    limit_ref, q_ref, k_ref, v_ref, o_ref, g_ref, log_ref, grad_ref,
    q_s, k_s, v_s, o_s, g_s, dq_s, dk_s, dv_s,
):
    pieces, _, rows, block = q_ref.shape
    length = pieces * rows
    heads = max(block // HEAD_DIM, 1)
    merge(q_ref, q_s)
    merge(k_ref, k_s)
    merge(v_ref, v_s)
    merge(o_ref, o_s)
    merge(g_ref, g_s)
    dead = dead_column(limit_ref, length)
    product = o_s[...] * g_s[...]
    for head in range(heads):
        own, spare = lane_parts(2 * HEAD_DIM, heads, head)
        log_parts = split_three(log_ref[0, 0])
        inner = jnp.sum(jnp.where(own, product, 0.0), -1, keepdims=True)
        inner_parts = split_three(inner)
        zero = jnp.zeros((length, 2 * HEAD_DIM), F32)
        q_tail, k_tail, v_tail, g_tail = zero, zero, zero, zero
        for place in range(3):
            q_tail = jnp.where(spare == place, -log_parts[place], q_tail)
            g_tail = jnp.where(spare == place, -inner_parts[place], g_tail)
            k_tail = jnp.where(spare == place, 1.0, k_tail)
            v_tail = jnp.where(spare == place, 1.0, v_tail)
        q_tail = jnp.where(spare == 3, 1.0, q_tail)
        k_tail = jnp.where(spare == 3, dead, k_tail)
        q = jnp.where(own, q_s[...] * 0.125, q_tail).astype(BF)
        k = jnp.where(own, k_s[...], k_tail).astype(BF)
        v = jnp.where(own, v_s[...], v_tail).astype(BF)
        g = jnp.where(own, g_s[...], g_tail).astype(BF)
        k_t = jnp.where(own, k_s[...] * 0.125, 0.0).T.astype(BF)
        dk = dv = None
        for start, size in spans(length, 512):
            q_part, g_part = q[start : start + size], g[start : start + size]
            probs = jnp.exp(dot_right_t(k, q_part))
            slopes = (probs * dot_right_t(v, g_part)).astype(BF)
            probs = probs.astype(BF)
            dv_part = dot(probs, g_part)
            dk_part = dot(slopes, q_part)
            dv = dv_part if dv is None else dv + dv_part
            dk = dk_part if dk is None else dk + dk_part
            dq_part = dot(k_t, slopes).T
            if head == 0:
                dq_s[pl.ds(start, size), :] = dq_part
            else:
                dq_s[pl.ds(start, size), :] += dq_part
        if head == 0:
            dk_s[...] = dk
            dv_s[...] = dv
        else:
            dk_s[...] = jnp.where(own, dk, dk_s[...])
            dv_s[...] = jnp.where(own, dv, dv_s[...])
    stride = grad_ref.shape[3] // 3
    for piece in range(pieces):
        part = pl.ds(piece * rows, rows)
        for which, grad in enumerate((dq_s, dk_s, dv_s)):
            at = pl.multiple_of(which * stride + pl.program_id(1) * block, block)
            grad_ref[piece, 0, :, pl.ds(at, block)] = grad[part, :].astype(BF)


def attend_specs(pieces, rows, first):
    def at(limit_index):
        return pl.BlockSpec(
            (pieces, 1, rows, 2 * HEAD_DIM),
            lambda image, pair, limits: (0, image, 0, limit_index + pair),
        )

    return at(first)


def attend_forward(triple, limits):
    pieces, images, rows, columns = triple.shape
    head_width = columns // 3
    length = pieces * rows
    pairs = head_width // (2 * HEAD_DIM)
    wide = pltpu.VMEM((length, 2 * HEAD_DIM), F32)
    spec = functools.partial(attend_specs, pieces, rows)
    heads = images * head_width // HEAD_DIM
    return pl.pallas_call(
        attend_forward_kernel,
        grid_spec=pltpu.PrefetchScalarGridSpec(
            num_scalar_prefetch=1,
            grid=(images, pairs),
            in_specs=[spec(0), spec(pairs), spec(2 * pairs)],
            out_specs=[
                spec(0),
                pl.BlockSpec((1, 1, length, 2 * HEAD_DIM), lambda i, p, limits: (i, p, 0, 0)),
            ],
            scratch_shapes=[wide] * 4,
        ),
        out_shape=[
            jax.ShapeDtypeStruct((pieces, images, rows, head_width), BF),
            jax.ShapeDtypeStruct((images, pairs, length, 2 * HEAD_DIM), F32),
        ],
        compiler_params=pltpu.CompilerParams(vmem_limit_bytes=50 * 2**20),
        cost_estimate=pl.CostEstimate(
            flops=heads * length * length * 1024,
            bytes_accessed=4 * triple.size,
            transcendentals=heads * length * length,
        ),
        name="attend_forward",
    )(limits, triple, triple, triple)


def attend_backward(triple, attended, grad, logs, limits):
    pieces, images, rows, columns = triple.shape
    head_width = columns // 3
    length = pieces * rows
    pairs = head_width // (2 * HEAD_DIM)
    wide = pltpu.VMEM((length, 2 * HEAD_DIM), F32)
    spec = functools.partial(attend_specs, pieces, rows)
    heads = images * head_width // HEAD_DIM
    return pl.pallas_call(
        attend_backward_kernel,
        grid_spec=pltpu.PrefetchScalarGridSpec(
            num_scalar_prefetch=1,
            grid=(images, pairs),
            in_specs=[
                spec(0),
                spec(pairs),
                spec(2 * pairs),
                spec(0),
                spec(0),
                pl.BlockSpec((1, 1, length, 2 * HEAD_DIM), lambda i, p, limits: (i, p, 0, 0)),
            ],
            out_specs=pl.BlockSpec(
                (pieces, 1, rows, columns), lambda image, pair, limits: (0, image, 0, 0)
            ),
            scratch_shapes=[wide] * 8,
        ),
        out_shape=jax.ShapeDtypeStruct(triple.shape, BF),
        compiler_params=pltpu.CompilerParams(vmem_limit_bytes=56 * 2**20),
        cost_estimate=pl.CostEstimate(
            flops=heads * length * length * 2560,
            bytes_accessed=8 * triple.size,
            transcendentals=heads * length * length,
        ),
        name="attend_backward",
    )(limits, triple, triple, triple, attended, grad, logs)


def project_kernel(rows_ref, gain_ref, shift_ref, weight_ref, bias_ref, normed_ref, triple_ref):
    normal, _ = normalize(rows_ref[0].astype(F32))
    normed = (normal * gain_ref[...] + shift_ref[...]).astype(BF)
    normed_ref[0] = normed
    triple_ref[0] = (dot(normed, weight_ref[...]) + bias_ref[...]).astype(BF)


def project(tokens, gain, shift, weight, bias):
    pieces, rows, width = tokens.shape
    columns = weight.shape[1]

    def whole(array):
        return pl.BlockSpec(array.shape, lambda i: (0, 0))

    def piece(columns):
        return pl.BlockSpec((1, rows, columns), lambda i: (i, 0, 0))

    return pl.pallas_call(
        project_kernel,
        grid=(pieces,),
        in_specs=[piece(width), whole(gain), whole(shift), whole(weight), whole(bias)],
        out_specs=[piece(width), piece(columns)],
        out_shape=[
            jax.ShapeDtypeStruct((pieces, rows, width), BF),
            jax.ShapeDtypeStruct((pieces, rows, columns), BF),
        ],
        compiler_params=pltpu.CompilerParams(vmem_limit_bytes=40 * 2**20),
        cost_estimate=pl.CostEstimate(
            flops=2 * pieces * rows * width * columns,
            bytes_accessed=2 * pieces * rows * (2 * width + columns),
            transcendentals=0,
        ),
        name="project",
    )(tokens, gain, shift, weight, bias)


def project_back_kernel(grad_ref, rows_ref, weight_ref, part_ref, gain_ref, shift_ref, total_ref):
    @pl.when(pl.program_id(0) == 0)
    def _():
        gain_ref[...] = jnp.zeros_like(gain_ref)
        shift_ref[...] = jnp.zeros_like(shift_ref)
        total_ref[...] = jnp.zeros_like(total_ref)

    normal, _ = normalize(rows_ref[0].astype(F32))
    part = dot_right_t(grad_ref[0], weight_ref[...])
    part_ref[0] = part.astype(BF)
    gain_ref[...] += jnp.sum(part * normal, 0, keepdims=True)
    shift_ref[...] += jnp.sum(part, 0, keepdims=True)
    total_ref[...] += jnp.sum(grad_ref[0].astype(F32), 0, keepdims=True)


def project_back(grad, tokens, weight):
    pieces, rows, width = tokens.shape
    columns = weight.shape[1]

    def piece(columns):
        return pl.BlockSpec((1, rows, columns), lambda i: (i, 0, 0))

    def whole(shape):
        return pl.BlockSpec(shape, lambda i: (0, 0))

    return pl.pallas_call(
        project_back_kernel,
        grid=(pieces,),
        in_specs=[piece(columns), piece(width), whole(weight.shape)],
        out_specs=[piece(width), whole((1, width)), whole((1, width)), whole((1, columns))],
        out_shape=[
            jax.ShapeDtypeStruct((pieces, rows, width), BF),
            jax.ShapeDtypeStruct((1, width), F32),
            jax.ShapeDtypeStruct((1, width), F32),
            jax.ShapeDtypeStruct((1, columns), F32),
        ],
        compiler_params=pltpu.CompilerParams(vmem_limit_bytes=40 * 2**20),
        cost_estimate=pl.CostEstimate(
            flops=2 * pieces * rows * width * columns,
            bytes_accessed=2 * pieces * rows * (2 * width + columns),
            transcendentals=0,
        ),
        name="project_back",
    )(grad, tokens, weight)


def gelu_parts(values):
    size = jnp.abs(values) * 0.7071067811865476
    bell = jnp.exp(-size * size)
    t = 1.0 / (1.0 + 0.3275911 * size)
    tail = t * (
        0.254829592
        + t * (-0.284496736 + t * (1.421413741 + t * (-1.453152027 + t * 1.061405429)))
    )
    tail = 0.5 * tail * bell
    return jnp.where(values >= 0.0, 1.0 - tail, tail), 0.3989422804014327 * bell


def expand_kernel(rows_ref, weight_ref, bias_ref, active_ref, slope_ref):
    count = rows_ref.shape[0]
    for start, size in spans(count, 352):
        expanded = dot(rows_ref[start : start + size, :], weight_ref[...]) + bias_ref[...]
        below, density = gelu_parts(expanded)
        active_ref[start : start + size, :] = (expanded * below).astype(BF)
        slope_ref[start : start + size, :] = (below + expanded * density).astype(BF)


def expand_rows(rows, weight, bias):
    count, width = rows.shape
    units = weight.shape[1]
    tile = 256
    shape = jax.ShapeDtypeStruct((count, units), BF)
    return pl.pallas_call(
        expand_kernel,
        grid=(units // tile,),
        in_specs=[
            pl.BlockSpec((count, width), lambda i: (0, 0)),
            pl.BlockSpec((width, tile), lambda i: (0, i)),
            pl.BlockSpec((1, tile), lambda i: (0, i)),
        ],
        out_specs=[pl.BlockSpec((count, tile), lambda i: (0, i))] * 2,
        out_shape=[shape] * 2,
        compiler_params=pltpu.CompilerParams(vmem_limit_bytes=48 * 2**20),
        cost_estimate=pl.CostEstimate(
            flops=4 * count * units * width,
            bytes_accessed=2 * (count * width + width * units + 2 * count * units),
            transcendentals=2 * count * units,
        ),
        name="expand_rows",
    )(rows, weight, bias)


def far_send(array, shift):
    count = lax.axis_size("far")
    return lax.ppermute(array, "far", [(i, (i + shift) % count) for i in range(count)])


def far_gather(array):
    count = lax.axis_size("far")
    return [array] + [far_send(array, count - r) for r in range(1, count)]


def far_exchange(slots):
    count = len(slots)
    out = [slots[0]] + [None] * (count - 1)
    for r in range(1, count):
        out[count - r] = far_send(slots[r], r)
    return out


def far_sum(slots):
    arrived = far_exchange(slots)
    return sum(part.astype(F32) for part in arrived)


def other_core(array):
    return lax.ppermute(array, "core", [(0, 1), (1, 0)])


def fsdp_gather(array):
    return lax.all_gather(array, "fsdp", axis=0, tiled=True)


def fsdp_scatter(array):
    return lax.psum_scatter(array, "fsdp", scatter_dimension=0, tiled=True)


def ring_send(array, step):
    count = lax.axis_size("fsdp")
    order = list(range(0, count, 2)) + list(range(1, count, 2))[::-1]
    pairs = [(order[i], order[(i + step) % count]) for i in range(count)]
    return lax.ppermute(array, "fsdp", pairs)


def ring_index(offset):
    count, index = lax.axis_size("fsdp"), lax.axis_index("fsdp")
    place = jnp.where(index % 2 == 0, index // 2, count - 1 - index // 2)
    place = (place + offset + count) % count
    return jnp.where(place < count // 2, 2 * place, 2 * (count - 1 - place) + 1)


def ring_gather(array):
    count = lax.axis_size("fsdp")
    out = jnp.zeros((count,) + array.shape, array.dtype)
    out = lax.dynamic_update_index_in_dim(out, array, ring_index(0), 0)
    up = down = array
    for step in range(1, count // 2 + 1):
        up = ring_send(up, 1)
        out = lax.dynamic_update_index_in_dim(out, up, ring_index(-step), 0)
        if step <= (count - 1) // 2:
            down = ring_send(down, -1)
            out = lax.dynamic_update_index_in_dim(out, down, ring_index(step), 0)
    return out


def ring_scatter(array):
    count = lax.axis_size("fsdp")

    def block(offset):
        return lax.dynamic_index_in_dim(array, ring_index(offset), 0, False).astype(F32)

    total = block(0)
    for direction, hops in ((1, count // 2), (-1, (count - 1) // 2)):
        moving = block(direction * hops)
        for step in range(1, hops + 1):
            moving = ring_send(moving.astype(BF), direction).astype(F32)
            if step < hops:
                moving = moving + block(direction * (hops - step))
        total = total + moving
    return total


def core_join(mine, axis, core):
    other = other_core(mine)
    return jnp.stack(
        [jnp.where(core == 0, mine, other), jnp.where(core == 0, other, mine)], axis
    )


def shards(
    images,
    cotangent,
    valid_count,
    first_gain,
    first_shift,
    triple_weight,
    query_bias,
    value_bias,
    output_weight,
    output_bias,
    attend_scale,
    second_gain,
    second_shift,
    expand_weight,
    expand_bias,
    reduce_weight,
    reduce_bias,
    feed_scale,
):
    image_count, local_len, width = images.shape
    own_rows = image_count * local_len
    far_count, fsdp_count = lax.axis_size("far"), lax.axis_size("fsdp")
    far, core = lax.axis_index("far"), lax.axis_index("core")
    seq_count = 2 * far_count
    shard = width // fsdp_count
    units = expand_weight.shape[1]
    unit_part = units // (2 * fsdp_count)
    near_heads = width // HEAD_DIM // seq_count
    head_width = near_heads * HEAD_DIM

    def my_heads(array, axis):
        shape = array.shape
        array = array.reshape(
            shape[:axis] + (far_count, near_heads, 2, HEAD_DIM) + shape[axis + 1 :]
        )
        array = lax.dynamic_index_in_dim(array, far, axis, False)
        array = lax.dynamic_index_in_dim(array, core, axis + 1, False)
        return array.reshape(shape[:axis] + (head_width,) + shape[axis + 1 :])

    triple_mine = my_heads(triple_weight.reshape(shard, 3, width), 2).reshape(shard, 3 * head_width)
    bias_mine = lax.dynamic_index_in_dim(expand_bias.reshape(2, unit_part), core, 0, False)
    bias_columns = unit_part // shard
    vectors = [
        first_gain, first_shift, query_bias, value_bias, output_bias, attend_scale,
        second_gain, second_shift, reduce_bias, feed_scale,
    ]
    vector_count = len(vectors)
    packed = jnp.concatenate(
        [triple_mine, jnp.stack(vectors, 1), bias_mine.reshape(shard, bias_columns)], 1
    )
    packed = jnp.pad(packed, ((0, 0), (0, -packed.shape[1] % 128)))
    packed = ring_gather(packed).reshape(width, -1)
    triple_whole = packed[:, : 3 * head_width]
    small = packed[:, 3 * head_width : 3 * head_width + vector_count + bias_columns]
    small = small.astype(F32).T
    (gain_1, shift_1, bias_q, bias_v, bias_o, scale_a, gain_2, shift_2, bias_r, scale_f) = [
        small[i] for i in range(vector_count)
    ]
    bias_e = (
        small[vector_count:]
        .reshape(bias_columns, fsdp_count, shard)
        .transpose(1, 2, 0)
        .reshape(1, fsdp_count * unit_part)
    )

    split_output = shard % (2 * HEAD_DIM) == 0
    if split_output:
        output_mine = lax.dynamic_index_in_dim(
            output_weight.reshape(shard // (2 * HEAD_DIM), 2, HEAD_DIM, width), core, 1, False
        ).reshape(shard // 2, width)
        output_whole = ring_gather(output_mine)
    else:
        output_whole = lax.dynamic_index_in_dim(
            fsdp_gather(output_weight).reshape(-1, 2, HEAD_DIM, width), core, 1, False
        )
    output_whole = output_whole.reshape(far_count, head_width, width)
    output_whole = jnp.roll(output_whole, -far, 0).reshape(width // 2, width)
    expand_mine = lax.dynamic_index_in_dim(
        expand_weight.reshape(shard, fsdp_count, 2, unit_part), core, 2, False
    ).reshape(shard, units // 2)
    expand_whole = fsdp_gather(expand_mine)
    reduce_mine = lax.dynamic_index_in_dim(
        reduce_weight.reshape(2, unit_part, width), core, 0, False
    )
    reduce_whole = fsdp_gather(reduce_mine)

    groups = 2 if image_count % 2 == 0 else 1
    group_images = image_count // groups
    rows = group_images * local_len
    joint_bias = jnp.concatenate(
        [my_heads(bias_q, 0), jnp.zeros((head_width,), F32), my_heads(bias_v, 0)]
    )
    tokens, normed, triples = [], [], []
    for group in range(groups):
        mine = images[group * group_images : (group + 1) * group_images].reshape(rows, width)
        slots = []
        for slot in far_gather(mine):
            slots += [slot, other_core(slot)]
        tokens.append(jnp.stack(slots, 0))
        first_normed, triple = project(
            tokens[-1], gain_1[None], shift_1[None], triple_whole, joint_bias[None]
        )
        normed.append(first_normed)
        triples.append(triple)

    last_slot = ((far_count - 1 - far) % far_count) * 2 + (1 - core)
    dead_from = last_slot * local_len + valid_count - (seq_count - 1) * local_len
    limits = jnp.stack(
        [dead_from, jnp.broadcast_to((last_slot + 1) * local_len, dead_from.shape)], 1
    ).astype(jnp.int32)

    direct = local_len % 8 == 0 and head_width % (2 * HEAD_DIM) == 0

    def to_kernel(array):
        array = array.reshape(seq_count, group_images, local_len, -1)
        if direct:
            return array
        parts = array.shape[-1] // head_width
        array = array.transpose(1, 0, 2, 3).reshape(
            1, group_images, seq_count * local_len, parts, head_width
        )
        lanes = -head_width % (2 * HEAD_DIM)
        array = jnp.pad(array, ((0, 0),) * 4 + ((0, lanes),))
        return array.reshape(1, group_images, seq_count * local_len, -1)

    def from_kernel(array, parts):
        if direct:
            return array.reshape(seq_count, rows, -1)
        array = array.reshape(group_images, seq_count, local_len, parts, -1)
        array = array[..., :head_width].transpose(1, 0, 2, 3, 4)
        return array.reshape(seq_count, rows, parts * head_width)

    kernel_in, kernel_out, kernel_logs, attended_rows, branch_parts = [], [], [], [], []
    for group in range(groups):
        picked = limits[group * group_images : (group + 1) * group_images]
        kernel_in.append(to_kernel(triples[group]))
        attended, logs = attend_forward(kernel_in[-1], picked)
        kernel_out.append(attended)
        kernel_logs.append(logs)
        attended = from_kernel(attended, 1).reshape(far_count, 2 * rows, head_width)
        attended = far_exchange([attended[r] for r in range(far_count)])
        attended_rows.append(jnp.concatenate(attended, 1))
        branch = dot(attended_rows[-1], output_whole)
        branch_parts.append(
            branch[:rows] + other_core(branch[rows:].astype(BF)).astype(F32) + bias_o
        )
    branch_attend = jnp.concatenate(branch_parts, 0)
    inputs = images.reshape(own_rows, width).astype(F32)
    residual = inputs + scale_a * branch_attend
    normal_2, factor_2 = normalize(residual)
    second_mine = (normal_2 * gain_2 + shift_2).astype(BF)
    second_normed = jnp.concatenate([second_mine, other_core(second_mine)], 0)
    activated, slope = expand_rows(second_normed, expand_whole, bias_e)
    branch = dot(activated, reduce_whole)
    branch_feed = (
        branch[:own_rows] + other_core(branch[own_rows:].astype(BF)).astype(F32) + bias_r
    )
    outputs = residual + scale_f * branch_feed

    cotangent = cotangent.reshape(own_rows, width)
    upstream = cotangent.astype(F32)
    both = jnp.concatenate([cotangent, other_core(cotangent)], 0)
    grad_feed = (scale_f * both.astype(F32)).astype(BF)
    grad_feed_scale = jnp.sum(upstream * branch_feed, 0)
    grad_reduce_bias = column_total(grad_feed[:own_rows])
    grad_reduce_weight = dot_left_t(activated, grad_feed).astype(BF)
    grad_expanded = (dot_right_t(grad_feed, reduce_whole) * slope.astype(F32)).astype(BF)
    grad_expanded, grad_reduce_weight = lax.optimization_barrier(
        (grad_expanded, grad_reduce_weight)
    )
    grad_reduce_weight = fsdp_scatter(grad_reduce_weight)
    grad_expand_bias = column_total(grad_expanded)
    grad_expand_weight = dot_left_t(second_normed, grad_expanded).astype(BF)
    grad_expanded, grad_expand_weight = lax.optimization_barrier(
        (grad_expanded, grad_expand_weight)
    )
    grad_expand_weight = fsdp_scatter(grad_expand_weight)
    partial = dot_right_t(grad_expanded, expand_whole)
    upper = partial[:own_rows] + other_core(partial[own_rows:].astype(BF)).astype(F32)
    grad_second_gain = jnp.sum(upper * normal_2, 0)
    grad_second_shift = jnp.sum(upper, 0)
    grad_residual = upstream + normalize_back(normal_2, factor_2, upper * gain_2)
    grad_attend_scale = jnp.sum(grad_residual * branch_attend, 0)
    grad_attend = (scale_a * grad_residual).astype(BF)
    grad_output_bias = column_total(grad_attend)
    grad_attend = jnp.concatenate([grad_attend, other_core(grad_attend)], 0)
    grad_attended = dot_right_t(grad_attend, output_whole).astype(BF)
    grad_attended = grad_attended.reshape(2, groups, rows, far_count, head_width)
    grad_sides = grad_attend.reshape(2, groups, rows, width)
    grad_output_weight = sum(
        dot_left_t(attended_rows[group], grad_sides[:, group].reshape(2 * rows, width))
        for group in range(groups)
    ).astype(BF)
    grad_output_weight = jnp.roll(
        grad_output_weight.reshape(far_count, head_width, width), far, 0
    ).reshape(width // 2, width)

    grad_heads = [
        to_kernel(
            jnp.stack(
                far_exchange(
                    [
                        grad_attended[:, group, :, r].reshape(2 * rows, head_width)
                        for r in range(far_count)
                    ]
                ),
                0,
            )
        )
        for group in range(groups)
    ]
    upper_parts, grad_triples = [], []
    grad_first_gain = grad_first_shift = column_sums = 0.0
    for group in range(groups):
        picked = limits[group * group_images : (group + 1) * group_images]
        grad_triple = from_kernel(
            attend_backward(
                kernel_in[group], kernel_out[group], grad_heads[group], kernel_logs[group], picked
            ),
            3,
        )
        grad_triples.append(grad_triple)
        partial, gain_part, shift_part, total_part = project_back(
            grad_triple, tokens[group], triple_whole
        )
        grad_first_gain = grad_first_gain + gain_part[0]
        grad_first_shift = grad_first_shift + shift_part[0]
        column_sums = column_sums + total_part[0]
        partial = partial.reshape(far_count, 2, rows, width)
        partial = partial[:, 0].astype(F32) + other_core(partial[:, 1]).astype(F32)
        partial = partial.astype(BF)
        upper_parts.append(far_sum([partial[r] for r in range(far_count)]))
    grad_triple_weight = sum(
        dot_left_t(
            normed[group].reshape(seq_count * rows, width),
            grad_triples[group].reshape(seq_count * rows, 3 * head_width),
        )
        for group in range(groups)
    ).astype(BF)
    upper = jnp.concatenate(upper_parts, 0)
    normal, factor = normalize(inputs)
    grad_images = grad_residual + normalize_back(normal, factor, upper * gain_1)

    def place_heads(vector):
        here = jnp.arange(far_count)[:, None, None, None] == far
        here = here & (jnp.arange(2)[None, None, :, None] == core)
        vector = vector.reshape(1, near_heads, 1, HEAD_DIM)
        return jnp.where(here, vector, 0.0).reshape(width)

    def place_units(vector):
        vector = vector.reshape(fsdp_count, shard, bias_columns)
        vector = vector.transpose(2, 0, 1).reshape(1, bias_columns, width)
        vector = jnp.where(jnp.arange(2)[:, None, None] == core, vector, 0.0)
        return [vector[i, j] for i in range(2) for j in range(bias_columns)]

    sums = [
        grad_first_gain, grad_first_shift,
        place_heads(column_sums[:head_width]), place_heads(column_sums[2 * head_width :]),
        grad_output_bias, grad_attend_scale, grad_second_gain, grad_second_shift,
        grad_reduce_bias, grad_feed_scale,
    ] + place_units(grad_expand_bias)
    sums = jnp.stack(sums, 0).astype(BF).T
    sums = jnp.pad(sums, ((0, 0), (0, -sums.shape[1] % 128)))
    grad_packed = jnp.concatenate([grad_triple_weight, sums], 1)
    grad_packed = ring_scatter(grad_packed.reshape(fsdp_count, shard, -1)).astype(BF)
    grad_packed = jnp.roll(jnp.stack(far_gather(grad_packed), 0), far, 0)
    grad_packed = core_join(grad_packed, 1, core).astype(F32)
    grad_triple_weight = (
        grad_packed[:, :, :, : 3 * head_width]
        .reshape(far_count, 2, shard, 3, near_heads, HEAD_DIM)
        .transpose(2, 3, 0, 4, 1, 5)
        .reshape(shard, 3 * width)
    )
    sums = jnp.sum(grad_packed[:, :, :, 3 * head_width :], (0, 1)).T

    def far_total(array):
        total = array.astype(F32)
        for r in range(1, far_count):
            total = total + far_send(array, r).astype(F32)
        return total

    if split_output:
        grad_output_weight = ring_scatter(
            grad_output_weight.reshape(fsdp_count, shard // 2, width)
        ).astype(BF)
        grad_output_weight = far_total(grad_output_weight).astype(BF)
        grad_output_weight = core_join(
            grad_output_weight.reshape(-1, HEAD_DIM, width), 1, core
        ).reshape(shard, width)
    else:
        spread = grad_output_weight.reshape(-1, 1, HEAD_DIM, width)
        spread = jnp.where(jnp.arange(2)[None, :, None, None] == core, spread, 0)
        spread = fsdp_scatter(spread.reshape(width, width))
        grad_output_weight = far_total(spread)
        grad_output_weight = grad_output_weight + other_core(grad_output_weight)
    grad_expand_weight = core_join(
        far_total(grad_expand_weight).astype(BF).reshape(shard, fsdp_count, unit_part), 2, core
    ).reshape(shard, units)
    grad_reduce_weight = core_join(far_total(grad_reduce_weight).astype(BF), 0, core).reshape(
        2 * unit_part, width
    )
    grad_expand_bias = (
        sums[10 : 10 + 2 * bias_columns]
        .reshape(2, bias_columns, shard)
        .transpose(0, 2, 1)
        .reshape(2 * unit_part)
    )
    return (
        outputs.reshape(image_count, local_len, width).astype(BF),
        grad_images.reshape(image_count, local_len, width),
        sums[0],
        sums[1],
        grad_triple_weight,
        sums[2],
        sums[3],
        grad_output_weight.astype(F32),
        sums[4],
        sums[5],
        sums[6],
        sums[7],
        grad_expand_weight.astype(F32),
        grad_expand_bias,
        grad_reduce_weight.astype(F32),
        sums[8],
        sums[9],
    )


def solution(mesh):
    fsdp, seq = mesh.devices.shape
    split = Mesh(mesh.devices.reshape(fsdp, seq // 2, 2), ("fsdp", "far", "core"))
    tokens = P("fsdp", ("far", "core"), None)
    row, matrix = P("fsdp"), P("fsdp", None)
    return jax.shard_map(
        shards,
        mesh=split,
        in_specs=(
            tokens, tokens, row, row, row, matrix, row, row, matrix,
            row, row, row, row, matrix, row, matrix, row, row,
        ),
        out_specs=(
            tokens, tokens, row, row, matrix, row, row, matrix,
            row, row, row, row, matrix, row, matrix, row, row,
        ),
        check_vma=False,
    )
```

```python
import functools

import jax
import jax.numpy as jnp
from jax import lax
from jax.experimental import pallas as pl
from jax.experimental.pallas import tpu as pltpu
from jax.sharding import Mesh, PartitionSpec as P

HEAD_DIM = 64
EPSILON = 1e-06
BF = jnp.bfloat16
F32 = jnp.float32
MASKED = -1e30


def dot(left, right):
    return lax.dot_general(left, right, (((1,), (0,)), ((), ())), preferred_element_type=F32)


def dot_left_t(left, right):
    return lax.dot_general(left, right, (((0,), (0,)), ((), ())), preferred_element_type=F32)


def dot_right_t(left, right):
    return lax.dot_general(left, right, (((1,), (1,)), ((), ())), preferred_element_type=F32)


def column_total(array):
    return dot(jnp.ones((8, array.shape[0]), BF), array)[0]


def normalize(rows):
    average = jnp.mean(rows, -1, keepdims=True)
    centered = rows - average
    variance = jnp.mean(centered * centered, -1, keepdims=True)
    factor = lax.rsqrt(variance + EPSILON)
    return centered * factor, factor


def normalize_back(normal, factor, weighted):
    return factor * (
        weighted
        - jnp.mean(weighted, -1, keepdims=True)
        - normal * jnp.mean(weighted * normal, -1, keepdims=True)
    )


def spans(total, step):
    return [(start, min(step, total - start)) for start in range(0, total, step)]


def merge(ref, out):
    pieces, _, rows, _ = ref.shape
    for piece in range(pieces):
        out[pl.ds(piece * rows, rows), :] = ref[piece, 0].astype(F32)


def lane_parts(block, heads, head):
    lane = lax.broadcasted_iota(jnp.int32, (1, block), 1)
    if heads == 1:
        return lane < HEAD_DIM, lane - HEAD_DIM
    if head == 0:
        return lane < HEAD_DIM, lane - HEAD_DIM
    return lane >= HEAD_DIM, lane


def split_three(values):
    high = values.astype(BF).astype(F32)
    rest = values - high
    middle = rest.astype(BF).astype(F32)
    return high, middle, rest - middle


def dead_column(limit_ref, length):
    image = pl.program_id(0)
    row = lax.broadcasted_iota(jnp.int32, (length, 1), 0)
    dead = (row >= limit_ref[image, 0]) & (row < limit_ref[image, 1])
    return jnp.where(dead, MASKED, 0.0)


def attend_forward_kernel(limit_ref, q_ref, k_ref, v_ref, out_ref, log_ref, q_s, k_s, v_s, o_s):
    pieces, _, rows, block = q_ref.shape
    length = pieces * rows
    heads = max(block // HEAD_DIM, 1)
    merge(q_ref, q_s)
    merge(k_ref, k_s)
    merge(v_ref, v_s)
    dead = dead_column(limit_ref, length)
    aug = []
    for head in range(heads):
        own, spare = lane_parts(2 * HEAD_DIM, heads, head)
        q = jnp.where(own, q_s[...] * 0.125, jnp.where(spare == 0, 1.0, 0.0)).astype(BF)
        k = jnp.where(own, k_s[...], jnp.where(spare == 0, dead, 0.0)).astype(BF)
        v = jnp.where(own, v_s[...], jnp.where(spare == 0, 1.0, 0.0)).astype(BF)
        aug.append((q, k, v))
    for start, size in spans(length, 352):
        results = []
        for head in range(heads):
            q, k, v = aug[head]
            scores = dot_right_t(q[start : start + size], k)
            top = jnp.max(scores, -1, keepdims=True)
            powers = jnp.exp(scores - top).astype(BF)
            mixed = dot(powers, v)
            own, spare = lane_parts(2 * HEAD_DIM, heads, head)
            at = HEAD_DIM if head == 0 else 0
            total = mixed[:, at : at + 1]
            results.append((mixed / total, top + jnp.log(total)))
        own, _ = lane_parts(2 * HEAD_DIM, heads, 0)
        if heads == 1:
            o_s[pl.ds(start, size), :] = results[0][0]
            log_ref[0, 0, pl.ds(start, size), :] = jnp.broadcast_to(
                results[0][1], (size, 2 * HEAD_DIM)
            )
        else:
            o_s[pl.ds(start, size), :] = jnp.where(own, results[0][0], results[1][0])
            log_ref[0, 0, pl.ds(start, size), :] = jnp.where(own, results[1][1], results[0][1])
    for piece in range(pieces):
        out_ref[piece, 0] = o_s[pl.ds(piece * rows, rows), :].astype(BF)


def attend_backward_kernel(
    limit_ref, q_ref, k_ref, v_ref, o_ref, g_ref, log_ref, grad_ref,
    q_s, k_s, v_s, o_s, g_s, dq_s, dk_s, dv_s,
):
    pieces, _, rows, block = q_ref.shape
    length = pieces * rows
    heads = max(block // HEAD_DIM, 1)
    merge(q_ref, q_s)
    merge(k_ref, k_s)
    merge(v_ref, v_s)
    merge(o_ref, o_s)
    merge(g_ref, g_s)
    dead = dead_column(limit_ref, length)
    product = o_s[...] * g_s[...]
    for head in range(heads):
        own, spare = lane_parts(2 * HEAD_DIM, heads, head)
        log_parts = split_three(log_ref[0, 0])
        inner = jnp.sum(jnp.where(own, product, 0.0), -1, keepdims=True)
        inner_parts = split_three(inner)
        zero = jnp.zeros((length, 2 * HEAD_DIM), F32)
        q_tail, k_tail, v_tail, g_tail = zero, zero, zero, zero
        for place in range(3):
            q_tail = jnp.where(spare == place, -log_parts[place], q_tail)
            g_tail = jnp.where(spare == place, -inner_parts[place], g_tail)
            k_tail = jnp.where(spare == place, 1.0, k_tail)
            v_tail = jnp.where(spare == place, 1.0, v_tail)
        q_tail = jnp.where(spare == 3, 1.0, q_tail)
        k_tail = jnp.where(spare == 3, dead, k_tail)
        q = jnp.where(own, q_s[...] * 0.125, q_tail).astype(BF)
        k = jnp.where(own, k_s[...], k_tail).astype(BF)
        v = jnp.where(own, v_s[...], v_tail).astype(BF)
        g = jnp.where(own, g_s[...], g_tail).astype(BF)
        k_t = jnp.where(own, k_s[...] * 0.125, 0.0).T.astype(BF)
        dk = dv = None
        for start, size in spans(length, 512):
            q_part, g_part = q[start : start + size], g[start : start + size]
            probs = jnp.exp(dot_right_t(k, q_part))
            slopes = (probs * dot_right_t(v, g_part)).astype(BF)
            probs = probs.astype(BF)
            dv_part = dot(probs, g_part)
            dk_part = dot(slopes, q_part)
            dv = dv_part if dv is None else dv + dv_part
            dk = dk_part if dk is None else dk + dk_part
            dq_part = dot(k_t, slopes).T
            if head == 0:
                dq_s[pl.ds(start, size), :] = dq_part
            else:
                dq_s[pl.ds(start, size), :] += dq_part
        if head == 0:
            dk_s[...] = dk
            dv_s[...] = dv
        else:
            dk_s[...] = jnp.where(own, dk, dk_s[...])
            dv_s[...] = jnp.where(own, dv, dv_s[...])
    stride = grad_ref.shape[3] // 3
    for piece in range(pieces):
        part = pl.ds(piece * rows, rows)
        for which, grad in enumerate((dq_s, dk_s, dv_s)):
            at = pl.multiple_of(which * stride + pl.program_id(1) * block, block)
            grad_ref[piece, 0, :, pl.ds(at, block)] = grad[part, :].astype(BF)


def attend_specs(pieces, rows, first):
    def at(limit_index):
        return pl.BlockSpec(
            (pieces, 1, rows, 2 * HEAD_DIM),
            lambda image, pair, limits: (0, image, 0, limit_index + pair),
        )

    return at(first)


def attend_forward(triple, limits):
    pieces, images, rows, columns = triple.shape
    head_width = columns // 3
    length = pieces * rows
    pairs = head_width // (2 * HEAD_DIM)
    wide = pltpu.VMEM((length, 2 * HEAD_DIM), F32)
    spec = functools.partial(attend_specs, pieces, rows)
    heads = images * head_width // HEAD_DIM
    return pl.pallas_call(
        attend_forward_kernel,
        grid_spec=pltpu.PrefetchScalarGridSpec(
            num_scalar_prefetch=1,
            grid=(images, pairs),
            in_specs=[spec(0), spec(pairs), spec(2 * pairs)],
            out_specs=[
                spec(0),
                pl.BlockSpec((1, 1, length, 2 * HEAD_DIM), lambda i, p, limits: (i, p, 0, 0)),
            ],
            scratch_shapes=[wide] * 4,
        ),
        out_shape=[
            jax.ShapeDtypeStruct((pieces, images, rows, head_width), BF),
            jax.ShapeDtypeStruct((images, pairs, length, 2 * HEAD_DIM), F32),
        ],
        compiler_params=pltpu.CompilerParams(vmem_limit_bytes=50 * 2**20),
        cost_estimate=pl.CostEstimate(
            flops=heads * length * length * 1024,
            bytes_accessed=4 * triple.size,
            transcendentals=heads * length * length,
        ),
        name="attend_forward",
    )(limits, triple, triple, triple)


def attend_backward(triple, attended, grad, logs, limits):
    pieces, images, rows, columns = triple.shape
    head_width = columns // 3
    length = pieces * rows
    pairs = head_width // (2 * HEAD_DIM)
    wide = pltpu.VMEM((length, 2 * HEAD_DIM), F32)
    spec = functools.partial(attend_specs, pieces, rows)
    heads = images * head_width // HEAD_DIM
    return pl.pallas_call(
        attend_backward_kernel,
        grid_spec=pltpu.PrefetchScalarGridSpec(
            num_scalar_prefetch=1,
            grid=(images, pairs),
            in_specs=[
                spec(0),
                spec(pairs),
                spec(2 * pairs),
                spec(0),
                spec(0),
                pl.BlockSpec((1, 1, length, 2 * HEAD_DIM), lambda i, p, limits: (i, p, 0, 0)),
            ],
            out_specs=pl.BlockSpec(
                (pieces, 1, rows, columns), lambda image, pair, limits: (0, image, 0, 0)
            ),
            scratch_shapes=[wide] * 8,
        ),
        out_shape=jax.ShapeDtypeStruct(triple.shape, BF),
        compiler_params=pltpu.CompilerParams(vmem_limit_bytes=56 * 2**20),
        cost_estimate=pl.CostEstimate(
            flops=heads * length * length * 2560,
            bytes_accessed=8 * triple.size,
            transcendentals=heads * length * length,
        ),
        name="attend_backward",
    )(limits, triple, triple, triple, attended, grad, logs)


def project_kernel(rows_ref, gain_ref, shift_ref, weight_ref, bias_ref, normed_ref, triple_ref):
    normal, _ = normalize(rows_ref[0].astype(F32))
    normed = (normal * gain_ref[...] + shift_ref[...]).astype(BF)
    normed_ref[0] = normed
    triple_ref[0] = (dot(normed, weight_ref[...]) + bias_ref[...]).astype(BF)


def project(tokens, gain, shift, weight, bias):
    pieces, rows, width = tokens.shape
    columns = weight.shape[1]

    def whole(array):
        return pl.BlockSpec(array.shape, lambda i: (0, 0))

    def piece(columns):
        return pl.BlockSpec((1, rows, columns), lambda i: (i, 0, 0))

    return pl.pallas_call(
        project_kernel,
        grid=(pieces,),
        in_specs=[piece(width), whole(gain), whole(shift), whole(weight), whole(bias)],
        out_specs=[piece(width), piece(columns)],
        out_shape=[
            jax.ShapeDtypeStruct((pieces, rows, width), BF),
            jax.ShapeDtypeStruct((pieces, rows, columns), BF),
        ],
        compiler_params=pltpu.CompilerParams(vmem_limit_bytes=40 * 2**20),
        cost_estimate=pl.CostEstimate(
            flops=2 * pieces * rows * width * columns,
            bytes_accessed=2 * pieces * rows * (2 * width + columns),
            transcendentals=0,
        ),
        name="project",
    )(tokens, gain, shift, weight, bias)


def project_back_kernel(grad_ref, rows_ref, weight_ref, part_ref, gain_ref, shift_ref, total_ref):
    @pl.when(pl.program_id(0) == 0)
    def _():
        gain_ref[...] = jnp.zeros_like(gain_ref)
        shift_ref[...] = jnp.zeros_like(shift_ref)
        total_ref[...] = jnp.zeros_like(total_ref)

    normal, _ = normalize(rows_ref[0].astype(F32))
    part = dot_right_t(grad_ref[0], weight_ref[...])
    part_ref[0] = part.astype(BF)
    gain_ref[...] += jnp.sum(part * normal, 0, keepdims=True)
    shift_ref[...] += jnp.sum(part, 0, keepdims=True)
    total_ref[...] += jnp.sum(grad_ref[0].astype(F32), 0, keepdims=True)


def project_back(grad, tokens, weight):
    pieces, rows, width = tokens.shape
    columns = weight.shape[1]

    def piece(columns):
        return pl.BlockSpec((1, rows, columns), lambda i: (i, 0, 0))

    def whole(shape):
        return pl.BlockSpec(shape, lambda i: (0, 0))

    return pl.pallas_call(
        project_back_kernel,
        grid=(pieces,),
        in_specs=[piece(columns), piece(width), whole(weight.shape)],
        out_specs=[piece(width), whole((1, width)), whole((1, width)), whole((1, columns))],
        out_shape=[
            jax.ShapeDtypeStruct((pieces, rows, width), BF),
            jax.ShapeDtypeStruct((1, width), F32),
            jax.ShapeDtypeStruct((1, width), F32),
            jax.ShapeDtypeStruct((1, columns), F32),
        ],
        compiler_params=pltpu.CompilerParams(vmem_limit_bytes=40 * 2**20),
        cost_estimate=pl.CostEstimate(
            flops=2 * pieces * rows * width * columns,
            bytes_accessed=2 * pieces * rows * (2 * width + columns),
            transcendentals=0,
        ),
        name="project_back",
    )(grad, tokens, weight)


def gelu_parts(values):
    size = jnp.abs(values) * 0.7071067811865476
    bell = jnp.exp(-size * size)
    t = 1.0 / (1.0 + 0.3275911 * size)
    tail = t * (
        0.254829592
        + t * (-0.284496736 + t * (1.421413741 + t * (-1.453152027 + t * 1.061405429)))
    )
    tail = 0.5 * tail * bell
    return jnp.where(values >= 0.0, 1.0 - tail, tail), 0.3989422804014327 * bell


def expand_kernel(rows_ref, weight_ref, bias_ref, active_ref, slope_ref):
    count, width = rows_ref.shape
    weight = weight_ref[...].reshape(width, weight_ref.shape[2])
    for start, size in spans(count, 352):
        expanded = dot(rows_ref[start : start + size, :], weight) + bias_ref[...]
        below, density = gelu_parts(expanded)
        active_ref[start : start + size, :] = (expanded * below).astype(BF)
        slope_ref[start : start + size, :] = (below + expanded * density).astype(BF)


def expand_rows(rows, feed_weights, bias):
    count, width = rows.shape
    devices = feed_weights.shape[0]
    shard = width // devices
    units = bias.shape[1]
    tile = 256
    across = width // tile
    shape = jax.ShapeDtypeStruct((count, units), BF)
    return pl.pallas_call(
        expand_kernel,
        grid=(units // tile,),
        in_specs=[
            pl.BlockSpec((count, width), lambda i: (0, 0)),
            pl.BlockSpec((devices, shard, tile), lambda i: (0, i // across, i % across)),
            pl.BlockSpec((1, tile), lambda i: (0, i)),
        ],
        out_specs=[pl.BlockSpec((count, tile), lambda i: (0, i))] * 2,
        out_shape=[shape] * 2,
        compiler_params=pltpu.CompilerParams(vmem_limit_bytes=48 * 2**20),
        cost_estimate=pl.CostEstimate(
            flops=4 * count * units * width,
            bytes_accessed=2 * (count * width + width * units + 2 * count * units),
            transcendentals=2 * count * units,
        ),
        name="expand_rows",
    )(rows, feed_weights, bias)


def feed_grads_kernel(rows_ref, active_ref, expanded_ref, feed_ref, out_ref):
    shard, width = rows_ref.shape[1], out_ref.shape[2]
    blocks = expanded_ref.shape[1] // width
    for block in range(blocks):
        out_ref[0, block * shard : (block + 1) * shard, :] = dot_left_t(
            rows_ref[...], expanded_ref[:, block * width : (block + 1) * width]
        ).astype(BF)
    out_ref[0, blocks * shard :, :] = dot_left_t(active_ref[...], feed_ref[...]).astype(BF)


def feed_grads(rows, active, grad_expanded, grad_feed, devices):
    count, width = rows.shape
    units = active.shape[1]
    shard, unit_part = width // devices, units // devices
    blocks = units // width
    if shard % 128 != 0 or unit_part % 128 != 0:
        expand = dot_left_t(rows, grad_expanded).astype(BF).reshape(devices, shard, blocks, width)
        expand = expand.transpose(0, 2, 1, 3).reshape(devices, blocks * shard, width)
        reduce = dot_left_t(active, grad_feed).astype(BF).reshape(devices, unit_part, width)
        return jnp.concatenate([expand, reduce], 1)
    height = blocks * shard + unit_part
    return pl.pallas_call(
        feed_grads_kernel,
        grid=(devices,),
        in_specs=[
            pl.BlockSpec((count, shard), lambda i: (0, i)),
            pl.BlockSpec((count, unit_part), lambda i: (0, i)),
            pl.BlockSpec((count, units), lambda i: (0, 0)),
            pl.BlockSpec((count, width), lambda i: (0, 0)),
        ],
        out_specs=pl.BlockSpec((1, height, width), lambda i: (i, 0, 0)),
        out_shape=jax.ShapeDtypeStruct((devices, height, width), BF),
        compiler_params=pltpu.CompilerParams(vmem_limit_bytes=52 * 2**20),
        cost_estimate=pl.CostEstimate(
            flops=4 * count * units * width,
            bytes_accessed=2 * (2 * count * (width + units) + 2 * width * units),
            transcendentals=0,
        ),
        name="feed_grads",
    )(rows, active, grad_expanded, grad_feed)


def far_send(array, shift):
    count = lax.axis_size("far")
    return lax.ppermute(array, "far", [(i, (i + shift) % count) for i in range(count)])


def far_gather(array):
    count = lax.axis_size("far")
    return [array] + [far_send(array, count - r) for r in range(1, count)]


def far_exchange(slots):
    count = len(slots)
    out = [slots[0]] + [None] * (count - 1)
    for r in range(1, count):
        out[count - r] = far_send(slots[r], r)
    return out


def far_sum(slots):
    arrived = far_exchange(slots)
    return sum(part.astype(F32) for part in arrived)


def other_core(array):
    return lax.ppermute(array, "core", [(0, 1), (1, 0)])


def fsdp_gather(array):
    return lax.all_gather(array, "fsdp", axis=0, tiled=True)


def fsdp_scatter(array):
    return lax.psum_scatter(array, "fsdp", scatter_dimension=0, tiled=True)


def ring_send(array, step):
    count = lax.axis_size("fsdp")
    order = list(range(0, count, 2)) + list(range(1, count, 2))[::-1]
    pairs = [(order[i], order[(i + step) % count]) for i in range(count)]
    return lax.ppermute(array, "fsdp", pairs)


def ring_index(offset):
    count, index = lax.axis_size("fsdp"), lax.axis_index("fsdp")
    place = jnp.where(index % 2 == 0, index // 2, count - 1 - index // 2)
    place = (place + offset + count) % count
    return jnp.where(place < count // 2, 2 * place, 2 * (count - 1 - place) + 1)


def ring_gather(array):
    count = lax.axis_size("fsdp")
    out = jnp.zeros((count,) + array.shape, array.dtype)
    out = lax.dynamic_update_index_in_dim(out, array, ring_index(0), 0)
    up = down = array
    for step in range(1, count // 2 + 1):
        up = ring_send(up, 1)
        out = lax.dynamic_update_index_in_dim(out, up, ring_index(-step), 0)
        if step <= (count - 1) // 2:
            down = ring_send(down, -1)
            out = lax.dynamic_update_index_in_dim(out, down, ring_index(step), 0)
    return out


def ring_scatter(array):
    count = lax.axis_size("fsdp")

    def block(offset):
        return lax.dynamic_index_in_dim(array, ring_index(offset), 0, False).astype(F32)

    total = block(0)
    for direction, hops in ((1, count // 2), (-1, (count - 1) // 2)):
        moving = block(direction * hops)
        for step in range(1, hops + 1):
            moving = ring_send(moving.astype(BF), direction).astype(F32)
            if step < hops:
                moving = moving + block(direction * (hops - step))
        total = total + moving
    return total


def after(array, *earlier):
    return lax.optimization_barrier((array,) + earlier)[0]


def core_join(mine, axis, core):
    other = other_core(mine)
    return jnp.stack(
        [jnp.where(core == 0, mine, other), jnp.where(core == 0, other, mine)], axis
    )


def shards(
    images,
    cotangent,
    valid_count,
    first_gain,
    first_shift,
    triple_weight,
    query_bias,
    value_bias,
    output_weight,
    output_bias,
    attend_scale,
    second_gain,
    second_shift,
    expand_weight,
    expand_bias,
    reduce_weight,
    reduce_bias,
    feed_scale,
):
    image_count, local_len, width = images.shape
    own_rows = image_count * local_len
    far_count, fsdp_count = lax.axis_size("far"), lax.axis_size("fsdp")
    far, core = lax.axis_index("far"), lax.axis_index("core")
    seq_count = 2 * far_count
    shard = width // fsdp_count
    units = expand_weight.shape[1]
    unit_part = units // (2 * fsdp_count)
    near_heads = width // HEAD_DIM // seq_count
    head_width = near_heads * HEAD_DIM

    def my_heads(array, axis):
        shape = array.shape
        array = array.reshape(
            shape[:axis] + (far_count, near_heads, 2, HEAD_DIM) + shape[axis + 1 :]
        )
        array = lax.dynamic_index_in_dim(array, far, axis, False)
        array = lax.dynamic_index_in_dim(array, core, axis + 1, False)
        return array.reshape(shape[:axis] + (head_width,) + shape[axis + 1 :])

    triple_mine = my_heads(triple_weight.reshape(shard, 3, width), 2).reshape(shard, 3 * head_width)
    bias_mine = lax.dynamic_index_in_dim(expand_bias.reshape(2, unit_part), core, 0, False)
    bias_columns = unit_part // shard
    vectors = [
        first_gain, first_shift, query_bias, value_bias, output_bias, attend_scale,
        second_gain, second_shift, reduce_bias, feed_scale,
    ]
    vector_count = len(vectors)
    packed = jnp.concatenate(
        [triple_mine, jnp.stack(vectors, 1), bias_mine.reshape(shard, bias_columns)], 1
    )
    packed = jnp.pad(packed, ((0, 0), (0, -packed.shape[1] % 128)))
    packed = ring_gather(packed).reshape(width, -1)
    triple_whole = packed[:, : 3 * head_width]
    small = packed[:, 3 * head_width : 3 * head_width + vector_count + bias_columns]
    small = small.astype(F32).T
    (gain_1, shift_1, bias_q, bias_v, bias_o, scale_a, gain_2, shift_2, bias_r, scale_f) = [
        small[i] for i in range(vector_count)
    ]
    bias_e = (
        small[vector_count:]
        .reshape(bias_columns, fsdp_count, shard)
        .transpose(1, 2, 0)
        .reshape(1, fsdp_count * unit_part)
    )

    split_output = shard % (2 * HEAD_DIM) == 0
    if split_output:
        output_mine = lax.dynamic_index_in_dim(
            output_weight.reshape(shard // (2 * HEAD_DIM), 2, HEAD_DIM, width), core, 1, False
        ).reshape(shard // 2, width)
        output_whole = ring_gather(output_mine)
    else:
        output_whole = lax.dynamic_index_in_dim(
            fsdp_gather(output_weight).reshape(-1, 2, HEAD_DIM, width), core, 1, False
        )
    output_whole = output_whole.reshape(far_count, head_width, width)
    output_whole = jnp.roll(output_whole, -far, 0).reshape(width // 2, width)
    blocks = units // 2 // width
    expand_mine = lax.dynamic_index_in_dim(
        expand_weight.reshape(shard, fsdp_count, 2, unit_part), core, 2, False
    ).reshape(shard, blocks, width)
    reduce_mine = lax.dynamic_index_in_dim(
        reduce_weight.reshape(2, unit_part, width), core, 0, False
    )
    feed_mine = jnp.concatenate([expand_mine[:, i] for i in range(blocks)] + [reduce_mine], 0)
    height = blocks * shard + unit_part
    feed_mine = lax.dynamic_slice_in_dim(
        feed_mine, far * (height // far_count), height // far_count, 0
    )
    feed_weights = lax.all_gather(after(feed_mine, packed), ("fsdp", "far"), axis=0, tiled=True)
    feed_weights = feed_weights.reshape(fsdp_count, height, width)
    expand_blocks = [
        feed_weights[:, i * shard : (i + 1) * shard].reshape(width, width) for i in range(blocks)
    ]
    reduce_whole = feed_weights[:, blocks * shard :].reshape(units // 2, width)

    groups = 2 if image_count % 2 == 0 else 1
    group_images = image_count // groups
    rows = group_images * local_len
    joint_bias = jnp.concatenate(
        [my_heads(bias_q, 0), jnp.zeros((head_width,), F32), my_heads(bias_v, 0)]
    )
    tokens, normed, triples = [], [], []
    for group in range(groups):
        mine = images[group * group_images : (group + 1) * group_images].reshape(rows, width)
        slots = []
        for slot in far_gather(mine):
            slots += [slot, other_core(slot)]
        tokens.append(jnp.stack(slots, 0))
        first_normed, triple = project(
            tokens[-1], gain_1[None], shift_1[None], triple_whole, joint_bias[None]
        )
        normed.append(first_normed)
        triples.append(triple)

    last_slot = ((far_count - 1 - far) % far_count) * 2 + (1 - core)
    dead_from = last_slot * local_len + valid_count - (seq_count - 1) * local_len
    limits = jnp.stack(
        [dead_from, jnp.broadcast_to((last_slot + 1) * local_len, dead_from.shape)], 1
    ).astype(jnp.int32)

    direct = local_len % 8 == 0 and head_width % (2 * HEAD_DIM) == 0

    def to_kernel(array):
        array = array.reshape(seq_count, group_images, local_len, -1)
        if direct:
            return array
        parts = array.shape[-1] // head_width
        array = array.transpose(1, 0, 2, 3).reshape(
            1, group_images, seq_count * local_len, parts, head_width
        )
        lanes = -head_width % (2 * HEAD_DIM)
        array = jnp.pad(array, ((0, 0),) * 4 + ((0, lanes),))
        return array.reshape(1, group_images, seq_count * local_len, -1)

    def from_kernel(array, parts):
        if direct:
            return array.reshape(seq_count, rows, -1)
        array = array.reshape(group_images, seq_count, local_len, parts, -1)
        array = array[..., :head_width].transpose(1, 0, 2, 3, 4)
        return array.reshape(seq_count, rows, parts * head_width)

    kernel_in, kernel_out, kernel_logs, attended_rows, branch_parts = [], [], [], [], []
    for group in range(groups):
        picked = limits[group * group_images : (group + 1) * group_images]
        kernel_in.append(to_kernel(triples[group]))
        attended, logs = attend_forward(kernel_in[-1], picked)
        kernel_out.append(attended)
        kernel_logs.append(logs)
        attended = from_kernel(attended, 1).reshape(far_count, 2 * rows, head_width)
        attended = far_exchange([attended[r] for r in range(far_count)])
        attended_rows.append(jnp.concatenate(attended, 1))
        branch = dot(attended_rows[-1], output_whole)
        branch_parts.append(
            branch[:rows] + other_core(branch[rows:].astype(BF)).astype(F32) + bias_o
        )
    branch_attend = jnp.concatenate(branch_parts, 0)
    inputs = images.reshape(own_rows, width).astype(F32)
    residual = inputs + scale_a * branch_attend
    normal_2, factor_2 = normalize(residual)
    second_mine = (normal_2 * gain_2 + shift_2).astype(BF)
    second_normed = jnp.concatenate([second_mine, other_core(second_mine)], 0)
    activated, slope = expand_rows(second_normed, feed_weights, bias_e)
    branch = dot(activated, reduce_whole)
    branch_feed = (
        branch[:own_rows] + other_core(branch[own_rows:].astype(BF)).astype(F32) + bias_r
    )
    outputs = residual + scale_f * branch_feed

    cotangent = cotangent.reshape(own_rows, width)
    upstream = cotangent.astype(F32)
    both = jnp.concatenate([cotangent, other_core(cotangent)], 0)
    grad_feed = (scale_f * both.astype(F32)).astype(BF)
    grad_feed_scale = jnp.sum(upstream * branch_feed, 0)
    grad_reduce_bias = column_total(grad_feed[:own_rows])
    grad_expanded = (dot_right_t(grad_feed, reduce_whole) * slope.astype(F32)).astype(BF)
    feed_sums = feed_grads(second_normed, activated, grad_expanded, grad_feed, fsdp_count)
    grad_expanded, feed_sums = lax.optimization_barrier((grad_expanded, feed_sums))
    feed_sums = lax.psum_scatter(
        feed_sums.reshape(fsdp_count * height, width),
        ("fsdp", "far"),
        scatter_dimension=0,
        tiled=True,
    )
    partial = sum(
        dot_right_t(grad_expanded[:, i * width : (i + 1) * width], expand_blocks[i])
        for i in range(blocks)
    )
    grad_expand_bias = column_total(grad_expanded)
    upper = partial[:own_rows] + other_core(partial[own_rows:].astype(BF)).astype(F32)
    grad_second_gain = jnp.sum(upper * normal_2, 0)
    grad_second_shift = jnp.sum(upper, 0)
    grad_residual = upstream + normalize_back(normal_2, factor_2, upper * gain_2)
    grad_attend_scale = jnp.sum(grad_residual * branch_attend, 0)
    grad_attend = (scale_a * grad_residual).astype(BF)
    grad_output_bias = column_total(grad_attend)
    grad_attend = jnp.concatenate([grad_attend, other_core(grad_attend)], 0)
    grad_attended = dot_right_t(grad_attend, output_whole).astype(BF)
    grad_attended = grad_attended.reshape(2, groups, rows, far_count, head_width)
    grad_sides = grad_attend.reshape(2, groups, rows, width)
    grad_output_weight = sum(
        dot_left_t(attended_rows[group], grad_sides[:, group].reshape(2 * rows, width))
        for group in range(groups)
    ).astype(BF)
    grad_output_weight = jnp.roll(
        grad_output_weight.reshape(far_count, head_width, width), far, 0
    ).reshape(width // 2, width)

    grad_heads = [
        to_kernel(
            jnp.stack(
                far_exchange(
                    [
                        grad_attended[:, group, :, r].reshape(2 * rows, head_width)
                        for r in range(far_count)
                    ]
                ),
                0,
            )
        )
        for group in range(groups)
    ]
    upper_parts, grad_triples = [], []
    grad_first_gain = grad_first_shift = column_sums = 0.0
    for group in range(groups):
        picked = limits[group * group_images : (group + 1) * group_images]
        grad_heads_in = grad_heads[group]
        if group > 0:
            grad_heads_in = after(grad_heads_in, partial)
        grad_triple = from_kernel(
            attend_backward(
                kernel_in[group], kernel_out[group], grad_heads_in, kernel_logs[group], picked
            ),
            3,
        )
        if group > 0:
            grad_triple = after(grad_triple, *moved)
        grad_triples.append(grad_triple)
        partial, gain_part, shift_part, total_part = project_back(
            grad_triple, tokens[group], triple_whole
        )
        grad_first_gain = grad_first_gain + gain_part[0]
        grad_first_shift = grad_first_shift + shift_part[0]
        column_sums = column_sums + total_part[0]
        partial = partial.reshape(far_count, 2, rows, width)
        partial = partial[:, 0].astype(F32) + other_core(partial[:, 1]).astype(F32)
        partial = partial.astype(BF)
        moved = far_exchange([partial[r] for r in range(far_count)])
        upper_parts.append(sum(part.astype(F32) for part in moved))
    grad_triple_weight = sum(
        dot_left_t(
            normed[group].reshape(seq_count * rows, width),
            grad_triples[group].reshape(seq_count * rows, 3 * head_width),
        )
        for group in range(groups)
    ).astype(BF)
    upper = jnp.concatenate(upper_parts, 0)
    normal, factor = normalize(inputs)
    grad_images = grad_residual + normalize_back(normal, factor, upper * gain_1)

    def place_heads(vector):
        here = jnp.arange(far_count)[:, None, None, None] == far
        here = here & (jnp.arange(2)[None, None, :, None] == core)
        vector = vector.reshape(1, near_heads, 1, HEAD_DIM)
        return jnp.where(here, vector, 0.0).reshape(width)

    def place_units(vector):
        vector = vector.reshape(fsdp_count, shard, bias_columns)
        vector = vector.transpose(2, 0, 1).reshape(1, bias_columns, width)
        vector = jnp.where(jnp.arange(2)[:, None, None] == core, vector, 0.0)
        return [vector[i, j] for i in range(2) for j in range(bias_columns)]

    sums = [
        grad_first_gain, grad_first_shift,
        place_heads(column_sums[:head_width]), place_heads(column_sums[2 * head_width :]),
        grad_output_bias, grad_attend_scale, grad_second_gain, grad_second_shift,
        grad_reduce_bias, grad_feed_scale,
    ] + place_units(grad_expand_bias)
    sums = jnp.stack(sums, 0).astype(BF).T
    sums = jnp.pad(sums, ((0, 0), (0, -sums.shape[1] % 128)))
    grad_packed = jnp.concatenate([grad_triple_weight, sums], 1)
    grad_packed = ring_scatter(grad_packed.reshape(fsdp_count, shard, -1)).astype(BF)
    grad_packed = jnp.roll(jnp.stack(far_gather(grad_packed), 0), far, 0)
    grad_packed = core_join(grad_packed, 1, core).astype(F32)
    grad_triple_weight = (
        grad_packed[:, :, :, : 3 * head_width]
        .reshape(far_count, 2, shard, 3, near_heads, HEAD_DIM)
        .transpose(2, 3, 0, 4, 1, 5)
        .reshape(shard, 3 * width)
    )
    sums = jnp.sum(grad_packed[:, :, :, 3 * head_width :], (0, 1)).T

    def far_total(array):
        total = array.astype(F32)
        for r in range(1, far_count):
            total = total + far_send(array, r).astype(F32)
        return total

    if split_output:
        grad_output_weight = ring_scatter(
            grad_output_weight.reshape(fsdp_count, shard // 2, width)
        ).astype(BF)
        grad_output_weight = far_total(grad_output_weight).astype(BF)
        grad_output_weight = core_join(
            grad_output_weight.reshape(-1, HEAD_DIM, width), 1, core
        ).reshape(shard, width)
    else:
        spread = grad_output_weight.reshape(-1, 1, HEAD_DIM, width)
        spread = jnp.where(jnp.arange(2)[None, :, None, None] == core, spread, 0)
        spread = fsdp_scatter(spread.reshape(width, width))
        grad_output_weight = far_total(spread)
        grad_output_weight = grad_output_weight + other_core(grad_output_weight)
    feed_sums = jnp.roll(jnp.stack(far_gather(core_join(feed_sums, 0, core)), 0), far, 0)
    feed_sums = feed_sums.transpose(1, 0, 2, 3).reshape(2, height, width).astype(F32)
    grad_expand_weight = (
        feed_sums[:, : blocks * shard]
        .reshape(2, blocks, shard, -1, unit_part)
        .transpose(2, 1, 3, 0, 4)
        .reshape(shard, units)
    )
    grad_reduce_weight = feed_sums[:, blocks * shard :].reshape(2 * unit_part, width)
    grad_expand_bias = (
        sums[10 : 10 + 2 * bias_columns]
        .reshape(2, bias_columns, shard)
        .transpose(0, 2, 1)
        .reshape(2 * unit_part)
    )
    return (
        outputs.reshape(image_count, local_len, width).astype(BF),
        grad_images.reshape(image_count, local_len, width),
        sums[0],
        sums[1],
        grad_triple_weight,
        sums[2],
        sums[3],
        grad_output_weight.astype(F32),
        sums[4],
        sums[5],
        sums[6],
        sums[7],
        grad_expand_weight,
        grad_expand_bias,
        grad_reduce_weight,
        sums[8],
        sums[9],
    )


def solution(mesh):
    fsdp, seq = mesh.devices.shape
    split = Mesh(mesh.devices.reshape(fsdp, seq // 2, 2), ("fsdp", "far", "core"))
    tokens = P("fsdp", ("far", "core"), None)
    row, matrix = P("fsdp"), P("fsdp", None)
    return jax.shard_map(
        shards,
        mesh=split,
        in_specs=(
            tokens, tokens, row, row, row, matrix, row, row, matrix,
            row, row, row, row, matrix, row, matrix, row, row,
        ),
        out_specs=(
            tokens, tokens, row, row, matrix, row, row, matrix,
            row, row, row, row, matrix, row, matrix, row, row,
        ),
        check_vma=False,
    )
```

```python
import functools

import jax
import jax.numpy as jnp
from jax import lax
from jax.experimental import pallas as pl
from jax.experimental.pallas import tpu as pltpu
from jax.sharding import Mesh, PartitionSpec as P

HEAD_DIM = 64
EPSILON = 1e-06
BF = jnp.bfloat16
F32 = jnp.float32
MASKED = -1e30


def dot(left, right):
    return lax.dot_general(left, right, (((1,), (0,)), ((), ())), preferred_element_type=F32)


def dot_left_t(left, right):
    return lax.dot_general(left, right, (((0,), (0,)), ((), ())), preferred_element_type=F32)


def dot_right_t(left, right):
    return lax.dot_general(left, right, (((1,), (1,)), ((), ())), preferred_element_type=F32)


def column_total(array):
    return dot(jnp.ones((8, array.shape[0]), BF), array)[0]


def normalize(rows):
    average = jnp.mean(rows, -1, keepdims=True)
    centered = rows - average
    variance = jnp.mean(centered * centered, -1, keepdims=True)
    factor = lax.rsqrt(variance + EPSILON)
    return centered * factor, factor


def normalize_back(normal, factor, weighted):
    return factor * (
        weighted
        - jnp.mean(weighted, -1, keepdims=True)
        - normal * jnp.mean(weighted * normal, -1, keepdims=True)
    )


def spans(total, step):
    return [(start, min(step, total - start)) for start in range(0, total, step)]


def merge(ref, out):
    pieces, _, rows, _ = ref.shape
    for piece in range(pieces):
        out[pl.ds(piece * rows, rows), :] = ref[piece, 0].astype(F32)


def lane_parts(block, heads, head):
    lane = lax.broadcasted_iota(jnp.int32, (1, block), 1)
    if heads == 1:
        return lane < HEAD_DIM, lane - HEAD_DIM
    if head == 0:
        return lane < HEAD_DIM, lane - HEAD_DIM
    return lane >= HEAD_DIM, lane


def split_three(values):
    high = values.astype(BF).astype(F32)
    rest = values - high
    middle = rest.astype(BF).astype(F32)
    return high, middle, rest - middle


def dead_column(limit_ref, length):
    image = pl.program_id(0)
    row = lax.broadcasted_iota(jnp.int32, (length, 1), 0)
    dead = (row >= limit_ref[image, 0]) & (row < limit_ref[image, 1])
    return jnp.where(dead, MASKED, 0.0)


def attend_forward_kernel(limit_ref, q_ref, k_ref, v_ref, out_ref, log_ref, q_s, k_s, v_s, o_s):
    pieces, _, rows, block = q_ref.shape
    length = pieces * rows
    heads = max(block // HEAD_DIM, 1)
    merge(q_ref, q_s)
    merge(k_ref, k_s)
    merge(v_ref, v_s)
    dead = dead_column(limit_ref, length)
    aug = []
    for head in range(heads):
        own, spare = lane_parts(2 * HEAD_DIM, heads, head)
        q = jnp.where(own, q_s[...] * 0.125, jnp.where(spare == 0, 1.0, 0.0)).astype(BF)
        k = jnp.where(own, k_s[...], jnp.where(spare == 0, dead, 0.0)).astype(BF)
        v = jnp.where(own, v_s[...], jnp.where(spare == 0, 1.0, 0.0)).astype(BF)
        aug.append((q, k, v))
    for start, size in spans(length, 352):
        results = []
        for head in range(heads):
            q, k, v = aug[head]
            scores = dot_right_t(q[start : start + size], k)
            top = jnp.max(scores, -1, keepdims=True)
            powers = jnp.exp(scores - top).astype(BF)
            mixed = dot(powers, v)
            own, spare = lane_parts(2 * HEAD_DIM, heads, head)
            at = HEAD_DIM if head == 0 else 0
            total = mixed[:, at : at + 1]
            results.append((mixed / total, top + jnp.log(total)))
        own, _ = lane_parts(2 * HEAD_DIM, heads, 0)
        if heads == 1:
            o_s[pl.ds(start, size), :] = results[0][0]
            log_ref[0, 0, pl.ds(start, size), :] = jnp.broadcast_to(
                results[0][1], (size, 2 * HEAD_DIM)
            )
        else:
            o_s[pl.ds(start, size), :] = jnp.where(own, results[0][0], results[1][0])
            log_ref[0, 0, pl.ds(start, size), :] = jnp.where(own, results[1][1], results[0][1])
    for piece in range(pieces):
        out_ref[piece, 0] = o_s[pl.ds(piece * rows, rows), :].astype(BF)


def attend_backward_kernel(
    limit_ref, q_ref, k_ref, v_ref, o_ref, g_ref, log_ref, grad_ref,
    q_s, k_s, v_s, o_s, g_s, dq_s, dk_s, dv_s,
):
    pieces, _, rows, block = q_ref.shape
    length = pieces * rows
    heads = max(block // HEAD_DIM, 1)
    merge(q_ref, q_s)
    merge(k_ref, k_s)
    merge(v_ref, v_s)
    merge(o_ref, o_s)
    merge(g_ref, g_s)
    dead = dead_column(limit_ref, length)
    product = o_s[...] * g_s[...]
    for head in range(heads):
        own, spare = lane_parts(2 * HEAD_DIM, heads, head)
        log_parts = split_three(log_ref[0, 0])
        inner = jnp.sum(jnp.where(own, product, 0.0), -1, keepdims=True)
        inner_parts = split_three(inner)
        zero = jnp.zeros((length, 2 * HEAD_DIM), F32)
        q_tail, k_tail, v_tail, g_tail = zero, zero, zero, zero
        for place in range(3):
            q_tail = jnp.where(spare == place, -log_parts[place], q_tail)
            g_tail = jnp.where(spare == place, -inner_parts[place], g_tail)
            k_tail = jnp.where(spare == place, 1.0, k_tail)
            v_tail = jnp.where(spare == place, 1.0, v_tail)
        q_tail = jnp.where(spare == 3, 1.0, q_tail)
        k_tail = jnp.where(spare == 3, dead, k_tail)
        q = jnp.where(own, q_s[...] * 0.125, q_tail).astype(BF)
        k = jnp.where(own, k_s[...], k_tail).astype(BF)
        v = jnp.where(own, v_s[...], v_tail).astype(BF)
        g = jnp.where(own, g_s[...], g_tail).astype(BF)
        k_t = jnp.where(own, k_s[...] * 0.125, 0.0).T.astype(BF)
        dk = dv = None
        for start, size in spans(length, 512):
            q_part, g_part = q[start : start + size], g[start : start + size]
            probs = jnp.exp(dot_right_t(k, q_part))
            slopes = (probs * dot_right_t(v, g_part)).astype(BF)
            probs = probs.astype(BF)
            dv_part = dot(probs, g_part)
            dk_part = dot(slopes, q_part)
            dv = dv_part if dv is None else dv + dv_part
            dk = dk_part if dk is None else dk + dk_part
            dq_part = dot(k_t, slopes).T
            if head == 0:
                dq_s[pl.ds(start, size), :] = dq_part
            else:
                dq_s[pl.ds(start, size), :] += dq_part
        if head == 0:
            dk_s[...] = dk
            dv_s[...] = dv
        else:
            dk_s[...] = jnp.where(own, dk, dk_s[...])
            dv_s[...] = jnp.where(own, dv, dv_s[...])
    stride = grad_ref.shape[3] // 3
    for piece in range(pieces):
        part = pl.ds(piece * rows, rows)
        for which, grad in enumerate((dq_s, dk_s, dv_s)):
            at = pl.multiple_of(which * stride + pl.program_id(1) * block, block)
            grad_ref[piece, 0, :, pl.ds(at, block)] = grad[part, :].astype(BF)


def attend_specs(pieces, rows, first):
    def at(limit_index):
        return pl.BlockSpec(
            (pieces, 1, rows, 2 * HEAD_DIM),
            lambda image, pair, limits: (0, image, 0, limit_index + pair),
        )

    return at(first)


def attend_forward(triple, limits):
    pieces, images, rows, columns = triple.shape
    head_width = columns // 3
    length = pieces * rows
    pairs = head_width // (2 * HEAD_DIM)
    wide = pltpu.VMEM((length, 2 * HEAD_DIM), F32)
    spec = functools.partial(attend_specs, pieces, rows)
    heads = images * head_width // HEAD_DIM
    return pl.pallas_call(
        attend_forward_kernel,
        grid_spec=pltpu.PrefetchScalarGridSpec(
            num_scalar_prefetch=1,
            grid=(images, pairs),
            in_specs=[spec(0), spec(pairs), spec(2 * pairs)],
            out_specs=[
                spec(0),
                pl.BlockSpec((1, 1, length, 2 * HEAD_DIM), lambda i, p, limits: (i, p, 0, 0)),
            ],
            scratch_shapes=[wide] * 4,
        ),
        out_shape=[
            jax.ShapeDtypeStruct((pieces, images, rows, head_width), BF),
            jax.ShapeDtypeStruct((images, pairs, length, 2 * HEAD_DIM), F32),
        ],
        compiler_params=pltpu.CompilerParams(vmem_limit_bytes=50 * 2**20),
        cost_estimate=pl.CostEstimate(
            flops=heads * length * length * 1024,
            bytes_accessed=4 * triple.size,
            transcendentals=heads * length * length,
        ),
        name="attend_forward",
    )(limits, triple, triple, triple)


def attend_backward(triple, attended, grad, logs, limits):
    pieces, images, rows, columns = triple.shape
    head_width = columns // 3
    length = pieces * rows
    pairs = head_width // (2 * HEAD_DIM)
    wide = pltpu.VMEM((length, 2 * HEAD_DIM), F32)
    spec = functools.partial(attend_specs, pieces, rows)
    heads = images * head_width // HEAD_DIM
    return pl.pallas_call(
        attend_backward_kernel,
        grid_spec=pltpu.PrefetchScalarGridSpec(
            num_scalar_prefetch=1,
            grid=(images, pairs),
            in_specs=[
                spec(0),
                spec(pairs),
                spec(2 * pairs),
                spec(0),
                spec(0),
                pl.BlockSpec((1, 1, length, 2 * HEAD_DIM), lambda i, p, limits: (i, p, 0, 0)),
            ],
            out_specs=pl.BlockSpec(
                (pieces, 1, rows, columns), lambda image, pair, limits: (0, image, 0, 0)
            ),
            scratch_shapes=[wide] * 8,
        ),
        out_shape=jax.ShapeDtypeStruct(triple.shape, BF),
        compiler_params=pltpu.CompilerParams(vmem_limit_bytes=56 * 2**20),
        cost_estimate=pl.CostEstimate(
            flops=heads * length * length * 2560,
            bytes_accessed=8 * triple.size,
            transcendentals=heads * length * length,
        ),
        name="attend_backward",
    )(limits, triple, triple, triple, attended, grad, logs)


def project_kernel(rows_ref, small_ref, weight_ref, bias_ref, normed_ref, triple_ref):
    normal, _ = normalize(rows_ref[0].astype(F32))
    normed = (normal * small_ref[0:1, :] + small_ref[1:2, :]).astype(BF)
    normed_ref[0] = normed
    triple_ref[0] = (dot(normed, weight_ref[...]) + bias_ref[...]).astype(BF)


def project(tokens, small, weight, bias):
    pieces, rows, width = tokens.shape
    columns = weight.shape[1]

    def whole(array):
        return pl.BlockSpec(array.shape, lambda i: (0, 0))

    def piece(columns):
        return pl.BlockSpec((1, rows, columns), lambda i: (i, 0, 0))

    return pl.pallas_call(
        project_kernel,
        grid=(pieces,),
        in_specs=[piece(width), whole(small), whole(weight), whole(bias)],
        out_specs=[piece(width), piece(columns)],
        out_shape=[
            jax.ShapeDtypeStruct((pieces, rows, width), BF),
            jax.ShapeDtypeStruct((pieces, rows, columns), BF),
        ],
        compiler_params=pltpu.CompilerParams(vmem_limit_bytes=40 * 2**20),
        cost_estimate=pl.CostEstimate(
            flops=2 * pieces * rows * width * columns,
            bytes_accessed=2 * pieces * rows * (2 * width + columns),
            transcendentals=0,
        ),
        name="project",
    )(tokens, small, weight, bias)


def project_back_kernel(grad_ref, rows_ref, weight_ref, part_ref, gain_ref, shift_ref, total_ref):
    @pl.when(pl.program_id(0) == 0)
    def _():
        gain_ref[...] = jnp.zeros_like(gain_ref)
        shift_ref[...] = jnp.zeros_like(shift_ref)
        total_ref[...] = jnp.zeros_like(total_ref)

    normal, _ = normalize(rows_ref[0].astype(F32))
    part = dot_right_t(grad_ref[0], weight_ref[...])
    part_ref[0] = part.astype(BF)
    gain_ref[...] += jnp.sum(part * normal, 0, keepdims=True)
    shift_ref[...] += jnp.sum(part, 0, keepdims=True)
    total_ref[...] += jnp.sum(grad_ref[0].astype(F32), 0, keepdims=True)


def project_back(grad, tokens, weight):
    pieces, rows, width = tokens.shape
    columns = weight.shape[1]

    def piece(columns):
        return pl.BlockSpec((1, rows, columns), lambda i: (i, 0, 0))

    def whole(shape):
        return pl.BlockSpec(shape, lambda i: (0, 0))

    return pl.pallas_call(
        project_back_kernel,
        grid=(pieces,),
        in_specs=[piece(columns), piece(width), whole(weight.shape)],
        out_specs=[piece(width), whole((1, width)), whole((1, width)), whole((1, columns))],
        out_shape=[
            jax.ShapeDtypeStruct((pieces, rows, width), BF),
            jax.ShapeDtypeStruct((1, width), F32),
            jax.ShapeDtypeStruct((1, width), F32),
            jax.ShapeDtypeStruct((1, columns), F32),
        ],
        compiler_params=pltpu.CompilerParams(vmem_limit_bytes=40 * 2**20),
        cost_estimate=pl.CostEstimate(
            flops=2 * pieces * rows * width * columns,
            bytes_accessed=2 * pieces * rows * (2 * width + columns),
            transcendentals=0,
        ),
        name="project_back",
    )(grad, tokens, weight)


def gelu_parts(values):
    size = jnp.abs(values) * 0.7071067811865476
    bell = jnp.exp(-size * size)
    t = 1.0 / (1.0 + 0.3275911 * size)
    tail = t * (
        0.254829592
        + t * (-0.284496736 + t * (1.421413741 + t * (-1.453152027 + t * 1.061405429)))
    )
    tail = 0.5 * tail * bell
    return jnp.where(values >= 0.0, 1.0 - tail, tail), 0.3989422804014327 * bell


def expand_kernel(rows_ref, weight_ref, bias_ref, active_ref, slope_ref):
    count = rows_ref.shape[0]
    for start, size in spans(count, 352):
        expanded = dot(rows_ref[start : start + size, :], weight_ref[...]) + bias_ref[...]
        below, density = gelu_parts(expanded)
        active_ref[start : start + size, :] = (expanded * below).astype(BF)
        slope_ref[start : start + size, :] = (below + expanded * density).astype(BF)


def expand_rows(rows, weight, bias):
    count, width = rows.shape
    units = weight.shape[1]
    tile = 256
    shape = jax.ShapeDtypeStruct((count, units), BF)
    return pl.pallas_call(
        expand_kernel,
        grid=(units // tile,),
        in_specs=[
            pl.BlockSpec((count, width), lambda i: (0, 0)),
            pl.BlockSpec((width, tile), lambda i: (0, i)),
            pl.BlockSpec((1, tile), lambda i: (0, i)),
        ],
        out_specs=[pl.BlockSpec((count, tile), lambda i: (0, i))] * 2,
        out_shape=[shape] * 2,
        compiler_params=pltpu.CompilerParams(vmem_limit_bytes=48 * 2**20),
        cost_estimate=pl.CostEstimate(
            flops=4 * count * units * width,
            bytes_accessed=2 * (count * width + width * units + 2 * count * units),
            transcendentals=2 * count * units,
        ),
        name="expand_rows",
    )(rows, weight, bias)


def feed_grads_kernel(*refs):
    groups = (len(refs) - 1) // 4
    out_ref = refs[-1]
    devices, height, _ = out_ref.shape
    for half, (lefts, rights) in enumerate(
        ((refs[:groups], refs[groups : 2 * groups]),
         (refs[2 * groups : 3 * groups], refs[3 * groups : 4 * groups]))
    ):
        total = None
        for left, right in zip(lefts, rights):
            part = dot_left_t(left[...], right[...])
            total = part if total is None else total + part
        part = height // 2
        for device in range(devices):
            out_ref[device, half * part : (half + 1) * part, :] = total[
                device * part : (device + 1) * part
            ].astype(BF)


def feed_grads(rows, grad_expanded, active, grad_feed, devices):
    groups = len(rows)
    count, width = rows[0].shape
    shard = width // devices
    side = pl.BlockSpec((count, 2 * shard), lambda i: (0, i))
    whole = pl.BlockSpec((count, width), lambda i: (0, 0))
    return pl.pallas_call(
        feed_grads_kernel,
        grid=(devices // 2,),
        in_specs=[side] * groups + [whole] * groups + [side] * groups + [whole] * groups,
        out_specs=pl.BlockSpec((2, 2 * shard, width), lambda i: (i, 0, 0)),
        out_shape=jax.ShapeDtypeStruct((devices, 2 * shard, width), BF),
        compiler_params=pltpu.CompilerParams(vmem_limit_bytes=52 * 2**20),
        cost_estimate=pl.CostEstimate(
            flops=4 * groups * count * width * width,
            bytes_accessed=8 * groups * count * width + 4 * width * width,
            transcendentals=0,
        ),
        name="feed_grads",
    )(*rows, *grad_expanded, *active, *grad_feed)


def assemble_kernel(order_ref, *refs):
    count = len(refs) - 3
    triple_ref, small_ref, output_ref = refs[count:]
    first, second = triple_ref.shape[2], small_ref.shape[2]
    _, half, width = output_ref.shape
    for piece in range(count):
        ref = refs[piece]
        place = order_ref[0, piece]
        triple_ref[place] = ref[:, :first]
        small_ref[place] = ref[:, first : first + second]
        place = order_ref[1, piece]
        for side in range(2):
            output_ref[place, :, side * (width // 2) : (side + 1) * (width // 2)] = ref[
                side * half : (side + 1) * half, first + second :
            ]


def assemble(order, pieces, first, second):
    count = len(pieces)
    shard, columns = pieces[0].shape
    width = 2 * (columns - first - second)
    shapes = [(count, shard, first), (count, shard, second), (count, shard // 2, width)]
    return pl.pallas_call(
        assemble_kernel,
        grid_spec=pltpu.PrefetchScalarGridSpec(
            num_scalar_prefetch=1,
            grid=(1,),
            in_specs=[pl.BlockSpec((shard, columns), lambda i, order: (0, 0))] * count,
            out_specs=[pl.BlockSpec(shape, lambda i, order: (0, 0, 0)) for shape in shapes],
        ),
        out_shape=[jax.ShapeDtypeStruct(shape, BF) for shape in shapes],
        compiler_params=pltpu.CompilerParams(vmem_limit_bytes=40 * 2**20),
        name="assemble",
    )(order, *pieces)


def far_send(array, shift):
    count = lax.axis_size("far")
    return lax.ppermute(array, "far", [(i, (i + shift) % count) for i in range(count)])


def far_gather(array):
    count = lax.axis_size("far")
    return [array] + [far_send(array, count - r) for r in range(1, count)]


def far_exchange(slots):
    count = len(slots)
    out = [slots[0]] + [None] * (count - 1)
    for r in range(1, count):
        out[count - r] = far_send(slots[r], r)
    return out


def other_core(array):
    return lax.ppermute(array, "core", [(0, 1), (1, 0)])


def fsdp_gather(array):
    return lax.all_gather(array, "fsdp", axis=0, tiled=True)


def fsdp_scatter(array):
    return lax.psum_scatter(array, "fsdp", scatter_dimension=0, tiled=True)


def ring_send(array, step):
    count = lax.axis_size("fsdp")
    order = list(range(0, count, 2)) + list(range(1, count, 2))[::-1]
    pairs = [(order[i], order[(i + step) % count]) for i in range(count)]
    return lax.ppermute(array, "fsdp", pairs)


def ring_index(offset):
    count, index = lax.axis_size("fsdp"), lax.axis_index("fsdp")
    place = jnp.where(index % 2 == 0, index // 2, count - 1 - index // 2)
    place = (place + offset + count) % count
    return jnp.where(place < count // 2, 2 * place, 2 * (count - 1 - place) + 1)


def ring_gather(array):
    count = lax.axis_size("fsdp")
    pieces, places = [array], [ring_index(0)]
    up = down = array
    for step in range(1, count // 2 + 1):
        up = ring_send(up, 1)
        pieces.append(up)
        places.append(ring_index(-step))
        if step <= (count - 1) // 2:
            down = ring_send(down, -1)
            pieces.append(down)
            places.append(ring_index(step))
    return lax.optimization_barrier(pieces), jnp.stack(places)


def ring_scatter(array):
    count = lax.axis_size("fsdp")

    def block(offset):
        return lax.dynamic_index_in_dim(array, ring_index(offset), 0, False).astype(F32)

    total = block(0)
    for direction, hops in ((1, count // 2), (-1, (count - 1) // 2)):
        moving = block(direction * hops)
        for step in range(1, hops + 1):
            moving = ring_send(moving.astype(BF), direction).astype(F32)
            if step < hops:
                moving = moving + block(direction * (hops - step))
        total = total + moving
    return total


def after(array, *earlier):
    return lax.optimization_barrier((array,) + earlier)[0]


def core_join(mine, axis, core):
    other = other_core(mine)
    return jnp.stack(
        [jnp.where(core == 0, mine, other), jnp.where(core == 0, other, mine)], axis
    )


def shards(
    images,
    cotangent,
    valid_count,
    first_gain,
    first_shift,
    triple_weight,
    query_bias,
    value_bias,
    output_weight,
    output_bias,
    attend_scale,
    second_gain,
    second_shift,
    expand_weight,
    expand_bias,
    reduce_weight,
    reduce_bias,
    feed_scale,
):
    image_count, local_len, width = images.shape
    own_rows = image_count * local_len
    far_count, fsdp_count = lax.axis_size("far"), lax.axis_size("fsdp")
    far, core = lax.axis_index("far"), lax.axis_index("core")
    seq_count, seq = 2 * far_count, 2 * far + core
    shard = width // fsdp_count
    units = expand_weight.shape[1]
    unit_part = units // (seq_count * fsdp_count)
    near_heads = width // HEAD_DIM // seq_count
    head_width = near_heads * HEAD_DIM

    def my_heads(array, axis):
        shape = array.shape
        array = array.reshape(
            shape[:axis] + (far_count, near_heads, 2, HEAD_DIM) + shape[axis + 1 :]
        )
        array = lax.dynamic_index_in_dim(array, far, axis, False)
        array = lax.dynamic_index_in_dim(array, core, axis + 1, False)
        return array.reshape(shape[:axis] + (head_width,) + shape[axis + 1 :])

    def my_units(array, axis):
        shape = array.shape
        array = array.reshape(
            shape[:axis] + (-1, seq_count, unit_part) + shape[axis + 1 :]
        )
        array = lax.dynamic_index_in_dim(array, seq, axis + 1, False)
        return array.reshape(shape[:axis] + (-1,) + shape[axis + 1 :])

    triple_mine = my_heads(triple_weight.reshape(shard, 3, width), 2).reshape(shard, 3 * head_width)
    triple_mine = jnp.pad(triple_mine, ((0, 0), (0, -(3 * head_width) % 128)))
    vectors = [
        first_gain, first_shift, query_bias, value_bias, output_bias, attend_scale,
        second_gain, second_shift, reduce_bias, feed_scale,
    ]
    vector_count = len(vectors)
    bias_columns = units // width
    small_mine = jnp.concatenate(
        [jnp.stack(vectors, 1), expand_bias.reshape(shard, bias_columns)], 1
    )
    small_mine = jnp.pad(small_mine, ((0, 0), (0, -small_mine.shape[1] % 128)))
    split_output = shard % (2 * HEAD_DIM) == 0
    if split_output:
        output_mine = lax.dynamic_index_in_dim(
            output_weight.reshape(shard // (2 * HEAD_DIM), 2, HEAD_DIM, width), core, 1, False
        ).reshape(shard // 2, 2, width // 2)
        output_mine = output_mine.transpose(1, 0, 2).reshape(shard, width // 2)
    else:
        output_mine = jnp.zeros((shard, 128), BF)
    pieces, places = ring_gather(jnp.concatenate([triple_mine, small_mine, output_mine], 1))
    rolled = (places - far * (fsdp_count // far_count)) % fsdp_count
    triple_whole, small, output_whole = assemble(
        jnp.stack([places, rolled]).astype(jnp.int32),
        pieces, triple_mine.shape[1], small_mine.shape[1],
    )
    triple_whole = triple_whole.reshape(width, -1)[:, : 3 * head_width]
    small = small.reshape(width, -1)[:, :16].astype(F32).T
    (gain_1, shift_1, bias_q, bias_v, bias_o, scale_a, gain_2, shift_2, bias_r, scale_f) = [
        small[i] for i in range(vector_count)
    ]
    bias_e = (
        small[vector_count : vector_count + bias_columns]
        .reshape(bias_columns, fsdp_count, shard)
        .transpose(1, 2, 0)
        .reshape(units)
    )
    bias_e = my_units(bias_e, 0)[None]
    if split_output:
        output_whole = output_whole.reshape(width // 2, width)
    else:
        output_whole = lax.dynamic_index_in_dim(
            fsdp_gather(output_weight).reshape(-1, 2, HEAD_DIM, width), core, 1, False
        )
        output_whole = output_whole.reshape(far_count, head_width, width)
        output_whole = jnp.roll(output_whole, -far, 0).reshape(width // 2, width)
    expand_mine = my_units(expand_weight, 1)
    reduce_mine = my_units(reduce_weight, 0)
    joined = units // seq_count == width and shard % 128 == 0
    if joined:
        feed_mine = after(jnp.concatenate([expand_mine, reduce_mine], 0), *pieces)
        feed_weights = fsdp_gather(feed_mine).reshape(fsdp_count, 2, shard, width)
        expand_whole = feed_weights[:, 0].reshape(width, width)
        reduce_whole = feed_weights[:, 1].reshape(width, width)
    else:
        expand_whole, reduce_whole = fsdp_gather(expand_mine), fsdp_gather(reduce_mine)

    groups = 2 if image_count % 2 == 0 else 1
    group_images = image_count // groups
    rows = group_images * local_len
    joint_bias = jnp.concatenate(
        [my_heads(bias_q, 0), jnp.zeros((head_width,), F32), my_heads(bias_v, 0)]
    )

    def group_rows(array, group):
        array = array[group * group_images : (group + 1) * group_images]
        return array.reshape(rows, width)

    def seq_gather(array):
        slots = []
        for slot in far_gather(array):
            slots += [slot, other_core(slot)]
        return jnp.stack(slots, 0)

    def seq_reduce(array):
        array = array.reshape(far_count, 2, rows, width)
        array = array[:, 0].astype(F32) + other_core(array[:, 1].astype(BF)).astype(F32)
        array = array.astype(BF)
        return array, lambda array: far_exchange([array[r] for r in range(far_count)])

    def total(arrays):
        return sum(array.astype(F32) for array in arrays)

    tokens, normed, triples = [], [], []
    for group in range(groups):
        tokens.append(seq_gather(group_rows(images, group)))
        first_normed, triple = project(tokens[-1], small, triple_whole, joint_bias[None])
        normed.append(first_normed)
        triples.append(triple)

    last_slot = ((far_count - 1 - far) % far_count) * 2 + (1 - core)
    dead_from = last_slot * local_len + valid_count - (seq_count - 1) * local_len
    limits = jnp.stack(
        [dead_from, jnp.broadcast_to((last_slot + 1) * local_len, dead_from.shape)], 1
    ).astype(jnp.int32)

    direct = local_len % 8 == 0 and head_width % (2 * HEAD_DIM) == 0

    def to_kernel(array):
        array = array.reshape(seq_count, group_images, local_len, -1)
        if direct:
            return array
        parts = array.shape[-1] // head_width
        array = array.transpose(1, 0, 2, 3).reshape(
            1, group_images, seq_count * local_len, parts, head_width
        )
        lanes = -head_width % (2 * HEAD_DIM)
        array = jnp.pad(array, ((0, 0),) * 4 + ((0, lanes),))
        return array.reshape(1, group_images, seq_count * local_len, -1)

    def from_kernel(array, parts):
        if direct:
            return array.reshape(seq_count, rows, -1)
        array = array.reshape(group_images, seq_count, local_len, parts, -1)
        array = array[..., :head_width].transpose(1, 0, 2, 3, 4)
        return array.reshape(seq_count, rows, parts * head_width)

    kernel_in, kernel_out, kernel_logs, attended_rows, branch_parts = [], [], [], [], []
    residuals, normal_2, factor_2, second_normed, activated, slopes = [], [], [], [], [], []
    for group in range(groups):
        picked = limits[group * group_images : (group + 1) * group_images]
        kernel_in.append(to_kernel(triples[group]))
        attended, logs = attend_forward(kernel_in[-1], picked)
        kernel_out.append(attended)
        kernel_logs.append(logs)
        attended = from_kernel(attended, 1).reshape(far_count, 2 * rows, head_width)
        attended = far_exchange([attended[r] for r in range(far_count)])
        attended_rows.append(jnp.concatenate(attended, 1))
    for group in range(groups):
        branch = dot(attended_rows[group], output_whole)
        branch = branch[:rows] + other_core(branch[rows:].astype(BF)).astype(F32) + bias_o
        branch_parts.append(branch)
        residual = group_rows(images, group).astype(F32) + scale_a * branch
        residuals.append(residual)
        normal, factor = normalize(residual)
        normal_2.append(normal)
        factor_2.append(factor)
        gathered = seq_gather((normal * gain_2 + shift_2).astype(BF))
        second_normed.append(gathered.reshape(seq_count * rows, width))
    for group in range(groups):
        active, slope = expand_rows(second_normed[group], expand_whole, bias_e)
        activated.append(active)
        slopes.append(slope)

    grad_feed, grad_expanded, upper_parts, moved = [], [], [], ()
    for group in range(groups):
        both = group_rows(cotangent, group)
        both = seq_gather(both).reshape(seq_count * rows, width)
        grad_feed.append((scale_f * both.astype(F32)).astype(BF))
    for group in range(groups):
        grad = dot_right_t(grad_feed[group], reduce_whole) * slopes[group].astype(F32)
        grad_expanded.append(grad.astype(BF))
        partial, send = seq_reduce(
            dot_right_t(grad_expanded[group], expand_whole).reshape(seq_count, rows, width)
        )
        moved = send(partial)
        upper_parts.append(total(moved))
    grad_expand_bias = sum(column_total(grad) for grad in grad_expanded)
    if joined:
        feed_sums = feed_grads(second_normed, grad_expanded, activated, grad_feed, fsdp_count)
        feed_sums = feed_sums.reshape(2 * width, width)
        upper_parts = [after(part, feed_sums) for part in upper_parts]
        feed_sums = fsdp_scatter(feed_sums).reshape(2, shard, width)
        expand_sums, reduce_sums = feed_sums[0], feed_sums[1]
    else:
        expand_sums = sum(dot_left_t(a, b) for a, b in zip(second_normed, grad_expanded))
        reduce_sums = sum(dot_left_t(a, b) for a, b in zip(activated, grad_feed))
        expand_sums = fsdp_scatter(expand_sums.astype(BF))
        reduce_sums = fsdp_scatter(reduce_sums.astype(BF))

    outputs, grad_feed_scale, grad_reduce_bias = [], 0.0, 0.0
    for group in range(groups):
        branch = dot(activated[group], reduce_whole).reshape(seq_count, rows, width)
        partial, send = seq_reduce(after(branch, *moved))
        branch = total(send(partial)) + bias_r
        outputs.append(residuals[group] + scale_f * branch)
        upstream = group_rows(cotangent, group).astype(F32)
        grad_feed_scale = grad_feed_scale + jnp.sum(upstream * branch, 0)
        grad_reduce_bias = grad_reduce_bias + column_total(grad_feed[group][:rows])
    outputs = jnp.concatenate(outputs, 0)

    grad_second_gain = grad_second_shift = grad_attend_scale = grad_output_bias = 0.0
    grad_residual, grad_sides, grad_attended = [], [], []
    for group in range(groups):
        upper = upper_parts[group]
        grad_second_gain = grad_second_gain + jnp.sum(upper * normal_2[group], 0)
        grad_second_shift = grad_second_shift + jnp.sum(upper, 0)
        grad = normalize_back(normal_2[group], factor_2[group], upper * gain_2)
        grad = group_rows(cotangent, group).astype(F32) + grad
        grad_residual.append(grad)
        grad_attend_scale = grad_attend_scale + jnp.sum(grad * branch_parts[group], 0)
        grad = (scale_a * grad).astype(BF)
        grad_output_bias = grad_output_bias + column_total(grad)
        grad_sides.append(jnp.concatenate([grad, other_core(grad)], 0))
        grad = dot_right_t(grad_sides[group], output_whole).astype(BF)
        grad_attended.append(
            [grad[:, r * head_width : (r + 1) * head_width] for r in range(far_count)]
        )
    grad_output_weight = sum(
        dot_left_t(attended_rows[group], grad_sides[group]) for group in range(groups)
    ).astype(BF)
    grad_output_weight = jnp.roll(
        grad_output_weight.reshape(far_count, head_width, width), far, 0
    ).reshape(width // 2, width)

    grad_heads = [to_kernel(jnp.stack(far_exchange(parts), 0)) for parts in grad_attended]
    upper_parts, grad_triples = [], []
    grad_first_gain = grad_first_shift = column_sums = 0.0
    for group in range(groups):
        picked = limits[group * group_images : (group + 1) * group_images]
        grad_heads_in = grad_heads[group]
        if group > 0:
            grad_heads_in = after(grad_heads_in, partial)
        grad_triple = from_kernel(
            attend_backward(
                kernel_in[group], kernel_out[group], grad_heads_in, kernel_logs[group], picked
            ),
            3,
        )
        if group > 0:
            grad_triple = after(grad_triple, *moved)
        grad_triples.append(grad_triple)
        partial, gain_part, shift_part, total_part = project_back(
            grad_triple, tokens[group], triple_whole
        )
        grad_first_gain = grad_first_gain + gain_part[0]
        grad_first_shift = grad_first_shift + shift_part[0]
        column_sums = column_sums + total_part[0]
        partial, send = seq_reduce(partial)
        moved = send(partial)
        upper_parts.append(total(moved))
    grad_triple_weight = sum(
        dot_left_t(
            normed[group].reshape(seq_count * rows, width),
            grad_triples[group].reshape(seq_count * rows, 3 * head_width),
        )
        for group in range(groups)
    ).astype(BF)
    grad_images = []
    for group in range(groups):
        normal, factor = normalize(group_rows(images, group).astype(F32))
        grad_images.append(
            grad_residual[group] + normalize_back(normal, factor, upper_parts[group] * gain_1)
        )
    grad_images = jnp.concatenate(grad_images, 0)

    def place_heads(vector):
        here = jnp.arange(far_count)[:, None, None, None] == far
        here = here & (jnp.arange(2)[None, None, :, None] == core)
        vector = vector.reshape(1, near_heads, 1, HEAD_DIM)
        return jnp.where(here, vector, 0.0).reshape(width)

    def place_units(vector):
        here = jnp.arange(seq_count)[None, :, None] == seq
        vector = jnp.where(here, vector.reshape(fsdp_count, 1, unit_part), 0.0)
        vector = vector.reshape(width, bias_columns)
        return [vector[:, i] for i in range(bias_columns)]

    sums = [
        grad_first_gain, grad_first_shift,
        place_heads(column_sums[:head_width]), place_heads(column_sums[2 * head_width :]),
        grad_output_bias, grad_attend_scale, grad_second_gain, grad_second_shift,
        grad_reduce_bias, grad_feed_scale,
    ] + place_units(grad_expand_bias)
    sums = jnp.stack(sums, 0).astype(BF).T
    sums = jnp.pad(sums, ((0, 0), (0, -sums.shape[1] % 128)))
    grad_packed = jnp.concatenate([grad_triple_weight, sums], 1)
    grad_packed = ring_scatter(grad_packed.reshape(fsdp_count, shard, -1)).astype(BF)
    grad_packed = jnp.roll(jnp.stack(far_gather(grad_packed), 0), far, 0)
    grad_packed = core_join(grad_packed, 1, core).astype(F32)
    grad_triple_weight = (
        grad_packed[:, :, :, : 3 * head_width]
        .reshape(far_count, 2, shard, 3, near_heads, HEAD_DIM)
        .transpose(2, 3, 0, 4, 1, 5)
        .reshape(shard, 3 * width)
    )
    sums = jnp.sum(grad_packed[:, :, :, 3 * head_width :], (0, 1)).T

    def far_total(array):
        total = array.astype(F32)
        for r in range(1, far_count):
            total = total + far_send(array, r).astype(F32)
        return total

    if split_output:
        grad_output_weight = far_total(fsdp_scatter(grad_output_weight)).astype(BF)
        grad_output_weight = core_join(
            grad_output_weight.reshape(-1, HEAD_DIM, width), 1, core
        ).reshape(shard, width)
    else:
        spread = grad_output_weight.reshape(-1, 1, HEAD_DIM, width)
        spread = jnp.where(jnp.arange(2)[None, :, None, None] == core, spread, 0)
        spread = fsdp_scatter(spread.reshape(width, width))
        grad_output_weight = far_total(spread)
        grad_output_weight = grad_output_weight + other_core(grad_output_weight)
    def seq_join(array):
        array = jnp.roll(jnp.stack(far_gather(array), 0), far, 0)
        return core_join(array, 1, core)

    feed_sums = seq_join(jnp.stack([expand_sums, reduce_sums]) if joined else expand_sums)
    if joined:
        expand_sums, reduce_sums = feed_sums[:, :, 0], feed_sums[:, :, 1]
    else:
        expand_sums, reduce_sums = feed_sums, seq_join(reduce_sums)
    grad_expand_weight = (
        expand_sums.astype(F32)
        .reshape(seq_count, shard, fsdp_count, unit_part)
        .transpose(1, 2, 0, 3)
        .reshape(shard, units)
    )
    grad_reduce_weight = reduce_sums.astype(F32).reshape(seq_count * unit_part, width)
    grad_expand_bias = sums[10 : 10 + bias_columns].T.reshape(units // fsdp_count)
    return (
        outputs.reshape(image_count, local_len, width).astype(BF),
        grad_images.reshape(image_count, local_len, width),
        sums[0],
        sums[1],
        grad_triple_weight,
        sums[2],
        sums[3],
        grad_output_weight.astype(F32),
        sums[4],
        sums[5],
        sums[6],
        sums[7],
        grad_expand_weight,
        grad_expand_bias,
        grad_reduce_weight,
        sums[8],
        sums[9],
    )


def layer_norm(inputs, gain, shift):
    average = jnp.mean(inputs, -1, keepdims=True)
    centered = inputs - average
    variance = jnp.mean(centered * centered, -1, keepdims=True)
    return centered * lax.rsqrt(variance + EPSILON) * gain + shift


def exact_gelu(values):
    return jax.nn.gelu(values, approximate=False)


def to_float(array):
    return array.astype(jnp.float32)


def plain_matmul(left, right):
    return jnp.dot(left, right, preferred_element_type=jnp.float32)


def plain_matmul_left_t(left, right):
    return lax.dot_general(
        left, right, (((0,), (0,)), ((), ())), preferred_element_type=jnp.float32
    )


def plain_matmul_right_t(left, right):
    return lax.dot_general(
        left, right, (((1,), (1,)), ((), ())), preferred_element_type=jnp.float32
    )


def plain_column_total(array):
    return plain_matmul(jnp.ones((1, array.shape[0]), jnp.bfloat16), array)[0]


def masked_scores(queries, key_rows, live_count, factor):
    scores = (
        jnp.einsum("qhd,khd->hqk", queries, key_rows, preferred_element_type=jnp.float32) * factor
    )
    live_keys = lax.broadcasted_iota(jnp.int32, (1, 1, key_rows.shape[0]), 2) < live_count
    return jnp.where(live_keys, scores, -1e30)


def plain_attend_forward(bundle):
    packed, live_count = bundle
    length, triple_count, local_width = packed.shape
    head_count = local_width // HEAD_DIM
    unpacked = packed.reshape(length, triple_count, head_count, HEAD_DIM)
    factor = HEAD_DIM ** (-0.5)
    scores = masked_scores(unpacked[:, 0], unpacked[:, 1], live_count, factor)
    highest = jnp.max(scores, -1, keepdims=True)
    powers = jnp.exp(scores - highest)
    row_total = jnp.sum(powers, -1, keepdims=True)
    weights_low = (powers / row_total).astype(jnp.bfloat16)
    mixed_rows = jnp.einsum(
        "hqk,khd->qhd", weights_low, unpacked[:, 2], preferred_element_type=jnp.float32
    )
    logsum = highest + jnp.log(row_total)
    return (mixed_rows.reshape(length, local_width).astype(jnp.bfloat16), logsum)


def plain_attend_backward(bundle):
    packed, grad_mixed, logsum, live_count = bundle
    length, triple_count, local_width = packed.shape
    head_count = local_width // HEAD_DIM
    unpacked = packed.reshape(length, triple_count, head_count, HEAD_DIM)
    factor = HEAD_DIM ** (-0.5)
    scores = masked_scores(unpacked[:, 0], unpacked[:, 1], live_count, factor)
    probs = jnp.exp(scores - logsum)
    grad_heads = grad_mixed.reshape(length, head_count, HEAD_DIM)
    grad_probs = jnp.einsum(
        "qhd,khd->hqk", grad_heads, unpacked[:, 2], preferred_element_type=jnp.float32
    )
    grad_values = jnp.einsum(
        "hqk,qhd->khd", probs.astype(jnp.bfloat16), grad_heads, preferred_element_type=jnp.float32
    )
    inner = jnp.sum(probs * grad_probs, -1, keepdims=True)
    grad_scores = (probs * (grad_probs - inner)).astype(jnp.bfloat16)
    grad_queries = (
        jnp.einsum("hqk,khd->qhd", grad_scores, unpacked[:, 1], preferred_element_type=jnp.float32)
        * factor
    )
    grad_keys = (
        jnp.einsum("hqk,qhd->khd", grad_scores, unpacked[:, 0], preferred_element_type=jnp.float32)
        * factor
    )
    stacked = jnp.stack([grad_queries, grad_keys, grad_values], 1)
    return stacked.reshape(length, triple_count, local_width).astype(jnp.bfloat16)


def plain_shards(
    images,
    cotangent,
    valid_count,
    first_gain,
    first_shift,
    triple_weight,
    query_bias,
    value_bias,
    output_weight,
    output_bias,
    attend_scale,
    second_gain,
    second_shift,
    expand_weight,
    expand_bias,
    reduce_weight,
    reduce_bias,
    feed_scale,
):
    image_count, local_len, width = images.shape
    gathered = (
        lax.all_gather(first_gain, "fsdp", axis=0, tiled=True),
        lax.all_gather(first_shift, "fsdp", axis=0, tiled=True),
        lax.all_gather(triple_weight, "fsdp", axis=0, tiled=True),
        lax.all_gather(query_bias, "fsdp", axis=0, tiled=True),
        lax.all_gather(value_bias, "fsdp", axis=0, tiled=True),
        lax.all_gather(output_weight, "fsdp", axis=0, tiled=True),
        lax.all_gather(output_bias, "fsdp", axis=0, tiled=True),
        lax.all_gather(attend_scale, "fsdp", axis=0, tiled=True),
        lax.all_gather(second_gain, "fsdp", axis=0, tiled=True),
        lax.all_gather(second_shift, "fsdp", axis=0, tiled=True),
        lax.all_gather(expand_weight, "fsdp", axis=0, tiled=True),
        lax.all_gather(expand_bias, "fsdp", axis=0, tiled=True),
        lax.all_gather(reduce_weight, "fsdp", axis=0, tiled=True),
        lax.all_gather(reduce_bias, "fsdp", axis=0, tiled=True),
        lax.all_gather(feed_scale, "fsdp", axis=0, tiled=True),
    )
    inputs = images.astype(jnp.float32).reshape(-1, width)
    first_normed = layer_norm(inputs, to_float(gathered[0]), to_float(gathered[1])).astype(
        jnp.bfloat16
    )
    joint_bias = to_float(jnp.concatenate([gathered[3], jnp.zeros_like(gathered[3]), gathered[4]]))
    triple = (plain_matmul(first_normed, gathered[2]) + joint_bias).astype(jnp.bfloat16)
    triple = triple.reshape(image_count, local_len, 3, width)
    by_heads = lax.all_to_all(triple, "seq", split_axis=3, concat_axis=1, tiled=True)
    attended, logsums = lax.map(plain_attend_forward, (by_heads, valid_count))
    by_tokens = lax.all_to_all(attended, "seq", split_axis=1, concat_axis=2, tiled=True)
    attended_rows = by_tokens.reshape(-1, width)
    branch_attend = plain_matmul(attended_rows, gathered[5]) + to_float(gathered[6])
    residual = inputs + to_float(gathered[7]) * branch_attend
    second_normed = layer_norm(residual, to_float(gathered[8]), to_float(gathered[9])).astype(
        jnp.bfloat16
    )
    expanded = plain_matmul(second_normed, gathered[10]) + to_float(gathered[11])
    activated = exact_gelu(expanded).astype(jnp.bfloat16)
    branch_feed = plain_matmul(activated, gathered[12]) + to_float(gathered[13])
    outputs = residual + to_float(gathered[14]) * branch_feed
    weights = (
        lax.all_gather(first_gain, "fsdp", axis=0, tiled=True),
        lax.all_gather(first_shift, "fsdp", axis=0, tiled=True),
        lax.all_gather(triple_weight, "fsdp", axis=0, tiled=True),
        lax.all_gather(query_bias, "fsdp", axis=0, tiled=True),
        lax.all_gather(value_bias, "fsdp", axis=0, tiled=True),
        lax.all_gather(output_weight, "fsdp", axis=0, tiled=True),
        lax.all_gather(output_bias, "fsdp", axis=0, tiled=True),
        lax.all_gather(attend_scale, "fsdp", axis=0, tiled=True),
        lax.all_gather(second_gain, "fsdp", axis=0, tiled=True),
        lax.all_gather(second_shift, "fsdp", axis=0, tiled=True),
        lax.all_gather(expand_weight, "fsdp", axis=0, tiled=True),
        lax.all_gather(expand_bias, "fsdp", axis=0, tiled=True),
        lax.all_gather(reduce_weight, "fsdp", axis=0, tiled=True),
        lax.all_gather(reduce_bias, "fsdp", axis=0, tiled=True),
        lax.all_gather(feed_scale, "fsdp", axis=0, tiled=True),
    )
    upstream = cotangent.astype(jnp.float32).reshape(-1, width)
    grad_feed_scale = jnp.sum(upstream * branch_feed, 0)
    grad_feed = (to_float(weights[14]) * upstream).astype(jnp.bfloat16)
    grad_reduce_bias = plain_column_total(grad_feed)
    grad_reduce_weight = plain_matmul_left_t(activated, grad_feed)
    grad_activated = plain_matmul_right_t(grad_feed, weights[12])
    unused, gelu_pull = jax.vjp(exact_gelu, expanded)
    grad_expanded = gelu_pull(grad_activated)[0].astype(jnp.bfloat16)
    grad_expand_bias = plain_column_total(grad_expanded)
    grad_expand_weight = plain_matmul_left_t(second_normed, grad_expanded)
    grad_second_normed = plain_matmul_right_t(grad_expanded, weights[10])
    unused, second_pull = jax.vjp(layer_norm, residual, to_float(weights[8]), to_float(weights[9]))
    grad_residual_norm, grad_second_gain, grad_second_shift = second_pull(grad_second_normed)
    grad_residual = upstream + grad_residual_norm
    grad_attend_scale = jnp.sum(grad_residual * branch_attend, 0)
    grad_attend = (to_float(weights[7]) * grad_residual).astype(jnp.bfloat16)
    grad_output_bias = plain_column_total(grad_attend)
    grad_output_weight = plain_matmul_left_t(attended_rows, grad_attend)
    grad_attended = plain_matmul_right_t(grad_attend, weights[5]).astype(jnp.bfloat16)
    grad_attended = grad_attended.reshape(image_count, local_len, width)
    grad_by_heads = lax.all_to_all(grad_attended, "seq", split_axis=2, concat_axis=1, tiled=True)
    grad_triple_heads = lax.map(plain_attend_backward, (by_heads, grad_by_heads, logsums, valid_count))
    grad_triple = lax.all_to_all(grad_triple_heads, "seq", split_axis=1, concat_axis=3, tiled=True)
    grad_triple = grad_triple.reshape(-1, 3 * width)
    column_sums = plain_column_total(grad_triple)
    grad_query_bias = column_sums[:width]
    grad_value_bias = column_sums[2 * width :]
    grad_triple_weight = plain_matmul_left_t(first_normed, grad_triple)
    grad_first_normed = plain_matmul_right_t(grad_triple, weights[2])
    unused, first_pull = jax.vjp(layer_norm, inputs, to_float(weights[0]), to_float(weights[1]))
    grad_inputs_norm, grad_first_gain, grad_first_shift = first_pull(grad_first_normed)
    grad_images = grad_residual + grad_inputs_norm
    owned = (
        lax.psum_scatter(
            grad_first_gain.astype(jnp.bfloat16), "fsdp", scatter_dimension=0, tiled=True
        ).astype(jnp.float32),
        lax.psum_scatter(
            grad_first_shift.astype(jnp.bfloat16), "fsdp", scatter_dimension=0, tiled=True
        ).astype(jnp.float32),
        lax.psum_scatter(
            grad_triple_weight.astype(jnp.bfloat16), "fsdp", scatter_dimension=0, tiled=True
        ).astype(jnp.float32),
        lax.psum_scatter(
            grad_query_bias.astype(jnp.bfloat16), "fsdp", scatter_dimension=0, tiled=True
        ).astype(jnp.float32),
        lax.psum_scatter(
            grad_value_bias.astype(jnp.bfloat16), "fsdp", scatter_dimension=0, tiled=True
        ).astype(jnp.float32),
        lax.psum_scatter(
            grad_output_weight.astype(jnp.bfloat16), "fsdp", scatter_dimension=0, tiled=True
        ).astype(jnp.float32),
        lax.psum_scatter(
            grad_output_bias.astype(jnp.bfloat16), "fsdp", scatter_dimension=0, tiled=True
        ).astype(jnp.float32),
        lax.psum_scatter(
            grad_attend_scale.astype(jnp.bfloat16), "fsdp", scatter_dimension=0, tiled=True
        ).astype(jnp.float32),
        lax.psum_scatter(
            grad_second_gain.astype(jnp.bfloat16), "fsdp", scatter_dimension=0, tiled=True
        ).astype(jnp.float32),
        lax.psum_scatter(
            grad_second_shift.astype(jnp.bfloat16), "fsdp", scatter_dimension=0, tiled=True
        ).astype(jnp.float32),
        lax.psum_scatter(
            grad_expand_weight.astype(jnp.bfloat16), "fsdp", scatter_dimension=0, tiled=True
        ).astype(jnp.float32),
        lax.psum_scatter(
            grad_expand_bias.astype(jnp.bfloat16), "fsdp", scatter_dimension=0, tiled=True
        ).astype(jnp.float32),
        lax.psum_scatter(
            grad_reduce_weight.astype(jnp.bfloat16), "fsdp", scatter_dimension=0, tiled=True
        ).astype(jnp.float32),
        lax.psum_scatter(
            grad_reduce_bias.astype(jnp.bfloat16), "fsdp", scatter_dimension=0, tiled=True
        ).astype(jnp.float32),
        lax.psum_scatter(
            grad_feed_scale.astype(jnp.bfloat16), "fsdp", scatter_dimension=0, tiled=True
        ).astype(jnp.float32),
    )
    summed = lax.psum(
        (
            owned[0],
            owned[1],
            owned[2],
            owned[3],
            owned[4],
            owned[5],
            owned[6],
            owned[7],
            owned[8],
            owned[9],
            owned[10],
            owned[11],
            owned[12],
            owned[13],
            owned[14],
        ),
        "seq",
    )
    return (
        outputs.reshape(image_count, local_len, width).astype(jnp.bfloat16),
        grad_images.reshape(image_count, local_len, width),
        summed[0],
        summed[1],
        summed[2],
        summed[3],
        summed[4],
        summed[5],
        summed[6],
        summed[7],
        summed[8],
        summed[9],
        summed[10],
        summed[11],
        summed[12],
        summed[13],
        summed[14],
    )


def solution(mesh):
    fsdp, seq = mesh.devices.shape
    if seq == 4:
        plan, tokens = shards, P("fsdp", ("far", "core"), None)
        mesh = Mesh(mesh.devices.reshape(fsdp, 2, 2), ("fsdp", "far", "core"))
    else:
        plan, tokens = plain_shards, P("fsdp", "seq", None)
    row, matrix = P("fsdp"), P("fsdp", None)
    return jax.shard_map(
        plan,
        mesh=mesh,
        in_specs=(
            tokens, tokens, row, row, row, matrix, row, row, matrix,
            row, row, row, row, matrix, row, matrix, row, row,
        ),
        out_specs=(
            tokens, tokens, row, row, matrix, row, row, matrix,
            row, row, row, row, matrix, row, matrix, row, row,
        ),
        check_vma=False,
    )
```

```python
import functools

import jax
import jax.numpy as jnp
from jax import lax
from jax.experimental import pallas as pl
from jax.experimental.pallas import tpu as pltpu
from jax.sharding import Mesh, PartitionSpec as P

HEAD_DIM = 64
EPSILON = 1e-06
BF = jnp.bfloat16
F32 = jnp.float32
MASKED = -1e30


def dot(left, right):
    return lax.dot_general(left, right, (((1,), (0,)), ((), ())), preferred_element_type=F32)


def dot_left_t(left, right):
    return lax.dot_general(left, right, (((0,), (0,)), ((), ())), preferred_element_type=F32)


def dot_right_t(left, right):
    return lax.dot_general(left, right, (((1,), (1,)), ((), ())), preferred_element_type=F32)


def column_total(array):
    return dot(jnp.ones((8, array.shape[0]), BF), array)[0]


def normalize(rows):
    average = jnp.mean(rows, -1, keepdims=True)
    centered = rows - average
    variance = jnp.mean(centered * centered, -1, keepdims=True)
    factor = lax.rsqrt(variance + EPSILON)
    return centered * factor, factor


def normalize_back(normal, factor, weighted):
    return factor * (
        weighted
        - jnp.mean(weighted, -1, keepdims=True)
        - normal * jnp.mean(weighted * normal, -1, keepdims=True)
    )


def spans(total, step):
    return [(start, min(step, total - start)) for start in range(0, total, step)]


def merge(ref, out):
    pieces, _, rows, _ = ref.shape
    for piece in range(pieces):
        out[pl.ds(piece * rows, rows), :] = ref[piece, 0].astype(F32)


def lane_parts(block, heads, head):
    lane = lax.broadcasted_iota(jnp.int32, (1, block), 1)
    if heads == 1:
        return lane < HEAD_DIM, lane - HEAD_DIM
    if head == 0:
        return lane < HEAD_DIM, lane - HEAD_DIM
    return lane >= HEAD_DIM, lane


def split_three(values):
    high = values.astype(BF).astype(F32)
    rest = values - high
    middle = rest.astype(BF).astype(F32)
    return high, middle, rest - middle


def dead_column(limit_ref, length):
    image = pl.program_id(0)
    row = lax.broadcasted_iota(jnp.int32, (length, 1), 0)
    dead = (row >= limit_ref[image, 0]) & (row < limit_ref[image, 1])
    return jnp.where(dead, MASKED, 0.0)


def attend_forward_kernel(limit_ref, q_ref, k_ref, v_ref, out_ref, log_ref, q_s, k_s, v_s, o_s):
    pieces, _, rows, block = q_ref.shape
    length = pieces * rows
    heads = max(block // HEAD_DIM, 1)
    merge(q_ref, q_s)
    merge(k_ref, k_s)
    merge(v_ref, v_s)
    dead = dead_column(limit_ref, length)
    aug = []
    for head in range(heads):
        own, spare = lane_parts(2 * HEAD_DIM, heads, head)
        q = jnp.where(own, q_s[...] * 0.125, jnp.where(spare == 0, 1.0, 0.0)).astype(BF)
        k = jnp.where(own, k_s[...], jnp.where(spare == 0, dead, 0.0)).astype(BF)
        v = jnp.where(own, v_s[...], jnp.where(spare == 0, 1.0, 0.0)).astype(BF)
        aug.append((q, k, v))
    for start, size in spans(length, 352):
        results = []
        for head in range(heads):
            q, k, v = aug[head]
            scores = dot_right_t(q[start : start + size], k)
            top = jnp.max(scores, -1, keepdims=True)
            powers = jnp.exp(scores - top).astype(BF)
            mixed = dot(powers, v)
            own, spare = lane_parts(2 * HEAD_DIM, heads, head)
            at = HEAD_DIM if head == 0 else 0
            total = mixed[:, at : at + 1]
            results.append((mixed / total, top + jnp.log(total)))
        own, _ = lane_parts(2 * HEAD_DIM, heads, 0)
        if heads == 1:
            o_s[pl.ds(start, size), :] = results[0][0]
            log_ref[0, 0, pl.ds(start, size), :] = jnp.broadcast_to(
                results[0][1], (size, 2 * HEAD_DIM)
            )
        else:
            o_s[pl.ds(start, size), :] = jnp.where(own, results[0][0], results[1][0])
            log_ref[0, 0, pl.ds(start, size), :] = jnp.where(own, results[1][1], results[0][1])
    for piece in range(pieces):
        out_ref[piece, 0] = o_s[pl.ds(piece * rows, rows), :].astype(BF)


def attend_backward_kernel(
    limit_ref, q_ref, k_ref, v_ref, o_ref, g_ref, log_ref, grad_ref,
    q_s, k_s, v_s, o_s, g_s, dq_s, dk_s, dv_s,
):
    pieces, _, rows, block = q_ref.shape
    length = pieces * rows
    heads = max(block // HEAD_DIM, 1)
    merge(q_ref, q_s)
    merge(k_ref, k_s)
    merge(v_ref, v_s)
    merge(o_ref, o_s)
    merge(g_ref, g_s)
    dead = dead_column(limit_ref, length)
    product = o_s[...] * g_s[...]
    for head in range(heads):
        own, spare = lane_parts(2 * HEAD_DIM, heads, head)
        log_parts = split_three(log_ref[0, 0])
        inner = jnp.sum(jnp.where(own, product, 0.0), -1, keepdims=True)
        inner_parts = split_three(inner)
        zero = jnp.zeros((length, 2 * HEAD_DIM), F32)
        q_tail, k_tail, v_tail, g_tail = zero, zero, zero, zero
        for place in range(3):
            q_tail = jnp.where(spare == place, -log_parts[place], q_tail)
            g_tail = jnp.where(spare == place, -inner_parts[place], g_tail)
            k_tail = jnp.where(spare == place, 1.0, k_tail)
            v_tail = jnp.where(spare == place, 1.0, v_tail)
        q_tail = jnp.where(spare == 3, 1.0, q_tail)
        k_tail = jnp.where(spare == 3, dead, k_tail)
        q = jnp.where(own, q_s[...] * 0.125, q_tail).astype(BF)
        k = jnp.where(own, k_s[...], k_tail).astype(BF)
        v = jnp.where(own, v_s[...], v_tail).astype(BF)
        g = jnp.where(own, g_s[...], g_tail).astype(BF)
        k_t = jnp.where(own, k_s[...] * 0.125, 0.0).T.astype(BF)
        dk = dv = None
        for start, size in spans(length, 512):
            q_part, g_part = q[start : start + size], g[start : start + size]
            probs = jnp.exp(dot_right_t(k, q_part))
            slopes = (probs * dot_right_t(v, g_part)).astype(BF)
            probs = probs.astype(BF)
            dv_part = dot(probs, g_part)
            dk_part = dot(slopes, q_part)
            dv = dv_part if dv is None else dv + dv_part
            dk = dk_part if dk is None else dk + dk_part
            dq_part = dot(k_t, slopes).T
            if head == 0:
                dq_s[pl.ds(start, size), :] = dq_part
            else:
                dq_s[pl.ds(start, size), :] += dq_part
        if head == 0:
            dk_s[...] = dk
            dv_s[...] = dv
        else:
            dk_s[...] = jnp.where(own, dk, dk_s[...])
            dv_s[...] = jnp.where(own, dv, dv_s[...])
    stride = grad_ref.shape[3] // 3
    for piece in range(pieces):
        part = pl.ds(piece * rows, rows)
        for which, grad in enumerate((dq_s, dk_s, dv_s)):
            at = pl.multiple_of(which * stride + pl.program_id(1) * block, block)
            grad_ref[piece, 0, :, pl.ds(at, block)] = grad[part, :].astype(BF)


def attend_specs(pieces, rows, first):
    def at(limit_index):
        return pl.BlockSpec(
            (pieces, 1, rows, 2 * HEAD_DIM),
            lambda image, pair, limits: (0, image, 0, limit_index + pair),
        )

    return at(first)


def attend_forward(triple, limits):
    pieces, images, rows, columns = triple.shape
    head_width = columns // 3
    length = pieces * rows
    pairs = head_width // (2 * HEAD_DIM)
    wide = pltpu.VMEM((length, 2 * HEAD_DIM), F32)
    spec = functools.partial(attend_specs, pieces, rows)
    heads = images * head_width // HEAD_DIM
    return pl.pallas_call(
        attend_forward_kernel,
        grid_spec=pltpu.PrefetchScalarGridSpec(
            num_scalar_prefetch=1,
            grid=(images, pairs),
            in_specs=[spec(0), spec(pairs), spec(2 * pairs)],
            out_specs=[
                spec(0),
                pl.BlockSpec((1, 1, length, 2 * HEAD_DIM), lambda i, p, limits: (i, p, 0, 0)),
            ],
            scratch_shapes=[wide] * 4,
        ),
        out_shape=[
            jax.ShapeDtypeStruct((pieces, images, rows, head_width), BF),
            jax.ShapeDtypeStruct((images, pairs, length, 2 * HEAD_DIM), F32),
        ],
        compiler_params=pltpu.CompilerParams(vmem_limit_bytes=50 * 2**20),
        cost_estimate=pl.CostEstimate(
            flops=heads * length * length * 1024,
            bytes_accessed=4 * triple.size,
            transcendentals=heads * length * length,
        ),
        name="attend_forward",
    )(limits, triple, triple, triple)


def attend_backward(triple, attended, grad, logs, limits):
    pieces, images, rows, columns = triple.shape
    head_width = columns // 3
    length = pieces * rows
    pairs = head_width // (2 * HEAD_DIM)
    wide = pltpu.VMEM((length, 2 * HEAD_DIM), F32)
    spec = functools.partial(attend_specs, pieces, rows)
    heads = images * head_width // HEAD_DIM
    return pl.pallas_call(
        attend_backward_kernel,
        grid_spec=pltpu.PrefetchScalarGridSpec(
            num_scalar_prefetch=1,
            grid=(images, pairs),
            in_specs=[
                spec(0),
                spec(pairs),
                spec(2 * pairs),
                spec(0),
                spec(0),
                pl.BlockSpec((1, 1, length, 2 * HEAD_DIM), lambda i, p, limits: (i, p, 0, 0)),
            ],
            out_specs=pl.BlockSpec(
                (pieces, 1, rows, columns), lambda image, pair, limits: (0, image, 0, 0)
            ),
            scratch_shapes=[wide] * 8,
        ),
        out_shape=jax.ShapeDtypeStruct(triple.shape, BF),
        compiler_params=pltpu.CompilerParams(vmem_limit_bytes=56 * 2**20),
        cost_estimate=pl.CostEstimate(
            flops=heads * length * length * 2560,
            bytes_accessed=8 * triple.size,
            transcendentals=heads * length * length,
        ),
        name="attend_backward",
    )(limits, triple, triple, triple, attended, grad, logs)


def project_kernel(rows_ref, small_ref, weight_ref, bias_ref, normed_ref, triple_ref):
    normal, _ = normalize(rows_ref[0].astype(F32))
    normed = (normal * small_ref[0:1, :] + small_ref[1:2, :]).astype(BF)
    normed_ref[0] = normed
    triple_ref[0] = (dot(normed, weight_ref[...]) + bias_ref[...]).astype(BF)


def project(tokens, small, weight, bias):
    pieces, rows, width = tokens.shape
    columns = weight.shape[1]

    def whole(array):
        return pl.BlockSpec(array.shape, lambda i: (0, 0))

    def piece(columns):
        return pl.BlockSpec((1, rows, columns), lambda i: (i, 0, 0))

    return pl.pallas_call(
        project_kernel,
        grid=(pieces,),
        in_specs=[piece(width), whole(small), whole(weight), whole(bias)],
        out_specs=[piece(width), piece(columns)],
        out_shape=[
            jax.ShapeDtypeStruct((pieces, rows, width), BF),
            jax.ShapeDtypeStruct((pieces, rows, columns), BF),
        ],
        compiler_params=pltpu.CompilerParams(vmem_limit_bytes=40 * 2**20),
        cost_estimate=pl.CostEstimate(
            flops=2 * pieces * rows * width * columns,
            bytes_accessed=2 * pieces * rows * (2 * width + columns),
            transcendentals=0,
        ),
        name="project",
    )(tokens, small, weight, bias)


def project_back_kernel(grad_ref, rows_ref, weight_ref, part_ref, gain_ref, shift_ref, total_ref):
    @pl.when(pl.program_id(0) == 0)
    def _():
        gain_ref[...] = jnp.zeros_like(gain_ref)
        shift_ref[...] = jnp.zeros_like(shift_ref)
        total_ref[...] = jnp.zeros_like(total_ref)

    normal, _ = normalize(rows_ref[0].astype(F32))
    part = dot_right_t(grad_ref[0], weight_ref[...])
    part_ref[0] = part.astype(BF)
    gain_ref[...] += jnp.sum(part * normal, 0, keepdims=True)
    shift_ref[...] += jnp.sum(part, 0, keepdims=True)
    total_ref[...] += jnp.sum(grad_ref[0].astype(F32), 0, keepdims=True)


def project_back(grad, tokens, weight):
    pieces, rows, width = tokens.shape
    columns = weight.shape[1]

    def piece(columns):
        return pl.BlockSpec((1, rows, columns), lambda i: (i, 0, 0))

    def whole(shape):
        return pl.BlockSpec(shape, lambda i: (0, 0))

    return pl.pallas_call(
        project_back_kernel,
        grid=(pieces,),
        in_specs=[piece(columns), piece(width), whole(weight.shape)],
        out_specs=[piece(width), whole((1, width)), whole((1, width)), whole((1, columns))],
        out_shape=[
            jax.ShapeDtypeStruct((pieces, rows, width), BF),
            jax.ShapeDtypeStruct((1, width), F32),
            jax.ShapeDtypeStruct((1, width), F32),
            jax.ShapeDtypeStruct((1, columns), F32),
        ],
        compiler_params=pltpu.CompilerParams(vmem_limit_bytes=40 * 2**20),
        cost_estimate=pl.CostEstimate(
            flops=2 * pieces * rows * width * columns,
            bytes_accessed=2 * pieces * rows * (2 * width + columns),
            transcendentals=0,
        ),
        name="project_back",
    )(grad, tokens, weight)


def gelu_parts(values):
    size = jnp.abs(values) * 0.7071067811865476
    bell = jnp.exp(-size * size)
    t = 1.0 / (1.0 + 0.3275911 * size)
    tail = t * (
        0.254829592
        + t * (-0.284496736 + t * (1.421413741 + t * (-1.453152027 + t * 1.061405429)))
    )
    tail = 0.5 * tail * bell
    return jnp.where(values >= 0.0, 1.0 - tail, tail), 0.3989422804014327 * bell


def expand_kernel(rows_ref, weight_ref, bias_ref, active_ref, slope_ref):
    count, width = rows_ref.shape
    weight = weight_ref[...].reshape(width, weight_ref.shape[2])
    for start, size in spans(count, 352):
        expanded = dot(rows_ref[start : start + size, :], weight) + bias_ref[...]
        below, density = gelu_parts(expanded)
        active_ref[start : start + size, :] = (expanded * below).astype(BF)
        slope_ref[start : start + size, :] = (below + expanded * density).astype(BF)


def expand_rows(rows, feed_weights, bias):
    count, width = rows.shape
    devices = feed_weights.shape[0]
    shard = width // devices
    units = bias.shape[1]
    tile = 256
    across = width // tile
    shape = jax.ShapeDtypeStruct((count, units), BF)
    return pl.pallas_call(
        expand_kernel,
        grid=(units // tile,),
        in_specs=[
            pl.BlockSpec((count, width), lambda i: (0, 0)),
            pl.BlockSpec((devices, shard, tile), lambda i: (0, i // across, i % across)),
            pl.BlockSpec((1, tile), lambda i: (0, i)),
        ],
        out_specs=[pl.BlockSpec((count, tile), lambda i: (0, i))] * 2,
        out_shape=[shape] * 2,
        compiler_params=pltpu.CompilerParams(vmem_limit_bytes=48 * 2**20),
        cost_estimate=pl.CostEstimate(
            flops=4 * count * units * width,
            bytes_accessed=2 * (count * width + width * units + 2 * count * units),
            transcendentals=2 * count * units,
        ),
        name="expand_rows",
    )(rows, feed_weights, bias)


def feed_grads_kernel(rows_ref, active_ref, expanded_ref, feed_ref, out_ref):
    shard, width = rows_ref.shape[1], out_ref.shape[2]
    blocks = expanded_ref.shape[1] // width
    for block in range(blocks):
        out_ref[0, block * shard : (block + 1) * shard, :] = dot_left_t(
            rows_ref[...], expanded_ref[:, block * width : (block + 1) * width]
        ).astype(BF)
    out_ref[0, blocks * shard :, :] = dot_left_t(active_ref[...], feed_ref[...]).astype(BF)


def feed_grads(rows, active, grad_expanded, grad_feed, devices):
    count, width = rows.shape
    units = active.shape[1]
    shard, unit_part = width // devices, units // devices
    blocks = units // width
    if shard % 128 != 0 or unit_part % 128 != 0:
        expand = dot_left_t(rows, grad_expanded).astype(BF).reshape(devices, shard, blocks, width)
        expand = expand.transpose(0, 2, 1, 3).reshape(devices, blocks * shard, width)
        reduce = dot_left_t(active, grad_feed).astype(BF).reshape(devices, unit_part, width)
        return jnp.concatenate([expand, reduce], 1)
    height = blocks * shard + unit_part
    return pl.pallas_call(
        feed_grads_kernel,
        grid=(devices,),
        in_specs=[
            pl.BlockSpec((count, shard), lambda i: (0, i)),
            pl.BlockSpec((count, unit_part), lambda i: (0, i)),
            pl.BlockSpec((count, units), lambda i: (0, 0)),
            pl.BlockSpec((count, width), lambda i: (0, 0)),
        ],
        out_specs=pl.BlockSpec((1, height, width), lambda i: (i, 0, 0)),
        out_shape=jax.ShapeDtypeStruct((devices, height, width), BF),
        compiler_params=pltpu.CompilerParams(vmem_limit_bytes=52 * 2**20),
        cost_estimate=pl.CostEstimate(
            flops=4 * count * units * width,
            bytes_accessed=2 * (2 * count * (width + units) + 2 * width * units),
            transcendentals=0,
        ),
        name="feed_grads",
    )(rows, active, grad_expanded, grad_feed)


def far_send(array, shift):
    count = lax.axis_size("far")
    return lax.ppermute(array, "far", [(i, (i + shift) % count) for i in range(count)])


def far_gather(array):
    count = lax.axis_size("far")
    return [array] + [far_send(array, count - r) for r in range(1, count)]


def far_exchange(slots):
    count = len(slots)
    out = [slots[0]] + [None] * (count - 1)
    for r in range(1, count):
        out[count - r] = far_send(slots[r], r)
    return out


def far_sum(slots):
    arrived = far_exchange(slots)
    return sum(part.astype(F32) for part in arrived)


def other_core(array):
    return lax.ppermute(array, "core", [(0, 1), (1, 0)])


def fsdp_gather(array):
    return lax.all_gather(array, "fsdp", axis=0, tiled=True)


def fsdp_scatter(array):
    return lax.psum_scatter(array, "fsdp", scatter_dimension=0, tiled=True)


def ring_send(array, step):
    count = lax.axis_size("fsdp")
    order = list(range(0, count, 2)) + list(range(1, count, 2))[::-1]
    pairs = [(order[i], order[(i + step) % count]) for i in range(count)]
    return lax.ppermute(array, "fsdp", pairs)


def ring_index(offset):
    count, index = lax.axis_size("fsdp"), lax.axis_index("fsdp")
    place = jnp.where(index % 2 == 0, index // 2, count - 1 - index // 2)
    place = (place + offset + count) % count
    return jnp.where(place < count // 2, 2 * place, 2 * (count - 1 - place) + 1)


def ring_scatter(array):
    count = lax.axis_size("fsdp")

    def block(offset):
        return lax.dynamic_index_in_dim(array, ring_index(offset), 0, False).astype(F32)

    total = block(0)
    for direction, hops in ((1, count // 2), (-1, (count - 1) // 2)):
        moving = block(direction * hops)
        for step in range(1, hops + 1):
            moving = ring_send(moving.astype(BF), direction).astype(F32)
            if step < hops:
                moving = moving + block(direction * (hops - step))
        total = total + moving
    return total


def after(array, *earlier):
    return lax.optimization_barrier((array,) + earlier)[0]


def core_join(mine, axis, core):
    other = other_core(mine)
    return jnp.stack(
        [jnp.where(core == 0, mine, other), jnp.where(core == 0, other, mine)], axis
    )


def shards(
    images,
    cotangent,
    valid_count,
    first_gain,
    first_shift,
    triple_weight,
    query_bias,
    value_bias,
    output_weight,
    output_bias,
    attend_scale,
    second_gain,
    second_shift,
    expand_weight,
    expand_bias,
    reduce_weight,
    reduce_bias,
    feed_scale,
):
    image_count, local_len, width = images.shape
    own_rows = image_count * local_len
    far_count, fsdp_count = lax.axis_size("far"), lax.axis_size("fsdp")
    far, core = lax.axis_index("far"), lax.axis_index("core")
    seq_count = 2 * far_count
    shard = width // fsdp_count
    units = expand_weight.shape[1]
    unit_part = units // (2 * fsdp_count)
    near_heads = width // HEAD_DIM // seq_count
    head_width = near_heads * HEAD_DIM

    def my_heads(array, axis):
        shape = array.shape
        array = array.reshape(
            shape[:axis] + (far_count, near_heads, 2, HEAD_DIM) + shape[axis + 1 :]
        )
        array = lax.dynamic_index_in_dim(array, far, axis, False)
        array = lax.dynamic_index_in_dim(array, core, axis + 1, False)
        return array.reshape(shape[:axis] + (head_width,) + shape[axis + 1 :])

    triple_mine = my_heads(triple_weight.reshape(shard, 3, width), 2).reshape(shard, 3 * head_width)
    bias_mine = lax.dynamic_index_in_dim(expand_bias.reshape(2, unit_part), core, 0, False)
    bias_columns = unit_part // shard
    vectors = [
        first_gain, first_shift, query_bias, value_bias, output_bias, attend_scale,
        second_gain, second_shift, reduce_bias, feed_scale,
    ]
    vector_count = len(vectors)
    small_mine = jnp.concatenate(
        [jnp.stack(vectors, 1), bias_mine.reshape(shard, bias_columns)], 1
    )
    small_mine = jnp.pad(small_mine, ((0, 0), (0, -small_mine.shape[1] % 128)))
    pairs = shard // (2 * HEAD_DIM)
    output_mine = lax.dynamic_index_in_dim(
        output_weight.reshape(pairs, 2, HEAD_DIM, width), core, 1, False
    )
    output_mine = output_mine.reshape(shard // 2, 2, width // 2).transpose(1, 0, 2)
    output_mine = output_mine.reshape(shard, width // 2)
    first = 3 * head_width
    second = first + small_mine.shape[1]
    packed = fsdp_gather(jnp.concatenate([triple_mine, small_mine, output_mine], 1))
    triple_whole = packed[:, :first]
    small = packed[:, first : first + 16].astype(F32).T
    output_whole = packed[:, second:].reshape(fsdp_count, 2, shard // 2, width // 2)
    output_whole = output_whole.transpose(0, 2, 1, 3).reshape(far_count, head_width, width)
    output_whole = jnp.roll(output_whole, -far, 0).reshape(width // 2, width)
    (gain_1, shift_1, bias_q, bias_v, bias_o, scale_a, gain_2, shift_2, bias_r, scale_f) = [
        small[i] for i in range(vector_count)
    ]
    bias_e = (
        small[vector_count : vector_count + bias_columns]
        .reshape(bias_columns, fsdp_count, shard)
        .transpose(1, 2, 0)
        .reshape(1, fsdp_count * unit_part)
    )

    blocks = units // 2 // width
    expand_mine = lax.dynamic_index_in_dim(
        expand_weight.reshape(shard, fsdp_count, 2, unit_part), core, 2, False
    ).reshape(shard, blocks, width)
    reduce_mine = lax.dynamic_index_in_dim(
        reduce_weight.reshape(2, unit_part, width), core, 0, False
    )
    feed_mine = jnp.concatenate([expand_mine[:, i] for i in range(blocks)] + [reduce_mine], 0)
    height = blocks * shard + unit_part
    feed_weights = fsdp_gather(feed_mine).reshape(fsdp_count, height, width)
    expand_blocks = [
        feed_weights[:, i * shard : (i + 1) * shard].reshape(width, width) for i in range(blocks)
    ]
    reduce_whole = feed_weights[:, blocks * shard :].reshape(units // 2, width)

    groups = 2 if image_count % 2 == 0 else 1
    group_images = image_count // groups
    rows = group_images * local_len
    joint_bias = jnp.concatenate(
        [my_heads(bias_q, 0), jnp.zeros((head_width,), F32), my_heads(bias_v, 0)]
    )
    tokens, normed, triples = [], [], []
    for group in range(groups):
        mine = images[group * group_images : (group + 1) * group_images].reshape(rows, width)
        slots = []
        for slot in far_gather(mine):
            slots += [slot, other_core(slot)]
        tokens.append(jnp.stack(slots, 0))
        first_normed, triple = project(
            tokens[-1], small, triple_whole, joint_bias[None]
        )
        normed.append(first_normed)
        triples.append(triple)

    last_slot = ((far_count - 1 - far) % far_count) * 2 + (1 - core)
    dead_from = last_slot * local_len + valid_count - (seq_count - 1) * local_len
    limits = jnp.stack(
        [dead_from, jnp.broadcast_to((last_slot + 1) * local_len, dead_from.shape)], 1
    ).astype(jnp.int32)

    direct = local_len % 8 == 0 and head_width % (2 * HEAD_DIM) == 0

    def to_kernel(array):
        array = array.reshape(seq_count, group_images, local_len, -1)
        if direct:
            return array
        parts = array.shape[-1] // head_width
        array = array.transpose(1, 0, 2, 3).reshape(
            1, group_images, seq_count * local_len, parts, head_width
        )
        lanes = -head_width % (2 * HEAD_DIM)
        array = jnp.pad(array, ((0, 0),) * 4 + ((0, lanes),))
        return array.reshape(1, group_images, seq_count * local_len, -1)

    def from_kernel(array, parts):
        if direct:
            return array.reshape(seq_count, rows, -1)
        array = array.reshape(group_images, seq_count, local_len, parts, -1)
        array = array[..., :head_width].transpose(1, 0, 2, 3, 4)
        return array.reshape(seq_count, rows, parts * head_width)

    kernel_in, kernel_out, kernel_logs, attended_rows, branch_parts = [], [], [], [], []
    for group in range(groups):
        picked = limits[group * group_images : (group + 1) * group_images]
        kernel_in.append(to_kernel(triples[group]))
        attended, logs = attend_forward(kernel_in[-1], picked)
        kernel_out.append(attended)
        kernel_logs.append(logs)
        attended = from_kernel(attended, 1).reshape(far_count, 2 * rows, head_width)
        attended = far_exchange([attended[r] for r in range(far_count)])
        attended_rows.append(jnp.concatenate(attended, 1))
        branch = dot(attended_rows[-1], output_whole)
        branch_parts.append(
            branch[:rows] + other_core(branch[rows:].astype(BF)).astype(F32) + bias_o
        )
    branch_attend = jnp.concatenate(branch_parts, 0)
    inputs = images.reshape(own_rows, width).astype(F32)
    residual = inputs + scale_a * branch_attend
    normal_2, factor_2 = normalize(residual)
    second_mine = (normal_2 * gain_2 + shift_2).astype(BF)
    second_normed = jnp.concatenate([second_mine, other_core(second_mine)], 0)
    activated, slope = expand_rows(second_normed, feed_weights, bias_e)
    branch = dot(activated, reduce_whole)
    branch_feed = (
        branch[:own_rows] + other_core(branch[own_rows:].astype(BF)).astype(F32) + bias_r
    )
    outputs = residual + scale_f * branch_feed

    cotangent = cotangent.reshape(own_rows, width)
    upstream = cotangent.astype(F32)
    both = jnp.concatenate([cotangent, other_core(cotangent)], 0)
    grad_feed = (scale_f * both.astype(F32)).astype(BF)
    grad_feed_scale = jnp.sum(upstream * branch_feed, 0)
    grad_reduce_bias = column_total(grad_feed[:own_rows])
    grad_expanded = (dot_right_t(grad_feed, reduce_whole) * slope.astype(F32)).astype(BF)
    feed_sums = feed_grads(second_normed, activated, grad_expanded, grad_feed, fsdp_count)
    grad_expanded, feed_sums = lax.optimization_barrier((grad_expanded, feed_sums))
    feed_sums = fsdp_scatter(feed_sums.reshape(fsdp_count * height, width))
    partial = sum(
        dot_right_t(grad_expanded[:, i * width : (i + 1) * width], expand_blocks[i])
        for i in range(blocks)
    )
    grad_expand_bias = column_total(grad_expanded)
    upper = partial[:own_rows] + other_core(partial[own_rows:].astype(BF)).astype(F32)
    grad_second_gain = jnp.sum(upper * normal_2, 0)
    grad_second_shift = jnp.sum(upper, 0)
    grad_residual = upstream + normalize_back(normal_2, factor_2, upper * gain_2)
    grad_attend_scale = jnp.sum(grad_residual * branch_attend, 0)
    grad_attend = (scale_a * grad_residual).astype(BF)
    grad_output_bias = column_total(grad_attend)
    grad_attend = jnp.concatenate([grad_attend, other_core(grad_attend)], 0)
    grad_attended = dot_right_t(grad_attend, output_whole).astype(BF)
    grad_attended = grad_attended.reshape(2, groups, rows, far_count, head_width)
    grad_sides = grad_attend.reshape(2, groups, rows, width)
    grad_output_weight = sum(
        dot_left_t(attended_rows[group], grad_sides[:, group].reshape(2 * rows, width))
        for group in range(groups)
    ).astype(BF)
    grad_output_weight = jnp.roll(
        grad_output_weight.reshape(far_count, head_width, width), far, 0
    ).reshape(width // 2, width)

    grad_heads = [
        to_kernel(
            jnp.stack(
                far_exchange(
                    [
                        grad_attended[:, group, :, r].reshape(2 * rows, head_width)
                        for r in range(far_count)
                    ]
                ),
                0,
            )
        )
        for group in range(groups)
    ]
    upper_parts, grad_triples = [], []
    grad_first_gain = grad_first_shift = column_sums = 0.0
    for group in range(groups):
        picked = limits[group * group_images : (group + 1) * group_images]
        grad_heads_in = grad_heads[group]
        if group > 0:
            grad_heads_in = after(grad_heads_in, partial)
        grad_triple = from_kernel(
            attend_backward(
                kernel_in[group], kernel_out[group], grad_heads_in, kernel_logs[group], picked
            ),
            3,
        )
        if group > 0:
            grad_triple = after(grad_triple, *moved)
        grad_triples.append(grad_triple)
        partial, gain_part, shift_part, total_part = project_back(
            grad_triple, tokens[group], triple_whole
        )
        grad_first_gain = grad_first_gain + gain_part[0]
        grad_first_shift = grad_first_shift + shift_part[0]
        column_sums = column_sums + total_part[0]
        partial = partial.reshape(far_count, 2, rows, width)
        partial = partial[:, 0].astype(F32) + other_core(partial[:, 1]).astype(F32)
        partial = partial.astype(BF)
        moved = far_exchange([partial[r] for r in range(far_count)])
        upper_parts.append(sum(part.astype(F32) for part in moved))
    grad_triple_weight = sum(
        dot_left_t(
            normed[group].reshape(seq_count * rows, width),
            grad_triples[group].reshape(seq_count * rows, 3 * head_width),
        )
        for group in range(groups)
    ).astype(BF)
    upper = jnp.concatenate(upper_parts, 0)
    normal, factor = normalize(inputs)
    grad_images = grad_residual + normalize_back(normal, factor, upper * gain_1)

    def place_heads(vector):
        here = jnp.arange(far_count)[:, None, None, None] == far
        here = here & (jnp.arange(2)[None, None, :, None] == core)
        vector = vector.reshape(1, near_heads, 1, HEAD_DIM)
        return jnp.where(here, vector, 0.0).reshape(width)

    def place_units(vector):
        vector = vector.reshape(fsdp_count, shard, bias_columns)
        vector = vector.transpose(2, 0, 1).reshape(1, bias_columns, width)
        vector = jnp.where(jnp.arange(2)[:, None, None] == core, vector, 0.0)
        return [vector[i, j] for i in range(2) for j in range(bias_columns)]

    sums = [
        grad_first_gain, grad_first_shift,
        place_heads(column_sums[:head_width]), place_heads(column_sums[2 * head_width :]),
        grad_output_bias, grad_attend_scale, grad_second_gain, grad_second_shift,
        grad_reduce_bias, grad_feed_scale,
    ] + place_units(grad_expand_bias)
    sums = jnp.stack(sums, 0).astype(BF).T
    sums = jnp.pad(sums, ((0, 0), (0, -sums.shape[1] % 128)))
    grad_output_weight = grad_output_weight.reshape(fsdp_count, shard // 2, 2, width // 2)
    grad_output_weight = grad_output_weight.transpose(0, 2, 1, 3).reshape(width, width // 2)
    grad_packed = jnp.concatenate([grad_triple_weight, sums, grad_output_weight], 1)
    grad_packed = ring_scatter(grad_packed.reshape(fsdp_count, shard, -1)).astype(BF)
    feed_sums = after(feed_sums, grad_packed)
    grad_packed = jnp.roll(jnp.stack(far_gather(grad_packed), 0), far, 0)
    grad_packed = core_join(grad_packed, 1, core)
    grad_triple_weight = (
        grad_packed[:, :, :, :first]
        .reshape(far_count, 2, shard, 3, near_heads, HEAD_DIM)
        .transpose(2, 3, 0, 4, 1, 5)
        .reshape(shard, 3 * width)
        .astype(F32)
    )
    sums = jnp.sum(grad_packed[:, :, :, first : first + 16].astype(F32), (0, 1)).T
    grad_output_weight = (
        jnp.sum(grad_packed[:, :, :, second:].astype(F32), 0)
        .reshape(2, 2, pairs, HEAD_DIM, width // 2)
        .transpose(2, 0, 3, 1, 4)
        .reshape(shard, width)
    )

    def far_total(array):
        total = array.astype(F32)
        for r in range(1, far_count):
            total = total + far_send(array, r).astype(F32)
        return total

    feed_sums = core_join(far_total(feed_sums).astype(BF), 0, core).astype(F32)
    grad_expand_weight = (
        feed_sums[:, : blocks * shard]
        .reshape(2, blocks, shard, -1, unit_part)
        .transpose(2, 1, 3, 0, 4)
        .reshape(shard, units)
    )
    grad_reduce_weight = feed_sums[:, blocks * shard :].reshape(2 * unit_part, width)
    grad_expand_bias = (
        sums[10 : 10 + 2 * bias_columns]
        .reshape(2, bias_columns, shard)
        .transpose(0, 2, 1)
        .reshape(2 * unit_part)
    )
    return (
        outputs.reshape(image_count, local_len, width).astype(BF),
        grad_images.reshape(image_count, local_len, width),
        sums[0],
        sums[1],
        grad_triple_weight,
        sums[2],
        sums[3],
        grad_output_weight,
        sums[4],
        sums[5],
        sums[6],
        sums[7],
        grad_expand_weight,
        grad_expand_bias,
        grad_reduce_weight,
        sums[8],
        sums[9],
    )


def layer_norm(inputs, gain, shift):
    average = jnp.mean(inputs, -1, keepdims=True)
    centered = inputs - average
    variance = jnp.mean(centered * centered, -1, keepdims=True)
    return centered * lax.rsqrt(variance + EPSILON) * gain + shift


def exact_gelu(values):
    return jax.nn.gelu(values, approximate=False)


def to_float(array):
    return array.astype(jnp.float32)


def plain_matmul(left, right):
    return jnp.dot(left, right, preferred_element_type=jnp.float32)


def plain_matmul_left_t(left, right):
    return lax.dot_general(
        left, right, (((0,), (0,)), ((), ())), preferred_element_type=jnp.float32
    )


def plain_matmul_right_t(left, right):
    return lax.dot_general(
        left, right, (((1,), (1,)), ((), ())), preferred_element_type=jnp.float32
    )


def plain_column_total(array):
    return plain_matmul(jnp.ones((1, array.shape[0]), jnp.bfloat16), array)[0]


def masked_scores(queries, key_rows, live_count, factor):
    scores = (
        jnp.einsum("qhd,khd->hqk", queries, key_rows, preferred_element_type=jnp.float32) * factor
    )
    live_keys = lax.broadcasted_iota(jnp.int32, (1, 1, key_rows.shape[0]), 2) < live_count
    return jnp.where(live_keys, scores, -1e30)


def plain_attend_forward(bundle):
    packed, live_count = bundle
    length, triple_count, local_width = packed.shape
    head_count = local_width // HEAD_DIM
    unpacked = packed.reshape(length, triple_count, head_count, HEAD_DIM)
    factor = HEAD_DIM ** (-0.5)
    scores = masked_scores(unpacked[:, 0], unpacked[:, 1], live_count, factor)
    highest = jnp.max(scores, -1, keepdims=True)
    powers = jnp.exp(scores - highest)
    row_total = jnp.sum(powers, -1, keepdims=True)
    weights_low = (powers / row_total).astype(jnp.bfloat16)
    mixed_rows = jnp.einsum(
        "hqk,khd->qhd", weights_low, unpacked[:, 2], preferred_element_type=jnp.float32
    )
    logsum = highest + jnp.log(row_total)
    return (mixed_rows.reshape(length, local_width).astype(jnp.bfloat16), logsum)


def plain_attend_backward(bundle):
    packed, grad_mixed, logsum, live_count = bundle
    length, triple_count, local_width = packed.shape
    head_count = local_width // HEAD_DIM
    unpacked = packed.reshape(length, triple_count, head_count, HEAD_DIM)
    factor = HEAD_DIM ** (-0.5)
    scores = masked_scores(unpacked[:, 0], unpacked[:, 1], live_count, factor)
    probs = jnp.exp(scores - logsum)
    grad_heads = grad_mixed.reshape(length, head_count, HEAD_DIM)
    grad_probs = jnp.einsum(
        "qhd,khd->hqk", grad_heads, unpacked[:, 2], preferred_element_type=jnp.float32
    )
    grad_values = jnp.einsum(
        "hqk,qhd->khd", probs.astype(jnp.bfloat16), grad_heads, preferred_element_type=jnp.float32
    )
    inner = jnp.sum(probs * grad_probs, -1, keepdims=True)
    grad_scores = (probs * (grad_probs - inner)).astype(jnp.bfloat16)
    grad_queries = (
        jnp.einsum("hqk,khd->qhd", grad_scores, unpacked[:, 1], preferred_element_type=jnp.float32)
        * factor
    )
    grad_keys = (
        jnp.einsum("hqk,qhd->khd", grad_scores, unpacked[:, 0], preferred_element_type=jnp.float32)
        * factor
    )
    stacked = jnp.stack([grad_queries, grad_keys, grad_values], 1)
    return stacked.reshape(length, triple_count, local_width).astype(jnp.bfloat16)


def plain_shards(
    images,
    cotangent,
    valid_count,
    first_gain,
    first_shift,
    triple_weight,
    query_bias,
    value_bias,
    output_weight,
    output_bias,
    attend_scale,
    second_gain,
    second_shift,
    expand_weight,
    expand_bias,
    reduce_weight,
    reduce_bias,
    feed_scale,
):
    image_count, local_len, width = images.shape
    gathered = (
        lax.all_gather(first_gain, "fsdp", axis=0, tiled=True),
        lax.all_gather(first_shift, "fsdp", axis=0, tiled=True),
        lax.all_gather(triple_weight, "fsdp", axis=0, tiled=True),
        lax.all_gather(query_bias, "fsdp", axis=0, tiled=True),
        lax.all_gather(value_bias, "fsdp", axis=0, tiled=True),
        lax.all_gather(output_weight, "fsdp", axis=0, tiled=True),
        lax.all_gather(output_bias, "fsdp", axis=0, tiled=True),
        lax.all_gather(attend_scale, "fsdp", axis=0, tiled=True),
        lax.all_gather(second_gain, "fsdp", axis=0, tiled=True),
        lax.all_gather(second_shift, "fsdp", axis=0, tiled=True),
        lax.all_gather(expand_weight, "fsdp", axis=0, tiled=True),
        lax.all_gather(expand_bias, "fsdp", axis=0, tiled=True),
        lax.all_gather(reduce_weight, "fsdp", axis=0, tiled=True),
        lax.all_gather(reduce_bias, "fsdp", axis=0, tiled=True),
        lax.all_gather(feed_scale, "fsdp", axis=0, tiled=True),
    )
    inputs = images.astype(jnp.float32).reshape(-1, width)
    first_normed = layer_norm(inputs, to_float(gathered[0]), to_float(gathered[1])).astype(
        jnp.bfloat16
    )
    joint_bias = to_float(jnp.concatenate([gathered[3], jnp.zeros_like(gathered[3]), gathered[4]]))
    triple = (plain_matmul(first_normed, gathered[2]) + joint_bias).astype(jnp.bfloat16)
    triple = triple.reshape(image_count, local_len, 3, width)
    by_heads = lax.all_to_all(triple, "seq", split_axis=3, concat_axis=1, tiled=True)
    attended, logsums = lax.map(plain_attend_forward, (by_heads, valid_count))
    by_tokens = lax.all_to_all(attended, "seq", split_axis=1, concat_axis=2, tiled=True)
    attended_rows = by_tokens.reshape(-1, width)
    branch_attend = plain_matmul(attended_rows, gathered[5]) + to_float(gathered[6])
    residual = inputs + to_float(gathered[7]) * branch_attend
    second_normed = layer_norm(residual, to_float(gathered[8]), to_float(gathered[9])).astype(
        jnp.bfloat16
    )
    expanded = plain_matmul(second_normed, gathered[10]) + to_float(gathered[11])
    activated = exact_gelu(expanded).astype(jnp.bfloat16)
    branch_feed = plain_matmul(activated, gathered[12]) + to_float(gathered[13])
    outputs = residual + to_float(gathered[14]) * branch_feed
    weights = (
        lax.all_gather(first_gain, "fsdp", axis=0, tiled=True),
        lax.all_gather(first_shift, "fsdp", axis=0, tiled=True),
        lax.all_gather(triple_weight, "fsdp", axis=0, tiled=True),
        lax.all_gather(query_bias, "fsdp", axis=0, tiled=True),
        lax.all_gather(value_bias, "fsdp", axis=0, tiled=True),
        lax.all_gather(output_weight, "fsdp", axis=0, tiled=True),
        lax.all_gather(output_bias, "fsdp", axis=0, tiled=True),
        lax.all_gather(attend_scale, "fsdp", axis=0, tiled=True),
        lax.all_gather(second_gain, "fsdp", axis=0, tiled=True),
        lax.all_gather(second_shift, "fsdp", axis=0, tiled=True),
        lax.all_gather(expand_weight, "fsdp", axis=0, tiled=True),
        lax.all_gather(expand_bias, "fsdp", axis=0, tiled=True),
        lax.all_gather(reduce_weight, "fsdp", axis=0, tiled=True),
        lax.all_gather(reduce_bias, "fsdp", axis=0, tiled=True),
        lax.all_gather(feed_scale, "fsdp", axis=0, tiled=True),
    )
    upstream = cotangent.astype(jnp.float32).reshape(-1, width)
    grad_feed_scale = jnp.sum(upstream * branch_feed, 0)
    grad_feed = (to_float(weights[14]) * upstream).astype(jnp.bfloat16)
    grad_reduce_bias = plain_column_total(grad_feed)
    grad_reduce_weight = plain_matmul_left_t(activated, grad_feed)
    grad_activated = plain_matmul_right_t(grad_feed, weights[12])
    unused, gelu_pull = jax.vjp(exact_gelu, expanded)
    grad_expanded = gelu_pull(grad_activated)[0].astype(jnp.bfloat16)
    grad_expand_bias = plain_column_total(grad_expanded)
    grad_expand_weight = plain_matmul_left_t(second_normed, grad_expanded)
    grad_second_normed = plain_matmul_right_t(grad_expanded, weights[10])
    unused, second_pull = jax.vjp(layer_norm, residual, to_float(weights[8]), to_float(weights[9]))
    grad_residual_norm, grad_second_gain, grad_second_shift = second_pull(grad_second_normed)
    grad_residual = upstream + grad_residual_norm
    grad_attend_scale = jnp.sum(grad_residual * branch_attend, 0)
    grad_attend = (to_float(weights[7]) * grad_residual).astype(jnp.bfloat16)
    grad_output_bias = plain_column_total(grad_attend)
    grad_output_weight = plain_matmul_left_t(attended_rows, grad_attend)
    grad_attended = plain_matmul_right_t(grad_attend, weights[5]).astype(jnp.bfloat16)
    grad_attended = grad_attended.reshape(image_count, local_len, width)
    grad_by_heads = lax.all_to_all(grad_attended, "seq", split_axis=2, concat_axis=1, tiled=True)
    grad_triple_heads = lax.map(plain_attend_backward, (by_heads, grad_by_heads, logsums, valid_count))
    grad_triple = lax.all_to_all(grad_triple_heads, "seq", split_axis=1, concat_axis=3, tiled=True)
    grad_triple = grad_triple.reshape(-1, 3 * width)
    column_sums = plain_column_total(grad_triple)
    grad_query_bias = column_sums[:width]
    grad_value_bias = column_sums[2 * width :]
    grad_triple_weight = plain_matmul_left_t(first_normed, grad_triple)
    grad_first_normed = plain_matmul_right_t(grad_triple, weights[2])
    unused, first_pull = jax.vjp(layer_norm, inputs, to_float(weights[0]), to_float(weights[1]))
    grad_inputs_norm, grad_first_gain, grad_first_shift = first_pull(grad_first_normed)
    grad_images = grad_residual + grad_inputs_norm
    owned = (
        lax.psum_scatter(
            grad_first_gain.astype(jnp.bfloat16), "fsdp", scatter_dimension=0, tiled=True
        ).astype(jnp.float32),
        lax.psum_scatter(
            grad_first_shift.astype(jnp.bfloat16), "fsdp", scatter_dimension=0, tiled=True
        ).astype(jnp.float32),
        lax.psum_scatter(
            grad_triple_weight.astype(jnp.bfloat16), "fsdp", scatter_dimension=0, tiled=True
        ).astype(jnp.float32),
        lax.psum_scatter(
            grad_query_bias.astype(jnp.bfloat16), "fsdp", scatter_dimension=0, tiled=True
        ).astype(jnp.float32),
        lax.psum_scatter(
            grad_value_bias.astype(jnp.bfloat16), "fsdp", scatter_dimension=0, tiled=True
        ).astype(jnp.float32),
        lax.psum_scatter(
            grad_output_weight.astype(jnp.bfloat16), "fsdp", scatter_dimension=0, tiled=True
        ).astype(jnp.float32),
        lax.psum_scatter(
            grad_output_bias.astype(jnp.bfloat16), "fsdp", scatter_dimension=0, tiled=True
        ).astype(jnp.float32),
        lax.psum_scatter(
            grad_attend_scale.astype(jnp.bfloat16), "fsdp", scatter_dimension=0, tiled=True
        ).astype(jnp.float32),
        lax.psum_scatter(
            grad_second_gain.astype(jnp.bfloat16), "fsdp", scatter_dimension=0, tiled=True
        ).astype(jnp.float32),
        lax.psum_scatter(
            grad_second_shift.astype(jnp.bfloat16), "fsdp", scatter_dimension=0, tiled=True
        ).astype(jnp.float32),
        lax.psum_scatter(
            grad_expand_weight.astype(jnp.bfloat16), "fsdp", scatter_dimension=0, tiled=True
        ).astype(jnp.float32),
        lax.psum_scatter(
            grad_expand_bias.astype(jnp.bfloat16), "fsdp", scatter_dimension=0, tiled=True
        ).astype(jnp.float32),
        lax.psum_scatter(
            grad_reduce_weight.astype(jnp.bfloat16), "fsdp", scatter_dimension=0, tiled=True
        ).astype(jnp.float32),
        lax.psum_scatter(
            grad_reduce_bias.astype(jnp.bfloat16), "fsdp", scatter_dimension=0, tiled=True
        ).astype(jnp.float32),
        lax.psum_scatter(
            grad_feed_scale.astype(jnp.bfloat16), "fsdp", scatter_dimension=0, tiled=True
        ).astype(jnp.float32),
    )
    summed = lax.psum(
        (
            owned[0],
            owned[1],
            owned[2],
            owned[3],
            owned[4],
            owned[5],
            owned[6],
            owned[7],
            owned[8],
            owned[9],
            owned[10],
            owned[11],
            owned[12],
            owned[13],
            owned[14],
        ),
        "seq",
    )
    return (
        outputs.reshape(image_count, local_len, width).astype(jnp.bfloat16),
        grad_images.reshape(image_count, local_len, width),
        summed[0],
        summed[1],
        summed[2],
        summed[3],
        summed[4],
        summed[5],
        summed[6],
        summed[7],
        summed[8],
        summed[9],
        summed[10],
        summed[11],
        summed[12],
        summed[13],
        summed[14],
    )


def solution(mesh):
    fsdp, seq = mesh.devices.shape
    if seq == 4 and fsdp == 8:
        plan, tokens = shards, P("fsdp", ("far", "core"), None)
        mesh = Mesh(mesh.devices.reshape(fsdp, 2, 2), ("fsdp", "far", "core"))
    else:
        plan, tokens = plain_shards, P("fsdp", "seq", None)
    row, matrix = P("fsdp"), P("fsdp", None)
    return jax.shard_map(
        plan,
        mesh=mesh,
        in_specs=(
            tokens, tokens, row, row, row, matrix, row, row, matrix,
            row, row, row, row, matrix, row, matrix, row, row,
        ),
        out_specs=(
            tokens, tokens, row, row, matrix, row, row, matrix,
            row, row, row, row, matrix, row, matrix, row, row,
        ),
        check_vma=False,
    )
```

```python
import functools

import jax
import jax.numpy as jnp
from jax import lax
from jax.experimental import pallas as pl
from jax.experimental.pallas import tpu as pltpu
from jax.sharding import Mesh, PartitionSpec as P

HEAD_DIM = 64
EPSILON = 1e-06
BF = jnp.bfloat16
F32 = jnp.float32
MASKED = -1e30


def dot(left, right):
    return lax.dot_general(left, right, (((1,), (0,)), ((), ())), preferred_element_type=F32)


def dot_left_t(left, right):
    return lax.dot_general(left, right, (((0,), (0,)), ((), ())), preferred_element_type=F32)


def dot_right_t(left, right):
    return lax.dot_general(left, right, (((1,), (1,)), ((), ())), preferred_element_type=F32)


def column_total(array):
    return dot(jnp.ones((8, array.shape[0]), BF), array)[0]


def normalize(rows):
    average = jnp.mean(rows, -1, keepdims=True)
    centered = rows - average
    variance = jnp.mean(centered * centered, -1, keepdims=True)
    factor = lax.rsqrt(variance + EPSILON)
    return centered * factor, factor


def normalize_back(normal, factor, weighted):
    return factor * (
        weighted
        - jnp.mean(weighted, -1, keepdims=True)
        - normal * jnp.mean(weighted * normal, -1, keepdims=True)
    )


def spans(total, step):
    return [(start, min(step, total - start)) for start in range(0, total, step)]


def merge(ref, out):
    pieces, _, rows, _ = ref.shape
    for piece in range(pieces):
        out[pl.ds(piece * rows, rows), :] = ref[piece, 0].astype(F32)


def lane_parts(block, heads, head):
    lane = lax.broadcasted_iota(jnp.int32, (1, block), 1)
    if heads == 1:
        return lane < HEAD_DIM, lane - HEAD_DIM
    if head == 0:
        return lane < HEAD_DIM, lane - HEAD_DIM
    return lane >= HEAD_DIM, lane


def split_three(values):
    high = values.astype(BF).astype(F32)
    rest = values - high
    middle = rest.astype(BF).astype(F32)
    return high, middle, rest - middle


def dead_column(limit_ref, length):
    image = pl.program_id(0)
    row = lax.broadcasted_iota(jnp.int32, (length, 1), 0)
    dead = (row >= limit_ref[image, 0]) & (row < limit_ref[image, 1])
    return jnp.where(dead, MASKED, 0.0)


def attend_forward_kernel(limit_ref, q_ref, k_ref, v_ref, out_ref, log_ref, q_s, k_s, v_s, o_s):
    pieces, _, rows, block = q_ref.shape
    length = pieces * rows
    heads = max(block // HEAD_DIM, 1)
    merge(q_ref, q_s)
    merge(k_ref, k_s)
    merge(v_ref, v_s)
    dead = dead_column(limit_ref, length)
    aug = []
    for head in range(heads):
        own, spare = lane_parts(2 * HEAD_DIM, heads, head)
        q = jnp.where(own, q_s[...] * 0.125, jnp.where(spare == 0, 1.0, 0.0)).astype(BF)
        k = jnp.where(own, k_s[...], jnp.where(spare == 0, dead, 0.0)).astype(BF)
        v = jnp.where(own, v_s[...], jnp.where(spare == 0, 1.0, 0.0)).astype(BF)
        aug.append((q, k, v))
    for start, size in spans(length, 352):
        results = []
        for head in range(heads):
            q, k, v = aug[head]
            scores = dot_right_t(q[start : start + size], k)
            top = jnp.max(scores, -1, keepdims=True)
            powers = jnp.exp(scores - top).astype(BF)
            mixed = dot(powers, v)
            own, spare = lane_parts(2 * HEAD_DIM, heads, head)
            at = HEAD_DIM if head == 0 else 0
            total = mixed[:, at : at + 1]
            results.append((mixed / total, top + jnp.log(total)))
        own, _ = lane_parts(2 * HEAD_DIM, heads, 0)
        if heads == 1:
            o_s[pl.ds(start, size), :] = results[0][0]
            log_ref[0, 0, pl.ds(start, size), :] = jnp.broadcast_to(
                results[0][1], (size, 2 * HEAD_DIM)
            )
        else:
            o_s[pl.ds(start, size), :] = jnp.where(own, results[0][0], results[1][0])
            log_ref[0, 0, pl.ds(start, size), :] = jnp.where(own, results[1][1], results[0][1])
    for piece in range(pieces):
        out_ref[piece, 0] = o_s[pl.ds(piece * rows, rows), :].astype(BF)


def attend_backward_kernel(
    limit_ref, q_ref, k_ref, v_ref, o_ref, g_ref, log_ref, grad_ref,
    q_s, k_s, v_s, o_s, g_s, dq_s, dk_s, dv_s,
):
    pieces, _, rows, block = q_ref.shape
    length = pieces * rows
    heads = max(block // HEAD_DIM, 1)
    merge(q_ref, q_s)
    merge(k_ref, k_s)
    merge(v_ref, v_s)
    merge(o_ref, o_s)
    merge(g_ref, g_s)
    dead = dead_column(limit_ref, length)
    product = o_s[...] * g_s[...]
    for head in range(heads):
        own, spare = lane_parts(2 * HEAD_DIM, heads, head)
        log_parts = split_three(log_ref[0, 0])
        inner = jnp.sum(jnp.where(own, product, 0.0), -1, keepdims=True)
        inner_parts = split_three(inner)
        zero = jnp.zeros((length, 2 * HEAD_DIM), F32)
        q_tail, k_tail, v_tail, g_tail = zero, zero, zero, zero
        for place in range(3):
            q_tail = jnp.where(spare == place, -log_parts[place], q_tail)
            g_tail = jnp.where(spare == place, -inner_parts[place], g_tail)
            k_tail = jnp.where(spare == place, 1.0, k_tail)
            v_tail = jnp.where(spare == place, 1.0, v_tail)
        q_tail = jnp.where(spare == 3, 1.0, q_tail)
        k_tail = jnp.where(spare == 3, dead, k_tail)
        q = jnp.where(own, q_s[...] * 0.125, q_tail).astype(BF)
        k = jnp.where(own, k_s[...], k_tail).astype(BF)
        v = jnp.where(own, v_s[...], v_tail).astype(BF)
        g = jnp.where(own, g_s[...], g_tail).astype(BF)
        k_t = jnp.where(own, k_s[...] * 0.125, 0.0).T.astype(BF)
        dk = dv = None
        for start, size in spans(length, 512):
            q_part, g_part = q[start : start + size], g[start : start + size]
            probs = jnp.exp(dot_right_t(k, q_part))
            slopes = (probs * dot_right_t(v, g_part)).astype(BF)
            probs = probs.astype(BF)
            dv_part = dot(probs, g_part)
            dk_part = dot(slopes, q_part)
            dv = dv_part if dv is None else dv + dv_part
            dk = dk_part if dk is None else dk + dk_part
            dq_part = dot(k_t, slopes).T
            if head == 0:
                dq_s[pl.ds(start, size), :] = dq_part
            else:
                dq_s[pl.ds(start, size), :] += dq_part
        if head == 0:
            dk_s[...] = dk
            dv_s[...] = dv
        else:
            dk_s[...] = jnp.where(own, dk, dk_s[...])
            dv_s[...] = jnp.where(own, dv, dv_s[...])
    stride = grad_ref.shape[3] // 3
    for piece in range(pieces):
        part = pl.ds(piece * rows, rows)
        for which, grad in enumerate((dq_s, dk_s, dv_s)):
            at = pl.multiple_of(which * stride + pl.program_id(1) * block, block)
            grad_ref[piece, 0, :, pl.ds(at, block)] = grad[part, :].astype(BF)


def attend_specs(pieces, rows, first):
    def at(limit_index):
        return pl.BlockSpec(
            (pieces, 1, rows, 2 * HEAD_DIM),
            lambda image, pair, limits: (0, image, 0, limit_index + pair),
        )

    return at(first)


def attend_forward(triple, limits):
    pieces, images, rows, columns = triple.shape
    head_width = columns // 3
    length = pieces * rows
    pairs = head_width // (2 * HEAD_DIM)
    wide = pltpu.VMEM((length, 2 * HEAD_DIM), F32)
    spec = functools.partial(attend_specs, pieces, rows)
    heads = images * head_width // HEAD_DIM
    return pl.pallas_call(
        attend_forward_kernel,
        grid_spec=pltpu.PrefetchScalarGridSpec(
            num_scalar_prefetch=1,
            grid=(images, pairs),
            in_specs=[spec(0), spec(pairs), spec(2 * pairs)],
            out_specs=[
                spec(0),
                pl.BlockSpec((1, 1, length, 2 * HEAD_DIM), lambda i, p, limits: (i, p, 0, 0)),
            ],
            scratch_shapes=[wide] * 4,
        ),
        out_shape=[
            jax.ShapeDtypeStruct((pieces, images, rows, head_width), BF),
            jax.ShapeDtypeStruct((images, pairs, length, 2 * HEAD_DIM), F32),
        ],
        compiler_params=pltpu.CompilerParams(vmem_limit_bytes=50 * 2**20),
        cost_estimate=pl.CostEstimate(
            flops=heads * length * length * 1024,
            bytes_accessed=4 * triple.size,
            transcendentals=heads * length * length,
        ),
        name="attend_forward",
    )(limits, triple, triple, triple)


def attend_backward(triple, attended, grad, logs, limits):
    pieces, images, rows, columns = triple.shape
    head_width = columns // 3
    length = pieces * rows
    pairs = head_width // (2 * HEAD_DIM)
    wide = pltpu.VMEM((length, 2 * HEAD_DIM), F32)
    spec = functools.partial(attend_specs, pieces, rows)
    heads = images * head_width // HEAD_DIM
    return pl.pallas_call(
        attend_backward_kernel,
        grid_spec=pltpu.PrefetchScalarGridSpec(
            num_scalar_prefetch=1,
            grid=(images, pairs),
            in_specs=[
                spec(0),
                spec(pairs),
                spec(2 * pairs),
                spec(0),
                spec(0),
                pl.BlockSpec((1, 1, length, 2 * HEAD_DIM), lambda i, p, limits: (i, p, 0, 0)),
            ],
            out_specs=pl.BlockSpec(
                (pieces, 1, rows, columns), lambda image, pair, limits: (0, image, 0, 0)
            ),
            scratch_shapes=[wide] * 8,
        ),
        out_shape=jax.ShapeDtypeStruct(triple.shape, BF),
        compiler_params=pltpu.CompilerParams(vmem_limit_bytes=56 * 2**20),
        cost_estimate=pl.CostEstimate(
            flops=heads * length * length * 2560,
            bytes_accessed=8 * triple.size,
            transcendentals=heads * length * length,
        ),
        name="attend_backward",
    )(limits, triple, triple, triple, attended, grad, logs)


def project_kernel(rows_ref, small_ref, weight_ref, bias_ref, normed_ref, triple_ref):
    normal, _ = normalize(rows_ref[0].astype(F32))
    normed = (normal * small_ref[0:1, :] + small_ref[1:2, :]).astype(BF)
    normed_ref[0] = normed
    triple_ref[0] = (dot(normed, weight_ref[...]) + bias_ref[...]).astype(BF)


def project(tokens, small, weight, bias):
    pieces, rows, width = tokens.shape
    columns = weight.shape[1]

    def whole(array):
        return pl.BlockSpec(array.shape, lambda i: (0, 0))

    def piece(columns):
        return pl.BlockSpec((1, rows, columns), lambda i: (i, 0, 0))

    return pl.pallas_call(
        project_kernel,
        grid=(pieces,),
        in_specs=[piece(width), whole(small), whole(weight), whole(bias)],
        out_specs=[piece(width), piece(columns)],
        out_shape=[
            jax.ShapeDtypeStruct((pieces, rows, width), BF),
            jax.ShapeDtypeStruct((pieces, rows, columns), BF),
        ],
        compiler_params=pltpu.CompilerParams(vmem_limit_bytes=40 * 2**20),
        cost_estimate=pl.CostEstimate(
            flops=2 * pieces * rows * width * columns,
            bytes_accessed=2 * pieces * rows * (2 * width + columns),
            transcendentals=0,
        ),
        name="project",
    )(tokens, small, weight, bias)


def project_back_kernel(grad_ref, rows_ref, weight_ref, part_ref, gain_ref, shift_ref, total_ref):
    @pl.when(pl.program_id(0) == 0)
    def _():
        gain_ref[...] = jnp.zeros_like(gain_ref)
        shift_ref[...] = jnp.zeros_like(shift_ref)
        total_ref[...] = jnp.zeros_like(total_ref)

    normal, _ = normalize(rows_ref[0].astype(F32))
    part = dot_right_t(grad_ref[0], weight_ref[...])
    part_ref[0] = part.astype(BF)
    gain_ref[...] += jnp.sum(part * normal, 0, keepdims=True)
    shift_ref[...] += jnp.sum(part, 0, keepdims=True)
    total_ref[...] += jnp.sum(grad_ref[0].astype(F32), 0, keepdims=True)


def project_back(grad, tokens, weight):
    pieces, rows, width = tokens.shape
    columns = weight.shape[1]

    def piece(columns):
        return pl.BlockSpec((1, rows, columns), lambda i: (i, 0, 0))

    def whole(shape):
        return pl.BlockSpec(shape, lambda i: (0, 0))

    return pl.pallas_call(
        project_back_kernel,
        grid=(pieces,),
        in_specs=[piece(columns), piece(width), whole(weight.shape)],
        out_specs=[piece(width), whole((1, width)), whole((1, width)), whole((1, columns))],
        out_shape=[
            jax.ShapeDtypeStruct((pieces, rows, width), BF),
            jax.ShapeDtypeStruct((1, width), F32),
            jax.ShapeDtypeStruct((1, width), F32),
            jax.ShapeDtypeStruct((1, columns), F32),
        ],
        compiler_params=pltpu.CompilerParams(vmem_limit_bytes=40 * 2**20),
        cost_estimate=pl.CostEstimate(
            flops=2 * pieces * rows * width * columns,
            bytes_accessed=2 * pieces * rows * (2 * width + columns),
            transcendentals=0,
        ),
        name="project_back",
    )(grad, tokens, weight)


def gelu_parts(values):
    size = jnp.abs(values) * 0.7071067811865476
    bell = jnp.exp(-size * size)
    t = 1.0 / (1.0 + 0.3275911 * size)
    tail = t * (
        0.254829592
        + t * (-0.284496736 + t * (1.421413741 + t * (-1.453152027 + t * 1.061405429)))
    )
    tail = 0.5 * tail * bell
    return jnp.where(values >= 0.0, 1.0 - tail, tail), 0.3989422804014327 * bell


def expand_kernel(rows_ref, weight_ref, bias_ref, active_ref, slope_ref):
    count, width = rows_ref.shape
    weight = weight_ref[...].reshape(width, weight_ref.shape[2])
    for start, size in spans(count, 352):
        expanded = dot(rows_ref[start : start + size, :], weight) + bias_ref[...]
        below, density = gelu_parts(expanded)
        active_ref[start : start + size, :] = (expanded * below).astype(BF)
        slope_ref[start : start + size, :] = (below + expanded * density).astype(BF)


def expand_rows(rows, feed_weights, bias):
    count, width = rows.shape
    devices = feed_weights.shape[0]
    shard = width // devices
    units = bias.shape[1]
    tile = 256
    across = width // tile
    shape = jax.ShapeDtypeStruct((count, units), BF)
    return pl.pallas_call(
        expand_kernel,
        grid=(units // tile,),
        in_specs=[
            pl.BlockSpec((count, width), lambda i: (0, 0)),
            pl.BlockSpec((devices, shard, tile), lambda i: (0, i // across, i % across)),
            pl.BlockSpec((1, tile), lambda i: (0, i)),
        ],
        out_specs=[pl.BlockSpec((count, tile), lambda i: (0, i))] * 2,
        out_shape=[shape] * 2,
        compiler_params=pltpu.CompilerParams(vmem_limit_bytes=48 * 2**20),
        cost_estimate=pl.CostEstimate(
            flops=4 * count * units * width,
            bytes_accessed=2 * (count * width + width * units + 2 * count * units),
            transcendentals=2 * count * units,
        ),
        name="expand_rows",
    )(rows, feed_weights, bias)


def feed_grads_kernel(rows_ref, active_ref, expanded_ref, feed_ref, out_ref):
    shard, width = rows_ref.shape[1], out_ref.shape[2]
    blocks = expanded_ref.shape[1] // width
    for block in range(blocks):
        out_ref[0, block * shard : (block + 1) * shard, :] = dot_left_t(
            rows_ref[...], expanded_ref[:, block * width : (block + 1) * width]
        ).astype(BF)
    out_ref[0, blocks * shard :, :] = dot_left_t(active_ref[...], feed_ref[...]).astype(BF)


def feed_grads(rows, active, grad_expanded, grad_feed, devices):
    count, width = rows.shape
    units = active.shape[1]
    shard, unit_part = width // devices, units // devices
    blocks = units // width
    if shard % 128 != 0 or unit_part % 128 != 0:
        expand = dot_left_t(rows, grad_expanded).astype(BF).reshape(devices, shard, blocks, width)
        expand = expand.transpose(0, 2, 1, 3).reshape(devices, blocks * shard, width)
        reduce = dot_left_t(active, grad_feed).astype(BF).reshape(devices, unit_part, width)
        return jnp.concatenate([expand, reduce], 1)
    height = blocks * shard + unit_part
    return pl.pallas_call(
        feed_grads_kernel,
        grid=(devices,),
        in_specs=[
            pl.BlockSpec((count, shard), lambda i: (0, i)),
            pl.BlockSpec((count, unit_part), lambda i: (0, i)),
            pl.BlockSpec((count, units), lambda i: (0, 0)),
            pl.BlockSpec((count, width), lambda i: (0, 0)),
        ],
        out_specs=pl.BlockSpec((1, height, width), lambda i: (i, 0, 0)),
        out_shape=jax.ShapeDtypeStruct((devices, height, width), BF),
        compiler_params=pltpu.CompilerParams(vmem_limit_bytes=52 * 2**20),
        cost_estimate=pl.CostEstimate(
            flops=4 * count * units * width,
            bytes_accessed=2 * (2 * count * (width + units) + 2 * width * units),
            transcendentals=0,
        ),
        name="feed_grads",
    )(rows, active, grad_expanded, grad_feed)


def far_send(array, shift):
    count = lax.axis_size("far")
    return lax.ppermute(array, "far", [(i, (i + shift) % count) for i in range(count)])


def far_gather(array):
    count = lax.axis_size("far")
    return [array] + [far_send(array, count - r) for r in range(1, count)]


def far_exchange(slots):
    count = len(slots)
    out = [slots[0]] + [None] * (count - 1)
    for r in range(1, count):
        out[count - r] = far_send(slots[r], r)
    return out


def far_sum(slots):
    arrived = far_exchange(slots)
    return sum(part.astype(F32) for part in arrived)


def other_core(array):
    return lax.ppermute(array, "core", [(0, 1), (1, 0)])


def fsdp_gather(array):
    return lax.all_gather(array, "fsdp", axis=0, tiled=True)


def fsdp_scatter(array):
    return lax.psum_scatter(array, "fsdp", scatter_dimension=0, tiled=True)


def ring_send(array, step):
    count = lax.axis_size("fsdp")
    order = list(range(0, count, 2)) + list(range(1, count, 2))[::-1]
    pairs = [(order[i], order[(i + step) % count]) for i in range(count)]
    return lax.ppermute(array, "fsdp", pairs)


def ring_index(offset):
    count, index = lax.axis_size("fsdp"), lax.axis_index("fsdp")
    place = jnp.where(index % 2 == 0, index // 2, count - 1 - index // 2)
    place = (place + offset + count) % count
    return jnp.where(place < count // 2, 2 * place, 2 * (count - 1 - place) + 1)


def ring_scatter(array):
    count = lax.axis_size("fsdp")

    def block(offset):
        return lax.dynamic_index_in_dim(array, ring_index(offset), 0, False).astype(F32)

    total = block(0)
    for direction, hops in ((1, count // 2), (-1, (count - 1) // 2)):
        moving = block(direction * hops)
        for step in range(1, hops + 1):
            moving = ring_send(moving.astype(BF), direction).astype(F32)
            if step < hops:
                moving = moving + block(direction * (hops - step))
        total = total + moving
    return total


def after(array, *earlier):
    return lax.optimization_barrier((array,) + earlier)[0]


def core_join(mine, axis, core):
    other = other_core(mine)
    return jnp.stack(
        [jnp.where(core == 0, mine, other), jnp.where(core == 0, other, mine)], axis
    )


def shards(
    images,
    cotangent,
    valid_count,
    first_gain,
    first_shift,
    triple_weight,
    query_bias,
    value_bias,
    output_weight,
    output_bias,
    attend_scale,
    second_gain,
    second_shift,
    expand_weight,
    expand_bias,
    reduce_weight,
    reduce_bias,
    feed_scale,
):
    image_count, local_len, width = images.shape
    own_rows = image_count * local_len
    far_count, fsdp_count = lax.axis_size("far"), lax.axis_size("fsdp")
    far, core = lax.axis_index("far"), lax.axis_index("core")
    seq_count = 2 * far_count
    shard = width // fsdp_count
    units = expand_weight.shape[1]
    unit_part = units // (2 * fsdp_count)
    near_heads = width // HEAD_DIM // seq_count
    head_width = near_heads * HEAD_DIM

    def my_heads(array, axis):
        shape = array.shape
        array = array.reshape(
            shape[:axis] + (far_count, near_heads, 2, HEAD_DIM) + shape[axis + 1 :]
        )
        array = lax.dynamic_index_in_dim(array, far, axis, False)
        array = lax.dynamic_index_in_dim(array, core, axis + 1, False)
        return array.reshape(shape[:axis] + (head_width,) + shape[axis + 1 :])

    triple_mine = my_heads(triple_weight.reshape(shard, 3, width), 2).reshape(shard, 3 * head_width)
    bias_mine = lax.dynamic_index_in_dim(expand_bias.reshape(2, unit_part), core, 0, False)
    bias_columns = unit_part // shard
    vectors = [
        first_gain, first_shift, query_bias, value_bias, output_bias, attend_scale,
        second_gain, second_shift, reduce_bias, feed_scale,
    ]
    vector_count = len(vectors)
    small_mine = jnp.concatenate(
        [jnp.stack(vectors, 1), bias_mine.reshape(shard, bias_columns)], 1
    )
    small_mine = jnp.pad(small_mine, ((0, 0), (0, -small_mine.shape[1] % 128)))
    pairs = shard // (2 * HEAD_DIM)
    output_mine = lax.dynamic_index_in_dim(
        output_weight.reshape(pairs, 2, HEAD_DIM, width), core, 1, False
    )
    output_mine = output_mine.reshape(shard // 2, 2, width // 2).transpose(1, 0, 2)
    output_mine = output_mine.reshape(shard, width // 2)
    first = 3 * head_width
    second = first + small_mine.shape[1]
    packed = fsdp_gather(jnp.concatenate([triple_mine, small_mine, output_mine], 1))
    triple_whole = packed[:, :first]
    small = packed[:, first : first + 16].astype(F32).T
    output_whole = packed[:, second:].reshape(fsdp_count, 2, shard // 2, width // 2)
    output_whole = output_whole.transpose(0, 2, 1, 3).reshape(far_count, head_width, width)
    output_whole = jnp.roll(output_whole, -far, 0).reshape(width // 2, width)
    (gain_1, shift_1, bias_q, bias_v, bias_o, scale_a, gain_2, shift_2, bias_r, scale_f) = [
        small[i] for i in range(vector_count)
    ]
    bias_e = (
        small[vector_count : vector_count + bias_columns]
        .reshape(bias_columns, fsdp_count, shard)
        .transpose(1, 2, 0)
        .reshape(1, fsdp_count * unit_part)
    )

    blocks = units // 2 // width
    expand_mine = lax.dynamic_index_in_dim(
        expand_weight.reshape(shard, fsdp_count, 2, unit_part), core, 2, False
    ).reshape(shard, blocks, width)
    reduce_mine = lax.dynamic_index_in_dim(
        reduce_weight.reshape(2, unit_part, width), core, 0, False
    )
    feed_mine = jnp.concatenate([expand_mine[:, i] for i in range(blocks)] + [reduce_mine], 0)
    height = blocks * shard + unit_part
    feed_weights = fsdp_gather(feed_mine).reshape(fsdp_count, height, width)
    expand_blocks = [
        feed_weights[:, i * shard : (i + 1) * shard].reshape(width, width) for i in range(blocks)
    ]
    reduce_whole = feed_weights[:, blocks * shard :].reshape(units // 2, width)

    groups = 2 if image_count % 2 == 0 else 1
    group_images = image_count // groups
    rows = group_images * local_len
    joint_bias = jnp.concatenate(
        [my_heads(bias_q, 0), jnp.zeros((head_width,), F32), my_heads(bias_v, 0)]
    )
    tokens, normed, triples = [], [], []
    for group in range(groups):
        mine = images[group * group_images : (group + 1) * group_images].reshape(rows, width)
        slots = []
        for slot in far_gather(mine):
            slots += [slot, other_core(slot)]
        tokens.append(jnp.stack(slots, 0))
        first_normed, triple = project(
            tokens[-1], small, triple_whole, joint_bias[None]
        )
        normed.append(first_normed)
        triples.append(triple)

    last_slot = ((far_count - 1 - far) % far_count) * 2 + (1 - core)
    dead_from = last_slot * local_len + valid_count - (seq_count - 1) * local_len
    limits = jnp.stack(
        [dead_from, jnp.broadcast_to((last_slot + 1) * local_len, dead_from.shape)], 1
    ).astype(jnp.int32)

    direct = local_len % 8 == 0 and head_width % (2 * HEAD_DIM) == 0

    def to_kernel(array):
        array = array.reshape(seq_count, group_images, local_len, -1)
        if direct:
            return array
        parts = array.shape[-1] // head_width
        array = array.transpose(1, 0, 2, 3).reshape(
            1, group_images, seq_count * local_len, parts, head_width
        )
        lanes = -head_width % (2 * HEAD_DIM)
        array = jnp.pad(array, ((0, 0),) * 4 + ((0, lanes),))
        return array.reshape(1, group_images, seq_count * local_len, -1)

    def from_kernel(array, parts):
        if direct:
            return array.reshape(seq_count, rows, -1)
        array = array.reshape(group_images, seq_count, local_len, parts, -1)
        array = array[..., :head_width].transpose(1, 0, 2, 3, 4)
        return array.reshape(seq_count, rows, parts * head_width)

    kernel_in, kernel_out, kernel_logs, attended_rows, branch_parts = [], [], [], [], []
    for group in range(groups):
        picked = limits[group * group_images : (group + 1) * group_images]
        kernel_in.append(to_kernel(triples[group]))
        attended, logs = attend_forward(kernel_in[-1], picked)
        kernel_out.append(attended)
        kernel_logs.append(logs)
        attended = from_kernel(attended, 1).reshape(far_count, 2 * rows, head_width)
        attended = far_exchange([attended[r] for r in range(far_count)])
        attended_rows.append(jnp.concatenate(attended, 1))
        branch = dot(attended_rows[-1], output_whole)
        branch_parts.append(
            branch[:rows] + other_core(branch[rows:].astype(BF)).astype(F32) + bias_o
        )
    branch_attend = jnp.concatenate(branch_parts, 0)
    inputs = images.reshape(own_rows, width).astype(F32)
    residual = inputs + scale_a * branch_attend
    normal_2, factor_2 = normalize(residual)
    second_mine = (normal_2 * gain_2 + shift_2).astype(BF)
    second_normed = jnp.concatenate([second_mine, other_core(second_mine)], 0)
    activated, slope = expand_rows(second_normed, feed_weights, bias_e)
    branch = dot(activated, reduce_whole)
    branch_feed = (
        branch[:own_rows] + other_core(branch[own_rows:].astype(BF)).astype(F32) + bias_r
    )
    outputs = residual + scale_f * branch_feed

    cotangent = cotangent.reshape(own_rows, width)
    upstream = cotangent.astype(F32)
    both = jnp.concatenate([cotangent, other_core(cotangent)], 0)
    grad_feed = (scale_f * both.astype(F32)).astype(BF)
    grad_feed_scale = jnp.sum(upstream * branch_feed, 0)
    grad_reduce_bias = column_total(grad_feed[:own_rows])
    grad_expanded = (dot_right_t(grad_feed, reduce_whole) * slope.astype(F32)).astype(BF)
    feed_sums = feed_grads(second_normed, activated, grad_expanded, grad_feed, fsdp_count)
    grad_expanded, feed_sums = lax.optimization_barrier((grad_expanded, feed_sums))
    feed_sums = fsdp_scatter(feed_sums.reshape(fsdp_count * height, width))
    partial = sum(
        dot_right_t(grad_expanded[:, i * width : (i + 1) * width], expand_blocks[i])
        for i in range(blocks)
    )
    grad_expand_bias = column_total(grad_expanded)
    upper = partial[:own_rows] + other_core(partial[own_rows:].astype(BF)).astype(F32)
    grad_second_gain = jnp.sum(upper * normal_2, 0)
    grad_second_shift = jnp.sum(upper, 0)
    grad_residual = upstream + normalize_back(normal_2, factor_2, upper * gain_2)
    grad_attend_scale = jnp.sum(grad_residual * branch_attend, 0)
    grad_attend = (scale_a * grad_residual).astype(BF)
    grad_output_bias = column_total(grad_attend)
    grad_other = other_core(grad_attend)
    grad_sides = []
    for group in range(groups):
        part = slice(group * rows, (group + 1) * rows)
        grad_sides.append(jnp.concatenate([grad_attend[part], grad_other[part]], 0))
    grad_attended = [
        [
            dot_right_t(side, output_whole[r * head_width : (r + 1) * head_width]).astype(BF)
            for r in range(far_count)
        ]
        for side in grad_sides
    ]
    grad_output_weight = sum(
        dot_left_t(attended_rows[group], grad_sides[group]) for group in range(groups)
    ).astype(BF)
    grad_output_weight = jnp.roll(
        grad_output_weight.reshape(far_count, head_width, width), far, 0
    ).reshape(width // 2, width)

    grad_heads = [to_kernel(jnp.stack(far_exchange(parts), 0)) for parts in grad_attended]
    upper_parts, grad_triples = [], []
    grad_first_gain = grad_first_shift = column_sums = 0.0
    for group in range(groups):
        picked = limits[group * group_images : (group + 1) * group_images]
        grad_heads_in = grad_heads[group]
        if group > 0:
            grad_heads_in = after(grad_heads_in, partial)
        grad_triple = from_kernel(
            attend_backward(
                kernel_in[group], kernel_out[group], grad_heads_in, kernel_logs[group], picked
            ),
            3,
        )
        if group > 0:
            grad_triple = after(grad_triple, *moved)
        grad_triples.append(grad_triple)
        partial, gain_part, shift_part, total_part = project_back(
            grad_triple, tokens[group], triple_whole
        )
        grad_first_gain = grad_first_gain + gain_part[0]
        grad_first_shift = grad_first_shift + shift_part[0]
        column_sums = column_sums + total_part[0]
        partial = partial.reshape(far_count, 2, rows, width)
        partial = partial[:, 0].astype(F32) + other_core(partial[:, 1]).astype(F32)
        partial = partial.astype(BF)
        moved = far_exchange([partial[r] for r in range(far_count)])
        upper_parts.append(sum(part.astype(F32) for part in moved))
    grad_triple_weight = sum(
        dot_left_t(
            normed[group].reshape(seq_count * rows, width),
            grad_triples[group].reshape(seq_count * rows, 3 * head_width),
        )
        for group in range(groups)
    ).astype(BF)
    upper = jnp.concatenate(upper_parts, 0)
    normal, factor = normalize(inputs)
    grad_images = grad_residual + normalize_back(normal, factor, upper * gain_1)

    def far_total(array):
        total = array.astype(F32)
        for r in range(1, far_count):
            total = total + far_send(array, r).astype(F32)
        return total

    def place_heads(vector):
        here = jnp.arange(far_count)[:, None, None, None] == far
        here = here & (jnp.arange(2)[None, None, :, None] == core)
        vector = vector.reshape(1, near_heads, 1, HEAD_DIM)
        return jnp.where(here, vector, 0.0).reshape(width)

    def place_units(vector):
        vector = vector.reshape(fsdp_count, shard, bias_columns)
        vector = vector.transpose(2, 0, 1).reshape(1, bias_columns, width)
        vector = jnp.where(jnp.arange(2)[:, None, None] == core, vector, 0.0)
        return [vector[i, j] for i in range(2) for j in range(bias_columns)]

    sums = [
        grad_first_gain, grad_first_shift,
        place_heads(column_sums[:head_width]), place_heads(column_sums[2 * head_width :]),
        grad_output_bias, grad_attend_scale, grad_second_gain, grad_second_shift,
        grad_reduce_bias, grad_feed_scale,
    ] + place_units(grad_expand_bias)
    sums = jnp.stack(sums, 0).astype(BF).T
    sums = jnp.pad(sums, ((0, 0), (0, -sums.shape[1] % 128)))
    grad_output_weight = grad_output_weight.reshape(fsdp_count, shard // 2, 2, width // 2)
    grad_output_weight = grad_output_weight.transpose(0, 2, 1, 3).reshape(width, width // 2)
    grad_triple_weight = after(grad_triple_weight, partial)
    grad_packed = jnp.concatenate([grad_triple_weight, sums, grad_output_weight], 1)
    grad_packed = ring_scatter(grad_packed.reshape(fsdp_count, shard, -1)).astype(BF)
    feed_sums = far_total(feed_sums).astype(BF)
    grad_packed = after(grad_packed, feed_sums, *moved)
    grad_packed = jnp.roll(jnp.stack(far_gather(grad_packed), 0), far, 0)
    grad_packed = core_join(grad_packed, 1, core)
    grad_triple_weight = (
        grad_packed[:, :, :, :first]
        .reshape(far_count, 2, shard, 3, near_heads, HEAD_DIM)
        .transpose(2, 3, 0, 4, 1, 5)
        .reshape(shard, 3 * width)
        .astype(F32)
    )
    sums = jnp.sum(grad_packed[:, :, :, first : first + 16].astype(F32), (0, 1)).T
    grad_output_weight = (
        jnp.sum(grad_packed[:, :, :, second:].astype(F32), 0)
        .reshape(2, 2, pairs, HEAD_DIM, width // 2)
        .transpose(2, 0, 3, 1, 4)
        .reshape(shard, width)
    )

    feed_sums = core_join(feed_sums, 0, core).astype(F32)
    grad_expand_weight = (
        feed_sums[:, : blocks * shard]
        .reshape(2, blocks, shard, -1, unit_part)
        .transpose(2, 1, 3, 0, 4)
        .reshape(shard, units)
    )
    grad_reduce_weight = feed_sums[:, blocks * shard :].reshape(2 * unit_part, width)
    grad_expand_bias = (
        sums[10 : 10 + 2 * bias_columns]
        .reshape(2, bias_columns, shard)
        .transpose(0, 2, 1)
        .reshape(2 * unit_part)
    )
    return (
        outputs.reshape(image_count, local_len, width).astype(BF),
        grad_images.reshape(image_count, local_len, width),
        sums[0],
        sums[1],
        grad_triple_weight,
        sums[2],
        sums[3],
        grad_output_weight,
        sums[4],
        sums[5],
        sums[6],
        sums[7],
        grad_expand_weight,
        grad_expand_bias,
        grad_reduce_weight,
        sums[8],
        sums[9],
    )


def layer_norm(inputs, gain, shift):
    average = jnp.mean(inputs, -1, keepdims=True)
    centered = inputs - average
    variance = jnp.mean(centered * centered, -1, keepdims=True)
    return centered * lax.rsqrt(variance + EPSILON) * gain + shift


def exact_gelu(values):
    return jax.nn.gelu(values, approximate=False)


def to_float(array):
    return array.astype(jnp.float32)


def plain_matmul(left, right):
    return jnp.dot(left, right, preferred_element_type=jnp.float32)


def plain_matmul_left_t(left, right):
    return lax.dot_general(
        left, right, (((0,), (0,)), ((), ())), preferred_element_type=jnp.float32
    )


def plain_matmul_right_t(left, right):
    return lax.dot_general(
        left, right, (((1,), (1,)), ((), ())), preferred_element_type=jnp.float32
    )


def plain_column_total(array):
    return plain_matmul(jnp.ones((1, array.shape[0]), jnp.bfloat16), array)[0]


def masked_scores(queries, key_rows, live_count, factor):
    scores = (
        jnp.einsum("qhd,khd->hqk", queries, key_rows, preferred_element_type=jnp.float32) * factor
    )
    live_keys = lax.broadcasted_iota(jnp.int32, (1, 1, key_rows.shape[0]), 2) < live_count
    return jnp.where(live_keys, scores, -1e30)


def plain_attend_forward(bundle):
    packed, live_count = bundle
    length, triple_count, local_width = packed.shape
    head_count = local_width // HEAD_DIM
    unpacked = packed.reshape(length, triple_count, head_count, HEAD_DIM)
    factor = HEAD_DIM ** (-0.5)
    scores = masked_scores(unpacked[:, 0], unpacked[:, 1], live_count, factor)
    highest = jnp.max(scores, -1, keepdims=True)
    powers = jnp.exp(scores - highest)
    row_total = jnp.sum(powers, -1, keepdims=True)
    weights_low = (powers / row_total).astype(jnp.bfloat16)
    mixed_rows = jnp.einsum(
        "hqk,khd->qhd", weights_low, unpacked[:, 2], preferred_element_type=jnp.float32
    )
    logsum = highest + jnp.log(row_total)
    return (mixed_rows.reshape(length, local_width).astype(jnp.bfloat16), logsum)


def plain_attend_backward(bundle):
    packed, grad_mixed, logsum, live_count = bundle
    length, triple_count, local_width = packed.shape
    head_count = local_width // HEAD_DIM
    unpacked = packed.reshape(length, triple_count, head_count, HEAD_DIM)
    factor = HEAD_DIM ** (-0.5)
    scores = masked_scores(unpacked[:, 0], unpacked[:, 1], live_count, factor)
    probs = jnp.exp(scores - logsum)
    grad_heads = grad_mixed.reshape(length, head_count, HEAD_DIM)
    grad_probs = jnp.einsum(
        "qhd,khd->hqk", grad_heads, unpacked[:, 2], preferred_element_type=jnp.float32
    )
    grad_values = jnp.einsum(
        "hqk,qhd->khd", probs.astype(jnp.bfloat16), grad_heads, preferred_element_type=jnp.float32
    )
    inner = jnp.sum(probs * grad_probs, -1, keepdims=True)
    grad_scores = (probs * (grad_probs - inner)).astype(jnp.bfloat16)
    grad_queries = (
        jnp.einsum("hqk,khd->qhd", grad_scores, unpacked[:, 1], preferred_element_type=jnp.float32)
        * factor
    )
    grad_keys = (
        jnp.einsum("hqk,qhd->khd", grad_scores, unpacked[:, 0], preferred_element_type=jnp.float32)
        * factor
    )
    stacked = jnp.stack([grad_queries, grad_keys, grad_values], 1)
    return stacked.reshape(length, triple_count, local_width).astype(jnp.bfloat16)


def plain_shards(
    images,
    cotangent,
    valid_count,
    first_gain,
    first_shift,
    triple_weight,
    query_bias,
    value_bias,
    output_weight,
    output_bias,
    attend_scale,
    second_gain,
    second_shift,
    expand_weight,
    expand_bias,
    reduce_weight,
    reduce_bias,
    feed_scale,
):
    image_count, local_len, width = images.shape
    gathered = (
        lax.all_gather(first_gain, "fsdp", axis=0, tiled=True),
        lax.all_gather(first_shift, "fsdp", axis=0, tiled=True),
        lax.all_gather(triple_weight, "fsdp", axis=0, tiled=True),
        lax.all_gather(query_bias, "fsdp", axis=0, tiled=True),
        lax.all_gather(value_bias, "fsdp", axis=0, tiled=True),
        lax.all_gather(output_weight, "fsdp", axis=0, tiled=True),
        lax.all_gather(output_bias, "fsdp", axis=0, tiled=True),
        lax.all_gather(attend_scale, "fsdp", axis=0, tiled=True),
        lax.all_gather(second_gain, "fsdp", axis=0, tiled=True),
        lax.all_gather(second_shift, "fsdp", axis=0, tiled=True),
        lax.all_gather(expand_weight, "fsdp", axis=0, tiled=True),
        lax.all_gather(expand_bias, "fsdp", axis=0, tiled=True),
        lax.all_gather(reduce_weight, "fsdp", axis=0, tiled=True),
        lax.all_gather(reduce_bias, "fsdp", axis=0, tiled=True),
        lax.all_gather(feed_scale, "fsdp", axis=0, tiled=True),
    )
    inputs = images.astype(jnp.float32).reshape(-1, width)
    first_normed = layer_norm(inputs, to_float(gathered[0]), to_float(gathered[1])).astype(
        jnp.bfloat16
    )
    joint_bias = to_float(jnp.concatenate([gathered[3], jnp.zeros_like(gathered[3]), gathered[4]]))
    triple = (plain_matmul(first_normed, gathered[2]) + joint_bias).astype(jnp.bfloat16)
    triple = triple.reshape(image_count, local_len, 3, width)
    by_heads = lax.all_to_all(triple, "seq", split_axis=3, concat_axis=1, tiled=True)
    attended, logsums = lax.map(plain_attend_forward, (by_heads, valid_count))
    by_tokens = lax.all_to_all(attended, "seq", split_axis=1, concat_axis=2, tiled=True)
    attended_rows = by_tokens.reshape(-1, width)
    branch_attend = plain_matmul(attended_rows, gathered[5]) + to_float(gathered[6])
    residual = inputs + to_float(gathered[7]) * branch_attend
    second_normed = layer_norm(residual, to_float(gathered[8]), to_float(gathered[9])).astype(
        jnp.bfloat16
    )
    expanded = plain_matmul(second_normed, gathered[10]) + to_float(gathered[11])
    activated = exact_gelu(expanded).astype(jnp.bfloat16)
    branch_feed = plain_matmul(activated, gathered[12]) + to_float(gathered[13])
    outputs = residual + to_float(gathered[14]) * branch_feed
    weights = (
        lax.all_gather(first_gain, "fsdp", axis=0, tiled=True),
        lax.all_gather(first_shift, "fsdp", axis=0, tiled=True),
        lax.all_gather(triple_weight, "fsdp", axis=0, tiled=True),
        lax.all_gather(query_bias, "fsdp", axis=0, tiled=True),
        lax.all_gather(value_bias, "fsdp", axis=0, tiled=True),
        lax.all_gather(output_weight, "fsdp", axis=0, tiled=True),
        lax.all_gather(output_bias, "fsdp", axis=0, tiled=True),
        lax.all_gather(attend_scale, "fsdp", axis=0, tiled=True),
        lax.all_gather(second_gain, "fsdp", axis=0, tiled=True),
        lax.all_gather(second_shift, "fsdp", axis=0, tiled=True),
        lax.all_gather(expand_weight, "fsdp", axis=0, tiled=True),
        lax.all_gather(expand_bias, "fsdp", axis=0, tiled=True),
        lax.all_gather(reduce_weight, "fsdp", axis=0, tiled=True),
        lax.all_gather(reduce_bias, "fsdp", axis=0, tiled=True),
        lax.all_gather(feed_scale, "fsdp", axis=0, tiled=True),
    )
    upstream = cotangent.astype(jnp.float32).reshape(-1, width)
    grad_feed_scale = jnp.sum(upstream * branch_feed, 0)
    grad_feed = (to_float(weights[14]) * upstream).astype(jnp.bfloat16)
    grad_reduce_bias = plain_column_total(grad_feed)
    grad_reduce_weight = plain_matmul_left_t(activated, grad_feed)
    grad_activated = plain_matmul_right_t(grad_feed, weights[12])
    unused, gelu_pull = jax.vjp(exact_gelu, expanded)
    grad_expanded = gelu_pull(grad_activated)[0].astype(jnp.bfloat16)
    grad_expand_bias = plain_column_total(grad_expanded)
    grad_expand_weight = plain_matmul_left_t(second_normed, grad_expanded)
    grad_second_normed = plain_matmul_right_t(grad_expanded, weights[10])
    unused, second_pull = jax.vjp(layer_norm, residual, to_float(weights[8]), to_float(weights[9]))
    grad_residual_norm, grad_second_gain, grad_second_shift = second_pull(grad_second_normed)
    grad_residual = upstream + grad_residual_norm
    grad_attend_scale = jnp.sum(grad_residual * branch_attend, 0)
    grad_attend = (to_float(weights[7]) * grad_residual).astype(jnp.bfloat16)
    grad_output_bias = plain_column_total(grad_attend)
    grad_output_weight = plain_matmul_left_t(attended_rows, grad_attend)
    grad_attended = plain_matmul_right_t(grad_attend, weights[5]).astype(jnp.bfloat16)
    grad_attended = grad_attended.reshape(image_count, local_len, width)
    grad_by_heads = lax.all_to_all(grad_attended, "seq", split_axis=2, concat_axis=1, tiled=True)
    grad_triple_heads = lax.map(plain_attend_backward, (by_heads, grad_by_heads, logsums, valid_count))
    grad_triple = lax.all_to_all(grad_triple_heads, "seq", split_axis=1, concat_axis=3, tiled=True)
    grad_triple = grad_triple.reshape(-1, 3 * width)
    column_sums = plain_column_total(grad_triple)
    grad_query_bias = column_sums[:width]
    grad_value_bias = column_sums[2 * width :]
    grad_triple_weight = plain_matmul_left_t(first_normed, grad_triple)
    grad_first_normed = plain_matmul_right_t(grad_triple, weights[2])
    unused, first_pull = jax.vjp(layer_norm, inputs, to_float(weights[0]), to_float(weights[1]))
    grad_inputs_norm, grad_first_gain, grad_first_shift = first_pull(grad_first_normed)
    grad_images = grad_residual + grad_inputs_norm
    owned = (
        lax.psum_scatter(
            grad_first_gain.astype(jnp.bfloat16), "fsdp", scatter_dimension=0, tiled=True
        ).astype(jnp.float32),
        lax.psum_scatter(
            grad_first_shift.astype(jnp.bfloat16), "fsdp", scatter_dimension=0, tiled=True
        ).astype(jnp.float32),
        lax.psum_scatter(
            grad_triple_weight.astype(jnp.bfloat16), "fsdp", scatter_dimension=0, tiled=True
        ).astype(jnp.float32),
        lax.psum_scatter(
            grad_query_bias.astype(jnp.bfloat16), "fsdp", scatter_dimension=0, tiled=True
        ).astype(jnp.float32),
        lax.psum_scatter(
            grad_value_bias.astype(jnp.bfloat16), "fsdp", scatter_dimension=0, tiled=True
        ).astype(jnp.float32),
        lax.psum_scatter(
            grad_output_weight.astype(jnp.bfloat16), "fsdp", scatter_dimension=0, tiled=True
        ).astype(jnp.float32),
        lax.psum_scatter(
            grad_output_bias.astype(jnp.bfloat16), "fsdp", scatter_dimension=0, tiled=True
        ).astype(jnp.float32),
        lax.psum_scatter(
            grad_attend_scale.astype(jnp.bfloat16), "fsdp", scatter_dimension=0, tiled=True
        ).astype(jnp.float32),
        lax.psum_scatter(
            grad_second_gain.astype(jnp.bfloat16), "fsdp", scatter_dimension=0, tiled=True
        ).astype(jnp.float32),
        lax.psum_scatter(
            grad_second_shift.astype(jnp.bfloat16), "fsdp", scatter_dimension=0, tiled=True
        ).astype(jnp.float32),
        lax.psum_scatter(
            grad_expand_weight.astype(jnp.bfloat16), "fsdp", scatter_dimension=0, tiled=True
        ).astype(jnp.float32),
        lax.psum_scatter(
            grad_expand_bias.astype(jnp.bfloat16), "fsdp", scatter_dimension=0, tiled=True
        ).astype(jnp.float32),
        lax.psum_scatter(
            grad_reduce_weight.astype(jnp.bfloat16), "fsdp", scatter_dimension=0, tiled=True
        ).astype(jnp.float32),
        lax.psum_scatter(
            grad_reduce_bias.astype(jnp.bfloat16), "fsdp", scatter_dimension=0, tiled=True
        ).astype(jnp.float32),
        lax.psum_scatter(
            grad_feed_scale.astype(jnp.bfloat16), "fsdp", scatter_dimension=0, tiled=True
        ).astype(jnp.float32),
    )
    summed = lax.psum(
        (
            owned[0],
            owned[1],
            owned[2],
            owned[3],
            owned[4],
            owned[5],
            owned[6],
            owned[7],
            owned[8],
            owned[9],
            owned[10],
            owned[11],
            owned[12],
            owned[13],
            owned[14],
        ),
        "seq",
    )
    return (
        outputs.reshape(image_count, local_len, width).astype(jnp.bfloat16),
        grad_images.reshape(image_count, local_len, width),
        summed[0],
        summed[1],
        summed[2],
        summed[3],
        summed[4],
        summed[5],
        summed[6],
        summed[7],
        summed[8],
        summed[9],
        summed[10],
        summed[11],
        summed[12],
        summed[13],
        summed[14],
    )


def solution(mesh):
    fsdp, seq = mesh.devices.shape
    if seq == 4 and fsdp == 8:
        plan, tokens = shards, P("fsdp", ("far", "core"), None)
        mesh = Mesh(mesh.devices.reshape(fsdp, 2, 2), ("fsdp", "far", "core"))
    else:
        plan, tokens = plain_shards, P("fsdp", "seq", None)
    row, matrix = P("fsdp"), P("fsdp", None)
    return jax.shard_map(
        plan,
        mesh=mesh,
        in_specs=(
            tokens, tokens, row, row, row, matrix, row, row, matrix,
            row, row, row, row, matrix, row, matrix, row, row,
        ),
        out_specs=(
            tokens, tokens, row, row, matrix, row, row, matrix,
            row, row, row, row, matrix, row, matrix, row, row,
        ),
        check_vma=False,
    )
```

```python
import functools

import jax
import jax.numpy as jnp
from jax import lax
from jax.experimental import pallas as pl
from jax.experimental.pallas import tpu as pltpu
from jax.sharding import Mesh, PartitionSpec as P

HEAD_DIM = 64
EPSILON = 1e-06
BF = jnp.bfloat16
F32 = jnp.float32
MASKED = -1e30


def dot(left, right):
    return lax.dot_general(left, right, (((1,), (0,)), ((), ())), preferred_element_type=F32)


def dot_left_t(left, right):
    return lax.dot_general(left, right, (((0,), (0,)), ((), ())), preferred_element_type=F32)


def dot_right_t(left, right):
    return lax.dot_general(left, right, (((1,), (1,)), ((), ())), preferred_element_type=F32)


def column_total(array):
    return dot(jnp.ones((8, array.shape[0]), BF), array)[0]


def normalize(rows):
    average = jnp.mean(rows, -1, keepdims=True)
    centered = rows - average
    variance = jnp.mean(centered * centered, -1, keepdims=True)
    factor = lax.rsqrt(variance + EPSILON)
    return centered * factor, factor


def normalize_back(normal, factor, weighted):
    return factor * (
        weighted
        - jnp.mean(weighted, -1, keepdims=True)
        - normal * jnp.mean(weighted * normal, -1, keepdims=True)
    )


def spans(total, step):
    return [(start, min(step, total - start)) for start in range(0, total, step)]


def merge(ref, out):
    pieces, _, rows, _ = ref.shape
    for piece in range(pieces):
        out[pl.ds(piece * rows, rows), :] = ref[piece, 0].astype(F32)


def lane_parts(block, heads, head):
    lane = lax.broadcasted_iota(jnp.int32, (1, block), 1)
    if heads == 1:
        return lane < HEAD_DIM, lane - HEAD_DIM
    if head == 0:
        return lane < HEAD_DIM, lane - HEAD_DIM
    return lane >= HEAD_DIM, lane


def split_three(values):
    high = values.astype(BF).astype(F32)
    rest = values - high
    middle = rest.astype(BF).astype(F32)
    return high, middle, rest - middle


def dead_column(limit_ref, length):
    image = pl.program_id(0)
    row = lax.broadcasted_iota(jnp.int32, (length, 1), 0)
    dead = (row >= limit_ref[image, 0]) & (row < limit_ref[image, 1])
    return jnp.where(dead, MASKED, 0.0)


def attend_forward_kernel(limit_ref, q_ref, k_ref, v_ref, out_ref, log_ref, q_s, k_s, v_s, o_s):
    pieces, _, rows, block = q_ref.shape
    length = pieces * rows
    heads = max(block // HEAD_DIM, 1)
    merge(q_ref, q_s)
    merge(k_ref, k_s)
    merge(v_ref, v_s)
    dead = dead_column(limit_ref, length)
    aug = []
    for head in range(heads):
        own, spare = lane_parts(2 * HEAD_DIM, heads, head)
        q = jnp.where(own, q_s[...] * 0.125, jnp.where(spare == 0, 1.0, 0.0)).astype(BF)
        k = jnp.where(own, k_s[...], jnp.where(spare == 0, dead, 0.0)).astype(BF)
        v = jnp.where(own, v_s[...], jnp.where(spare == 0, 1.0, 0.0)).astype(BF)
        aug.append((q, k, v))
    for start, size in spans(length, 352):
        results = []
        for head in range(heads):
            q, k, v = aug[head]
            scores = dot_right_t(q[start : start + size], k)
            top = jnp.max(scores, -1, keepdims=True)
            powers = jnp.exp(scores - top).astype(BF)
            mixed = dot(powers, v)
            own, spare = lane_parts(2 * HEAD_DIM, heads, head)
            at = HEAD_DIM if head == 0 else 0
            total = mixed[:, at : at + 1]
            results.append((mixed / total, top + jnp.log(total)))
        own, _ = lane_parts(2 * HEAD_DIM, heads, 0)
        if heads == 1:
            o_s[pl.ds(start, size), :] = results[0][0]
            log_ref[0, 0, pl.ds(start, size), :] = jnp.broadcast_to(
                results[0][1], (size, 2 * HEAD_DIM)
            )
        else:
            o_s[pl.ds(start, size), :] = jnp.where(own, results[0][0], results[1][0])
            log_ref[0, 0, pl.ds(start, size), :] = jnp.where(own, results[1][1], results[0][1])
    for piece in range(pieces):
        out_ref[piece, 0] = o_s[pl.ds(piece * rows, rows), :].astype(BF)


def attend_backward_kernel(
    limit_ref, q_ref, k_ref, v_ref, o_ref, g_ref, log_ref, grad_ref,
    q_s, k_s, v_s, o_s, g_s, dq_s, dk_s, dv_s,
):
    pieces, _, rows, block = q_ref.shape
    length = pieces * rows
    heads = max(block // HEAD_DIM, 1)
    merge(q_ref, q_s)
    merge(k_ref, k_s)
    merge(v_ref, v_s)
    merge(o_ref, o_s)
    merge(g_ref, g_s)
    dead = dead_column(limit_ref, length)
    product = o_s[...] * g_s[...]
    for head in range(heads):
        own, spare = lane_parts(2 * HEAD_DIM, heads, head)
        log_parts = split_three(log_ref[0, 0])
        inner = jnp.sum(jnp.where(own, product, 0.0), -1, keepdims=True)
        inner_parts = split_three(inner)
        zero = jnp.zeros((length, 2 * HEAD_DIM), F32)
        q_tail, k_tail, v_tail, g_tail = zero, zero, zero, zero
        for place in range(3):
            q_tail = jnp.where(spare == place, -log_parts[place], q_tail)
            g_tail = jnp.where(spare == place, -inner_parts[place], g_tail)
            k_tail = jnp.where(spare == place, 1.0, k_tail)
            v_tail = jnp.where(spare == place, 1.0, v_tail)
        q_tail = jnp.where(spare == 3, 1.0, q_tail)
        k_tail = jnp.where(spare == 3, dead, k_tail)
        q = jnp.where(own, q_s[...] * 0.125, q_tail).astype(BF)
        k = jnp.where(own, k_s[...], k_tail).astype(BF)
        v = jnp.where(own, v_s[...], v_tail).astype(BF)
        g = jnp.where(own, g_s[...], g_tail).astype(BF)
        k_t = jnp.where(own, k_s[...] * 0.125, 0.0).T.astype(BF)
        dk = dv = None
        for start, size in spans(length, 512):
            q_part, g_part = q[start : start + size], g[start : start + size]
            probs = jnp.exp(dot_right_t(k, q_part))
            slopes = (probs * dot_right_t(v, g_part)).astype(BF)
            probs = probs.astype(BF)
            dv_part = dot(probs, g_part)
            dk_part = dot(slopes, q_part)
            dv = dv_part if dv is None else dv + dv_part
            dk = dk_part if dk is None else dk + dk_part
            dq_part = dot(k_t, slopes).T
            if head == 0:
                dq_s[pl.ds(start, size), :] = dq_part
            else:
                dq_s[pl.ds(start, size), :] += dq_part
        if head == 0:
            dk_s[...] = dk
            dv_s[...] = dv
        else:
            dk_s[...] = jnp.where(own, dk, dk_s[...])
            dv_s[...] = jnp.where(own, dv, dv_s[...])
    stride = grad_ref.shape[3] // 3
    for piece in range(pieces):
        part = pl.ds(piece * rows, rows)
        for which, grad in enumerate((dq_s, dk_s, dv_s)):
            at = pl.multiple_of(which * stride + pl.program_id(1) * block, block)
            grad_ref[piece, 0, :, pl.ds(at, block)] = grad[part, :].astype(BF)


def attend_specs(pieces, rows, first):
    def at(limit_index):
        return pl.BlockSpec(
            (pieces, 1, rows, 2 * HEAD_DIM),
            lambda image, pair, limits: (0, image, 0, limit_index + pair),
        )

    return at(first)


def attend_forward(triple, limits):
    pieces, images, rows, columns = triple.shape
    head_width = columns // 3
    length = pieces * rows
    pairs = head_width // (2 * HEAD_DIM)
    wide = pltpu.VMEM((length, 2 * HEAD_DIM), F32)
    spec = functools.partial(attend_specs, pieces, rows)
    heads = images * head_width // HEAD_DIM
    return pl.pallas_call(
        attend_forward_kernel,
        grid_spec=pltpu.PrefetchScalarGridSpec(
            num_scalar_prefetch=1,
            grid=(images, pairs),
            in_specs=[spec(0), spec(pairs), spec(2 * pairs)],
            out_specs=[
                spec(0),
                pl.BlockSpec((1, 1, length, 2 * HEAD_DIM), lambda i, p, limits: (i, p, 0, 0)),
            ],
            scratch_shapes=[wide] * 4,
        ),
        out_shape=[
            jax.ShapeDtypeStruct((pieces, images, rows, head_width), BF),
            jax.ShapeDtypeStruct((images, pairs, length, 2 * HEAD_DIM), F32),
        ],
        compiler_params=pltpu.CompilerParams(vmem_limit_bytes=50 * 2**20),
        cost_estimate=pl.CostEstimate(
            flops=heads * length * length * 1024,
            bytes_accessed=4 * triple.size,
            transcendentals=heads * length * length,
        ),
        name="attend_forward",
    )(limits, triple, triple, triple)


def attend_backward(triple, attended, grad, logs, limits):
    pieces, images, rows, columns = triple.shape
    head_width = columns // 3
    length = pieces * rows
    pairs = head_width // (2 * HEAD_DIM)
    wide = pltpu.VMEM((length, 2 * HEAD_DIM), F32)
    spec = functools.partial(attend_specs, pieces, rows)
    heads = images * head_width // HEAD_DIM
    return pl.pallas_call(
        attend_backward_kernel,
        grid_spec=pltpu.PrefetchScalarGridSpec(
            num_scalar_prefetch=1,
            grid=(images, pairs),
            in_specs=[
                spec(0),
                spec(pairs),
                spec(2 * pairs),
                spec(0),
                spec(0),
                pl.BlockSpec((1, 1, length, 2 * HEAD_DIM), lambda i, p, limits: (i, p, 0, 0)),
            ],
            out_specs=pl.BlockSpec(
                (pieces, 1, rows, columns), lambda image, pair, limits: (0, image, 0, 0)
            ),
            scratch_shapes=[wide] * 8,
        ),
        out_shape=jax.ShapeDtypeStruct(triple.shape, BF),
        compiler_params=pltpu.CompilerParams(vmem_limit_bytes=56 * 2**20),
        cost_estimate=pl.CostEstimate(
            flops=heads * length * length * 2560,
            bytes_accessed=8 * triple.size,
            transcendentals=heads * length * length,
        ),
        name="attend_backward",
    )(limits, triple, triple, triple, attended, grad, logs)


def project_kernel(rows_ref, small_ref, weight_ref, bias_ref, normed_ref, triple_ref):
    normal, _ = normalize(rows_ref[0].astype(F32))
    normed = (normal * small_ref[0:1, :] + small_ref[1:2, :]).astype(BF)
    normed_ref[0] = normed
    triple_ref[0] = (dot(normed, weight_ref[...]) + bias_ref[...]).astype(BF)


def project(tokens, small, weight, bias):
    pieces, rows, width = tokens.shape
    columns = weight.shape[1]

    def whole(array):
        return pl.BlockSpec(array.shape, lambda i: (0, 0))

    def piece(columns):
        return pl.BlockSpec((1, rows, columns), lambda i: (i, 0, 0))

    return pl.pallas_call(
        project_kernel,
        grid=(pieces,),
        in_specs=[piece(width), whole(small), whole(weight), whole(bias)],
        out_specs=[piece(width), piece(columns)],
        out_shape=[
            jax.ShapeDtypeStruct((pieces, rows, width), BF),
            jax.ShapeDtypeStruct((pieces, rows, columns), BF),
        ],
        compiler_params=pltpu.CompilerParams(vmem_limit_bytes=40 * 2**20),
        cost_estimate=pl.CostEstimate(
            flops=2 * pieces * rows * width * columns,
            bytes_accessed=2 * pieces * rows * (2 * width + columns),
            transcendentals=0,
        ),
        name="project",
    )(tokens, small, weight, bias)


def project_back_kernel(grad_ref, rows_ref, weight_ref, part_ref, gain_ref, shift_ref, total_ref):
    @pl.when(pl.program_id(0) == 0)
    def _():
        gain_ref[...] = jnp.zeros_like(gain_ref)
        shift_ref[...] = jnp.zeros_like(shift_ref)
        total_ref[...] = jnp.zeros_like(total_ref)

    normal, _ = normalize(rows_ref[0].astype(F32))
    part = dot_right_t(grad_ref[0], weight_ref[...])
    part_ref[0] = part.astype(BF)
    gain_ref[...] += jnp.sum(part * normal, 0, keepdims=True)
    shift_ref[...] += jnp.sum(part, 0, keepdims=True)
    total_ref[...] += jnp.sum(grad_ref[0].astype(F32), 0, keepdims=True)


def project_back(grad, tokens, weight):
    pieces, rows, width = tokens.shape
    columns = weight.shape[1]

    def piece(columns):
        return pl.BlockSpec((1, rows, columns), lambda i: (i, 0, 0))

    def whole(shape):
        return pl.BlockSpec(shape, lambda i: (0, 0))

    return pl.pallas_call(
        project_back_kernel,
        grid=(pieces,),
        in_specs=[piece(columns), piece(width), whole(weight.shape)],
        out_specs=[piece(width), whole((1, width)), whole((1, width)), whole((1, columns))],
        out_shape=[
            jax.ShapeDtypeStruct((pieces, rows, width), BF),
            jax.ShapeDtypeStruct((1, width), F32),
            jax.ShapeDtypeStruct((1, width), F32),
            jax.ShapeDtypeStruct((1, columns), F32),
        ],
        compiler_params=pltpu.CompilerParams(vmem_limit_bytes=40 * 2**20),
        cost_estimate=pl.CostEstimate(
            flops=2 * pieces * rows * width * columns,
            bytes_accessed=2 * pieces * rows * (2 * width + columns),
            transcendentals=0,
        ),
        name="project_back",
    )(grad, tokens, weight)


def gelu_parts(values):
    size = jnp.abs(values) * 0.7071067811865476
    bell = jnp.exp(-size * size)
    t = 1.0 / (1.0 + 0.3275911 * size)
    tail = t * (
        0.254829592
        + t * (-0.284496736 + t * (1.421413741 + t * (-1.453152027 + t * 1.061405429)))
    )
    tail = 0.5 * tail * bell
    return jnp.where(values >= 0.0, 1.0 - tail, tail), 0.3989422804014327 * bell


def expand_kernel(rows_ref, weight_ref, bias_ref, active_ref, slope_ref):
    count, width = rows_ref.shape
    weight = weight_ref[...].reshape(width, weight_ref.shape[2])
    for start, size in spans(count, 352):
        expanded = dot(rows_ref[start : start + size, :], weight) + bias_ref[...]
        below, density = gelu_parts(expanded)
        active_ref[start : start + size, :] = (expanded * below).astype(BF)
        slope_ref[start : start + size, :] = (below + expanded * density).astype(BF)


def expand_rows(rows, feed_weights, bias):
    count, width = rows.shape
    devices = feed_weights.shape[0]
    shard = width // devices
    units = bias.shape[1]
    tile = 256
    across = width // tile
    shape = jax.ShapeDtypeStruct((count, units), BF)
    return pl.pallas_call(
        expand_kernel,
        grid=(units // tile,),
        in_specs=[
            pl.BlockSpec((count, width), lambda i: (0, 0)),
            pl.BlockSpec((devices, shard, tile), lambda i: (0, i // across, i % across)),
            pl.BlockSpec((1, tile), lambda i: (0, i)),
        ],
        out_specs=[pl.BlockSpec((count, tile), lambda i: (0, i))] * 2,
        out_shape=[shape] * 2,
        compiler_params=pltpu.CompilerParams(vmem_limit_bytes=48 * 2**20),
        cost_estimate=pl.CostEstimate(
            flops=4 * count * units * width,
            bytes_accessed=2 * (count * width + width * units + 2 * count * units),
            transcendentals=2 * count * units,
        ),
        name="expand_rows",
    )(rows, feed_weights, bias)


def feed_grads_kernel(rows_ref, active_ref, expanded_ref, feed_ref, out_ref):
    shard, width = rows_ref.shape[1], out_ref.shape[2]
    blocks = expanded_ref.shape[1] // width
    for block in range(blocks):
        out_ref[0, block * shard : (block + 1) * shard, :] = dot_left_t(
            rows_ref[...], expanded_ref[:, block * width : (block + 1) * width]
        ).astype(BF)
    out_ref[0, blocks * shard :, :] = dot_left_t(active_ref[...], feed_ref[...]).astype(BF)


def feed_grads(rows, active, grad_expanded, grad_feed, devices):
    count, width = rows.shape
    units = active.shape[1]
    shard, unit_part = width // devices, units // devices
    blocks = units // width
    if shard % 128 != 0 or unit_part % 128 != 0:
        expand = dot_left_t(rows, grad_expanded).astype(BF).reshape(devices, shard, blocks, width)
        expand = expand.transpose(0, 2, 1, 3).reshape(devices, blocks * shard, width)
        reduce = dot_left_t(active, grad_feed).astype(BF).reshape(devices, unit_part, width)
        return jnp.concatenate([expand, reduce], 1)
    height = blocks * shard + unit_part
    return pl.pallas_call(
        feed_grads_kernel,
        grid=(devices,),
        in_specs=[
            pl.BlockSpec((count, shard), lambda i: (0, i)),
            pl.BlockSpec((count, unit_part), lambda i: (0, i)),
            pl.BlockSpec((count, units), lambda i: (0, 0)),
            pl.BlockSpec((count, width), lambda i: (0, 0)),
        ],
        out_specs=pl.BlockSpec((1, height, width), lambda i: (i, 0, 0)),
        out_shape=jax.ShapeDtypeStruct((devices, height, width), BF),
        compiler_params=pltpu.CompilerParams(vmem_limit_bytes=52 * 2**20),
        cost_estimate=pl.CostEstimate(
            flops=4 * count * units * width,
            bytes_accessed=2 * (2 * count * (width + units) + 2 * width * units),
            transcendentals=0,
        ),
        name="feed_grads",
    )(rows, active, grad_expanded, grad_feed)


def far_send(array, shift):
    count = lax.axis_size("far")
    return lax.ppermute(array, "far", [(i, (i + shift) % count) for i in range(count)])


def far_gather(array):
    count = lax.axis_size("far")
    return [array] + [far_send(array, count - r) for r in range(1, count)]


def far_exchange(slots):
    count = len(slots)
    out = [slots[0]] + [None] * (count - 1)
    for r in range(1, count):
        out[count - r] = far_send(slots[r], r)
    return out


def far_sum(slots):
    arrived = far_exchange(slots)
    return sum(part.astype(F32) for part in arrived)


def other_core(array):
    return lax.ppermute(array, "core", [(0, 1), (1, 0)])


def fsdp_gather(array):
    return lax.all_gather(array, "fsdp", axis=0, tiled=True)


def fsdp_scatter(array):
    return lax.psum_scatter(array, "fsdp", scatter_dimension=0, tiled=True)


def ring_send(array, step):
    count = lax.axis_size("fsdp")
    order = list(range(0, count, 2)) + list(range(1, count, 2))[::-1]
    pairs = [(order[i], order[(i + step) % count]) for i in range(count)]
    return lax.ppermute(array, "fsdp", pairs)


def ring_index(offset):
    count, index = lax.axis_size("fsdp"), lax.axis_index("fsdp")
    place = jnp.where(index % 2 == 0, index // 2, count - 1 - index // 2)
    place = (place + offset + count) % count
    return jnp.where(place < count // 2, 2 * place, 2 * (count - 1 - place) + 1)


def ring_scatter(array):
    count = lax.axis_size("fsdp")

    def block(offset):
        return lax.dynamic_index_in_dim(array, ring_index(offset), 0, False).astype(F32)

    total = block(0)
    for direction, hops in ((1, count // 2), (-1, (count - 1) // 2)):
        moving = block(direction * hops)
        for step in range(1, hops + 1):
            moving = ring_send(moving.astype(BF), direction).astype(F32)
            if step < hops:
                moving = moving + block(direction * (hops - step))
        total = total + moving
    return total


def after(array, *earlier):
    return lax.optimization_barrier((array,) + earlier)[0]


def core_join(mine, axis, core):
    other = other_core(mine)
    return jnp.stack(
        [jnp.where(core == 0, mine, other), jnp.where(core == 0, other, mine)], axis
    )


def shards(
    images,
    cotangent,
    valid_count,
    first_gain,
    first_shift,
    triple_weight,
    query_bias,
    value_bias,
    output_weight,
    output_bias,
    attend_scale,
    second_gain,
    second_shift,
    expand_weight,
    expand_bias,
    reduce_weight,
    reduce_bias,
    feed_scale,
):
    image_count, local_len, width = images.shape
    own_rows = image_count * local_len
    far_count, fsdp_count = lax.axis_size("far"), lax.axis_size("fsdp")
    far, core = lax.axis_index("far"), lax.axis_index("core")
    seq_count = 2 * far_count
    shard = width // fsdp_count
    units = expand_weight.shape[1]
    unit_part = units // (2 * fsdp_count)
    near_heads = width // HEAD_DIM // seq_count
    head_width = near_heads * HEAD_DIM

    def my_heads(array, axis):
        shape = array.shape
        array = array.reshape(
            shape[:axis] + (far_count, near_heads, 2, HEAD_DIM) + shape[axis + 1 :]
        )
        array = lax.dynamic_index_in_dim(array, far, axis, False)
        array = lax.dynamic_index_in_dim(array, core, axis + 1, False)
        return array.reshape(shape[:axis] + (head_width,) + shape[axis + 1 :])

    triple_mine = my_heads(triple_weight.reshape(shard, 3, width), 2).reshape(shard, 3 * head_width)
    bias_mine = lax.dynamic_index_in_dim(expand_bias.reshape(2, unit_part), core, 0, False)
    bias_columns = unit_part // shard
    vectors = [
        first_gain, first_shift, query_bias, value_bias, output_bias, attend_scale,
        second_gain, second_shift, reduce_bias, feed_scale,
    ]
    vector_count = len(vectors)
    small_mine = jnp.concatenate(
        [jnp.stack(vectors, 1), bias_mine.reshape(shard, bias_columns)], 1
    )
    small_mine = jnp.pad(small_mine, ((0, 0), (0, -small_mine.shape[1] % 128)))
    pairs = shard // (2 * HEAD_DIM)
    output_mine = lax.dynamic_index_in_dim(
        output_weight.reshape(pairs, 2, HEAD_DIM, width), core, 1, False
    )
    output_mine = output_mine.reshape(shard // 2, 2, width // 2).transpose(1, 0, 2)
    output_mine = output_mine.reshape(shard, width // 2)
    first = 3 * head_width
    second = first + small_mine.shape[1]
    packed = fsdp_gather(jnp.concatenate([triple_mine, small_mine, output_mine], 1))
    triple_whole = packed[:, :first]
    small = packed[:, first : first + 16].astype(F32).T
    output_whole = packed[:, second:].reshape(fsdp_count, 2, shard // 2, width // 2)
    output_whole = output_whole.transpose(0, 2, 1, 3).reshape(far_count, head_width, width)
    output_whole = jnp.roll(output_whole, -far, 0).reshape(width // 2, width)
    (gain_1, shift_1, bias_q, bias_v, bias_o, scale_a, gain_2, shift_2, bias_r, scale_f) = [
        small[i] for i in range(vector_count)
    ]
    bias_e = (
        small[vector_count : vector_count + bias_columns]
        .reshape(bias_columns, fsdp_count, shard)
        .transpose(1, 2, 0)
        .reshape(1, fsdp_count * unit_part)
    )

    blocks = units // 2 // width
    expand_mine = lax.dynamic_index_in_dim(
        expand_weight.reshape(shard, fsdp_count, 2, unit_part), core, 2, False
    ).reshape(shard, blocks, width)
    reduce_mine = lax.dynamic_index_in_dim(
        reduce_weight.reshape(2, unit_part, width), core, 0, False
    )
    feed_mine = jnp.concatenate([expand_mine[:, i] for i in range(blocks)] + [reduce_mine], 0)
    height = blocks * shard + unit_part
    feed_weights = fsdp_gather(feed_mine).reshape(fsdp_count, height, width)
    expand_blocks = [
        feed_weights[:, i * shard : (i + 1) * shard].reshape(width, width) for i in range(blocks)
    ]
    reduce_whole = feed_weights[:, blocks * shard :].reshape(units // 2, width)

    groups = 2 if image_count % 2 == 0 else 1
    group_images = image_count // groups
    rows = group_images * local_len
    joint_bias = jnp.concatenate(
        [my_heads(bias_q, 0), jnp.zeros((head_width,), F32), my_heads(bias_v, 0)]
    )
    tokens, normed, triples = [], [], []
    for group in range(groups):
        mine = images[group * group_images : (group + 1) * group_images].reshape(rows, width)
        slots = []
        for slot in far_gather(mine):
            slots += [slot, other_core(slot)]
        tokens.append(jnp.stack(slots, 0))
        first_normed, triple = project(
            tokens[-1], small, triple_whole, joint_bias[None]
        )
        normed.append(first_normed)
        triples.append(triple)

    last_slot = ((far_count - 1 - far) % far_count) * 2 + (1 - core)
    dead_from = last_slot * local_len + valid_count - (seq_count - 1) * local_len
    limits = jnp.stack(
        [dead_from, jnp.broadcast_to((last_slot + 1) * local_len, dead_from.shape)], 1
    ).astype(jnp.int32)

    direct = local_len % 8 == 0 and head_width % (2 * HEAD_DIM) == 0

    def to_kernel(array):
        array = array.reshape(seq_count, group_images, local_len, -1)
        if direct:
            return array
        parts = array.shape[-1] // head_width
        array = array.transpose(1, 0, 2, 3).reshape(
            1, group_images, seq_count * local_len, parts, head_width
        )
        lanes = -head_width % (2 * HEAD_DIM)
        array = jnp.pad(array, ((0, 0),) * 4 + ((0, lanes),))
        return array.reshape(1, group_images, seq_count * local_len, -1)

    def from_kernel(array, parts):
        if direct:
            return array.reshape(seq_count, rows, -1)
        array = array.reshape(group_images, seq_count, local_len, parts, -1)
        array = array[..., :head_width].transpose(1, 0, 2, 3, 4)
        return array.reshape(seq_count, rows, parts * head_width)

    kernel_in, kernel_out, kernel_logs, attended_rows, branch_parts = [], [], [], [], []
    for group in range(groups):
        picked = limits[group * group_images : (group + 1) * group_images]
        kernel_in.append(to_kernel(triples[group]))
        attended, logs = attend_forward(kernel_in[-1], picked)
        kernel_out.append(attended)
        kernel_logs.append(logs)
        attended = from_kernel(attended, 1).reshape(far_count, 2 * rows, head_width)
        attended = far_exchange([attended[r] for r in range(far_count)])
        attended_rows.append(jnp.concatenate(attended, 1))
        branch = dot(attended_rows[-1], output_whole)
        branch_parts.append(
            branch[:rows] + other_core(branch[rows:].astype(BF)).astype(F32) + bias_o
        )
    branch_attend = jnp.concatenate(branch_parts, 0)
    inputs = images.reshape(own_rows, width).astype(F32)
    residual = inputs + scale_a * branch_attend
    normal_2, factor_2 = normalize(residual)
    second_mine = (normal_2 * gain_2 + shift_2).astype(BF)
    second_normed = jnp.concatenate([second_mine, other_core(second_mine)], 0)
    activated, slope = expand_rows(second_normed, feed_weights, bias_e)

    cotangent = cotangent.reshape(own_rows, width)
    upstream = cotangent.astype(F32)
    both = jnp.concatenate([cotangent, other_core(cotangent)], 0)
    grad_feed = (scale_f * both.astype(F32)).astype(BF)
    grad_reduce_bias = column_total(grad_feed[:own_rows])
    grad_expanded = (dot_right_t(grad_feed, reduce_whole) * slope.astype(F32)).astype(BF)
    feed_sums = feed_grads(second_normed, activated, grad_expanded, grad_feed, fsdp_count)
    grad_expanded, feed_sums = lax.optimization_barrier((grad_expanded, feed_sums))
    feed_sums = fsdp_scatter(feed_sums.reshape(fsdp_count * height, width))
    partial = sum(
        dot_right_t(grad_expanded[:, i * width : (i + 1) * width], expand_blocks[i])
        for i in range(blocks)
    )
    upper = partial[:own_rows] + other_core(partial[own_rows:].astype(BF)).astype(F32)
    grad_second_gain = jnp.sum(upper * normal_2, 0)
    grad_second_shift = jnp.sum(upper, 0)
    grad_residual = upstream + normalize_back(normal_2, factor_2, upper * gain_2)
    grad_attend_scale = jnp.sum(grad_residual * branch_attend, 0)
    grad_attend = (scale_a * grad_residual).astype(BF)
    grad_output_bias = column_total(grad_attend)
    grad_other = other_core(grad_attend)
    grad_sides = []
    for group in range(groups):
        part = slice(group * rows, (group + 1) * rows)
        grad_sides.append(jnp.concatenate([grad_attend[part], grad_other[part]], 0))
    grad_attended = [
        [
            dot_right_t(side, output_whole[r * head_width : (r + 1) * head_width]).astype(BF)
            for r in range(far_count)
        ]
        for side in grad_sides
    ]
    grad_output_weight = sum(
        dot_left_t(attended_rows[group], grad_sides[group]) for group in range(groups)
    ).astype(BF)
    grad_output_weight = jnp.roll(
        grad_output_weight.reshape(far_count, head_width, width), far, 0
    ).reshape(width // 2, width)

    grad_heads = [to_kernel(jnp.stack(far_exchange(parts), 0)) for parts in grad_attended]
    sent = [part for parts in grad_attended for part in parts]
    branch = dot(after(activated, *sent), reduce_whole)
    grad_expand_bias = column_total(after(grad_expanded, *sent))
    grad_heads[0] = after(grad_heads[0], branch, grad_expand_bias)
    branch_feed = (
        branch[:own_rows] + other_core(branch[own_rows:].astype(BF)).astype(F32) + bias_r
    )
    outputs = residual + scale_f * branch_feed
    grad_feed_scale = jnp.sum(upstream * branch_feed, 0)

    upper_parts, grad_triples = [], []
    grad_first_gain = grad_first_shift = column_sums = 0.0
    for group in range(groups):
        picked = limits[group * group_images : (group + 1) * group_images]
        grad_heads_in = grad_heads[group]
        if group > 0:
            grad_heads_in = after(grad_heads_in, partial)
        grad_triple = from_kernel(
            attend_backward(
                kernel_in[group], kernel_out[group], grad_heads_in, kernel_logs[group], picked
            ),
            3,
        )
        if group > 0:
            grad_triple = after(grad_triple, *moved)
        grad_triples.append(grad_triple)
        partial, gain_part, shift_part, total_part = project_back(
            grad_triple, tokens[group], triple_whole
        )
        grad_first_gain = grad_first_gain + gain_part[0]
        grad_first_shift = grad_first_shift + shift_part[0]
        column_sums = column_sums + total_part[0]
        partial = partial.reshape(far_count, 2, rows, width)
        partial = partial[:, 0].astype(F32) + other_core(partial[:, 1]).astype(F32)
        partial = partial.astype(BF)
        moved = far_exchange([partial[r] for r in range(far_count)])
        upper_parts.append(sum(part.astype(F32) for part in moved))
    grad_triple_weight = sum(
        dot_left_t(
            normed[group].reshape(seq_count * rows, width),
            grad_triples[group].reshape(seq_count * rows, 3 * head_width),
        )
        for group in range(groups)
    ).astype(BF)
    upper = jnp.concatenate(upper_parts, 0)
    normal, factor = normalize(inputs)
    grad_images = grad_residual + normalize_back(normal, factor, upper * gain_1)

    def far_total(array):
        total = array.astype(F32)
        for r in range(1, far_count):
            total = total + far_send(array, r).astype(F32)
        return total

    def place_heads(vector):
        here = jnp.arange(far_count)[:, None, None, None] == far
        here = here & (jnp.arange(2)[None, None, :, None] == core)
        vector = vector.reshape(1, near_heads, 1, HEAD_DIM)
        return jnp.where(here, vector, 0.0).reshape(width)

    def place_units(vector):
        vector = vector.reshape(fsdp_count, shard, bias_columns)
        vector = vector.transpose(2, 0, 1).reshape(1, bias_columns, width)
        vector = jnp.where(jnp.arange(2)[:, None, None] == core, vector, 0.0)
        return [vector[i, j] for i in range(2) for j in range(bias_columns)]

    sums = [
        grad_first_gain, grad_first_shift,
        place_heads(column_sums[:head_width]), place_heads(column_sums[2 * head_width :]),
        grad_output_bias, grad_attend_scale, grad_second_gain, grad_second_shift,
        grad_reduce_bias, grad_feed_scale,
    ] + place_units(grad_expand_bias)
    sums = jnp.stack(sums, 0).astype(BF).T
    sums = jnp.pad(sums, ((0, 0), (0, -sums.shape[1] % 128)))
    grad_output_weight = grad_output_weight.reshape(fsdp_count, shard // 2, 2, width // 2)
    grad_output_weight = grad_output_weight.transpose(0, 2, 1, 3).reshape(width, width // 2)
    grad_triple_weight = after(grad_triple_weight, partial)
    grad_packed = jnp.concatenate([grad_triple_weight, sums, grad_output_weight], 1)
    grad_packed = ring_scatter(grad_packed.reshape(fsdp_count, shard, -1)).astype(BF)
    feed_sums = far_total(feed_sums).astype(BF)
    grad_packed = after(grad_packed, feed_sums, *moved)
    grad_packed = jnp.roll(jnp.stack(far_gather(grad_packed), 0), far, 0)
    grad_packed = core_join(grad_packed, 1, core)
    grad_triple_weight = (
        grad_packed[:, :, :, :first]
        .reshape(far_count, 2, shard, 3, near_heads, HEAD_DIM)
        .transpose(2, 3, 0, 4, 1, 5)
        .reshape(shard, 3 * width)
        .astype(F32)
    )
    sums = jnp.sum(grad_packed[:, :, :, first : first + 16].astype(F32), (0, 1)).T
    grad_output_weight = (
        jnp.sum(grad_packed[:, :, :, second:].astype(F32), 0)
        .reshape(2, 2, pairs, HEAD_DIM, width // 2)
        .transpose(2, 0, 3, 1, 4)
        .reshape(shard, width)
    )

    feed_sums = core_join(feed_sums, 0, core).astype(F32)
    grad_expand_weight = (
        feed_sums[:, : blocks * shard]
        .reshape(2, blocks, shard, -1, unit_part)
        .transpose(2, 1, 3, 0, 4)
        .reshape(shard, units)
    )
    grad_reduce_weight = feed_sums[:, blocks * shard :].reshape(2 * unit_part, width)
    grad_expand_bias = (
        sums[10 : 10 + 2 * bias_columns]
        .reshape(2, bias_columns, shard)
        .transpose(0, 2, 1)
        .reshape(2 * unit_part)
    )
    return (
        outputs.reshape(image_count, local_len, width).astype(BF),
        grad_images.reshape(image_count, local_len, width),
        sums[0],
        sums[1],
        grad_triple_weight,
        sums[2],
        sums[3],
        grad_output_weight,
        sums[4],
        sums[5],
        sums[6],
        sums[7],
        grad_expand_weight,
        grad_expand_bias,
        grad_reduce_weight,
        sums[8],
        sums[9],
    )


def layer_norm(inputs, gain, shift):
    average = jnp.mean(inputs, -1, keepdims=True)
    centered = inputs - average
    variance = jnp.mean(centered * centered, -1, keepdims=True)
    return centered * lax.rsqrt(variance + EPSILON) * gain + shift


def exact_gelu(values):
    return jax.nn.gelu(values, approximate=False)


def to_float(array):
    return array.astype(jnp.float32)


def plain_matmul(left, right):
    return jnp.dot(left, right, preferred_element_type=jnp.float32)


def plain_matmul_left_t(left, right):
    return lax.dot_general(
        left, right, (((0,), (0,)), ((), ())), preferred_element_type=jnp.float32
    )


def plain_matmul_right_t(left, right):
    return lax.dot_general(
        left, right, (((1,), (1,)), ((), ())), preferred_element_type=jnp.float32
    )


def plain_column_total(array):
    return plain_matmul(jnp.ones((1, array.shape[0]), jnp.bfloat16), array)[0]


def masked_scores(queries, key_rows, live_count, factor):
    scores = (
        jnp.einsum("qhd,khd->hqk", queries, key_rows, preferred_element_type=jnp.float32) * factor
    )
    live_keys = lax.broadcasted_iota(jnp.int32, (1, 1, key_rows.shape[0]), 2) < live_count
    return jnp.where(live_keys, scores, -1e30)


def plain_attend_forward(bundle):
    packed, live_count = bundle
    length, triple_count, local_width = packed.shape
    head_count = local_width // HEAD_DIM
    unpacked = packed.reshape(length, triple_count, head_count, HEAD_DIM)
    factor = HEAD_DIM ** (-0.5)
    scores = masked_scores(unpacked[:, 0], unpacked[:, 1], live_count, factor)
    highest = jnp.max(scores, -1, keepdims=True)
    powers = jnp.exp(scores - highest)
    row_total = jnp.sum(powers, -1, keepdims=True)
    weights_low = (powers / row_total).astype(jnp.bfloat16)
    mixed_rows = jnp.einsum(
        "hqk,khd->qhd", weights_low, unpacked[:, 2], preferred_element_type=jnp.float32
    )
    logsum = highest + jnp.log(row_total)
    return (mixed_rows.reshape(length, local_width).astype(jnp.bfloat16), logsum)


def plain_attend_backward(bundle):
    packed, grad_mixed, logsum, live_count = bundle
    length, triple_count, local_width = packed.shape
    head_count = local_width // HEAD_DIM
    unpacked = packed.reshape(length, triple_count, head_count, HEAD_DIM)
    factor = HEAD_DIM ** (-0.5)
    scores = masked_scores(unpacked[:, 0], unpacked[:, 1], live_count, factor)
    probs = jnp.exp(scores - logsum)
    grad_heads = grad_mixed.reshape(length, head_count, HEAD_DIM)
    grad_probs = jnp.einsum(
        "qhd,khd->hqk", grad_heads, unpacked[:, 2], preferred_element_type=jnp.float32
    )
    grad_values = jnp.einsum(
        "hqk,qhd->khd", probs.astype(jnp.bfloat16), grad_heads, preferred_element_type=jnp.float32
    )
    inner = jnp.sum(probs * grad_probs, -1, keepdims=True)
    grad_scores = (probs * (grad_probs - inner)).astype(jnp.bfloat16)
    grad_queries = (
        jnp.einsum("hqk,khd->qhd", grad_scores, unpacked[:, 1], preferred_element_type=jnp.float32)
        * factor
    )
    grad_keys = (
        jnp.einsum("hqk,qhd->khd", grad_scores, unpacked[:, 0], preferred_element_type=jnp.float32)
        * factor
    )
    stacked = jnp.stack([grad_queries, grad_keys, grad_values], 1)
    return stacked.reshape(length, triple_count, local_width).astype(jnp.bfloat16)


def plain_shards(
    images,
    cotangent,
    valid_count,
    first_gain,
    first_shift,
    triple_weight,
    query_bias,
    value_bias,
    output_weight,
    output_bias,
    attend_scale,
    second_gain,
    second_shift,
    expand_weight,
    expand_bias,
    reduce_weight,
    reduce_bias,
    feed_scale,
):
    image_count, local_len, width = images.shape
    gathered = (
        lax.all_gather(first_gain, "fsdp", axis=0, tiled=True),
        lax.all_gather(first_shift, "fsdp", axis=0, tiled=True),
        lax.all_gather(triple_weight, "fsdp", axis=0, tiled=True),
        lax.all_gather(query_bias, "fsdp", axis=0, tiled=True),
        lax.all_gather(value_bias, "fsdp", axis=0, tiled=True),
        lax.all_gather(output_weight, "fsdp", axis=0, tiled=True),
        lax.all_gather(output_bias, "fsdp", axis=0, tiled=True),
        lax.all_gather(attend_scale, "fsdp", axis=0, tiled=True),
        lax.all_gather(second_gain, "fsdp", axis=0, tiled=True),
        lax.all_gather(second_shift, "fsdp", axis=0, tiled=True),
        lax.all_gather(expand_weight, "fsdp", axis=0, tiled=True),
        lax.all_gather(expand_bias, "fsdp", axis=0, tiled=True),
        lax.all_gather(reduce_weight, "fsdp", axis=0, tiled=True),
        lax.all_gather(reduce_bias, "fsdp", axis=0, tiled=True),
        lax.all_gather(feed_scale, "fsdp", axis=0, tiled=True),
    )
    inputs = images.astype(jnp.float32).reshape(-1, width)
    first_normed = layer_norm(inputs, to_float(gathered[0]), to_float(gathered[1])).astype(
        jnp.bfloat16
    )
    joint_bias = to_float(jnp.concatenate([gathered[3], jnp.zeros_like(gathered[3]), gathered[4]]))
    triple = (plain_matmul(first_normed, gathered[2]) + joint_bias).astype(jnp.bfloat16)
    triple = triple.reshape(image_count, local_len, 3, width)
    by_heads = lax.all_to_all(triple, "seq", split_axis=3, concat_axis=1, tiled=True)
    attended, logsums = lax.map(plain_attend_forward, (by_heads, valid_count))
    by_tokens = lax.all_to_all(attended, "seq", split_axis=1, concat_axis=2, tiled=True)
    attended_rows = by_tokens.reshape(-1, width)
    branch_attend = plain_matmul(attended_rows, gathered[5]) + to_float(gathered[6])
    residual = inputs + to_float(gathered[7]) * branch_attend
    second_normed = layer_norm(residual, to_float(gathered[8]), to_float(gathered[9])).astype(
        jnp.bfloat16
    )
    expanded = plain_matmul(second_normed, gathered[10]) + to_float(gathered[11])
    activated = exact_gelu(expanded).astype(jnp.bfloat16)
    branch_feed = plain_matmul(activated, gathered[12]) + to_float(gathered[13])
    outputs = residual + to_float(gathered[14]) * branch_feed
    weights = (
        lax.all_gather(first_gain, "fsdp", axis=0, tiled=True),
        lax.all_gather(first_shift, "fsdp", axis=0, tiled=True),
        lax.all_gather(triple_weight, "fsdp", axis=0, tiled=True),
        lax.all_gather(query_bias, "fsdp", axis=0, tiled=True),
        lax.all_gather(value_bias, "fsdp", axis=0, tiled=True),
        lax.all_gather(output_weight, "fsdp", axis=0, tiled=True),
        lax.all_gather(output_bias, "fsdp", axis=0, tiled=True),
        lax.all_gather(attend_scale, "fsdp", axis=0, tiled=True),
        lax.all_gather(second_gain, "fsdp", axis=0, tiled=True),
        lax.all_gather(second_shift, "fsdp", axis=0, tiled=True),
        lax.all_gather(expand_weight, "fsdp", axis=0, tiled=True),
        lax.all_gather(expand_bias, "fsdp", axis=0, tiled=True),
        lax.all_gather(reduce_weight, "fsdp", axis=0, tiled=True),
        lax.all_gather(reduce_bias, "fsdp", axis=0, tiled=True),
        lax.all_gather(feed_scale, "fsdp", axis=0, tiled=True),
    )
    upstream = cotangent.astype(jnp.float32).reshape(-1, width)
    grad_feed_scale = jnp.sum(upstream * branch_feed, 0)
    grad_feed = (to_float(weights[14]) * upstream).astype(jnp.bfloat16)
    grad_reduce_bias = plain_column_total(grad_feed)
    grad_reduce_weight = plain_matmul_left_t(activated, grad_feed)
    grad_activated = plain_matmul_right_t(grad_feed, weights[12])
    unused, gelu_pull = jax.vjp(exact_gelu, expanded)
    grad_expanded = gelu_pull(grad_activated)[0].astype(jnp.bfloat16)
    grad_expand_bias = plain_column_total(grad_expanded)
    grad_expand_weight = plain_matmul_left_t(second_normed, grad_expanded)
    grad_second_normed = plain_matmul_right_t(grad_expanded, weights[10])
    unused, second_pull = jax.vjp(layer_norm, residual, to_float(weights[8]), to_float(weights[9]))
    grad_residual_norm, grad_second_gain, grad_second_shift = second_pull(grad_second_normed)
    grad_residual = upstream + grad_residual_norm
    grad_attend_scale = jnp.sum(grad_residual * branch_attend, 0)
    grad_attend = (to_float(weights[7]) * grad_residual).astype(jnp.bfloat16)
    grad_output_bias = plain_column_total(grad_attend)
    grad_output_weight = plain_matmul_left_t(attended_rows, grad_attend)
    grad_attended = plain_matmul_right_t(grad_attend, weights[5]).astype(jnp.bfloat16)
    grad_attended = grad_attended.reshape(image_count, local_len, width)
    grad_by_heads = lax.all_to_all(grad_attended, "seq", split_axis=2, concat_axis=1, tiled=True)
    grad_triple_heads = lax.map(plain_attend_backward, (by_heads, grad_by_heads, logsums, valid_count))
    grad_triple = lax.all_to_all(grad_triple_heads, "seq", split_axis=1, concat_axis=3, tiled=True)
    grad_triple = grad_triple.reshape(-1, 3 * width)
    column_sums = plain_column_total(grad_triple)
    grad_query_bias = column_sums[:width]
    grad_value_bias = column_sums[2 * width :]
    grad_triple_weight = plain_matmul_left_t(first_normed, grad_triple)
    grad_first_normed = plain_matmul_right_t(grad_triple, weights[2])
    unused, first_pull = jax.vjp(layer_norm, inputs, to_float(weights[0]), to_float(weights[1]))
    grad_inputs_norm, grad_first_gain, grad_first_shift = first_pull(grad_first_normed)
    grad_images = grad_residual + grad_inputs_norm
    owned = (
        lax.psum_scatter(
            grad_first_gain.astype(jnp.bfloat16), "fsdp", scatter_dimension=0, tiled=True
        ).astype(jnp.float32),
        lax.psum_scatter(
            grad_first_shift.astype(jnp.bfloat16), "fsdp", scatter_dimension=0, tiled=True
        ).astype(jnp.float32),
        lax.psum_scatter(
            grad_triple_weight.astype(jnp.bfloat16), "fsdp", scatter_dimension=0, tiled=True
        ).astype(jnp.float32),
        lax.psum_scatter(
            grad_query_bias.astype(jnp.bfloat16), "fsdp", scatter_dimension=0, tiled=True
        ).astype(jnp.float32),
        lax.psum_scatter(
            grad_value_bias.astype(jnp.bfloat16), "fsdp", scatter_dimension=0, tiled=True
        ).astype(jnp.float32),
        lax.psum_scatter(
            grad_output_weight.astype(jnp.bfloat16), "fsdp", scatter_dimension=0, tiled=True
        ).astype(jnp.float32),
        lax.psum_scatter(
            grad_output_bias.astype(jnp.bfloat16), "fsdp", scatter_dimension=0, tiled=True
        ).astype(jnp.float32),
        lax.psum_scatter(
            grad_attend_scale.astype(jnp.bfloat16), "fsdp", scatter_dimension=0, tiled=True
        ).astype(jnp.float32),
        lax.psum_scatter(
            grad_second_gain.astype(jnp.bfloat16), "fsdp", scatter_dimension=0, tiled=True
        ).astype(jnp.float32),
        lax.psum_scatter(
            grad_second_shift.astype(jnp.bfloat16), "fsdp", scatter_dimension=0, tiled=True
        ).astype(jnp.float32),
        lax.psum_scatter(
            grad_expand_weight.astype(jnp.bfloat16), "fsdp", scatter_dimension=0, tiled=True
        ).astype(jnp.float32),
        lax.psum_scatter(
            grad_expand_bias.astype(jnp.bfloat16), "fsdp", scatter_dimension=0, tiled=True
        ).astype(jnp.float32),
        lax.psum_scatter(
            grad_reduce_weight.astype(jnp.bfloat16), "fsdp", scatter_dimension=0, tiled=True
        ).astype(jnp.float32),
        lax.psum_scatter(
            grad_reduce_bias.astype(jnp.bfloat16), "fsdp", scatter_dimension=0, tiled=True
        ).astype(jnp.float32),
        lax.psum_scatter(
            grad_feed_scale.astype(jnp.bfloat16), "fsdp", scatter_dimension=0, tiled=True
        ).astype(jnp.float32),
    )
    summed = lax.psum(
        (
            owned[0],
            owned[1],
            owned[2],
            owned[3],
            owned[4],
            owned[5],
            owned[6],
            owned[7],
            owned[8],
            owned[9],
            owned[10],
            owned[11],
            owned[12],
            owned[13],
            owned[14],
        ),
        "seq",
    )
    return (
        outputs.reshape(image_count, local_len, width).astype(jnp.bfloat16),
        grad_images.reshape(image_count, local_len, width),
        summed[0],
        summed[1],
        summed[2],
        summed[3],
        summed[4],
        summed[5],
        summed[6],
        summed[7],
        summed[8],
        summed[9],
        summed[10],
        summed[11],
        summed[12],
        summed[13],
        summed[14],
    )


def solution(mesh):
    fsdp, seq = mesh.devices.shape
    if seq == 4 and fsdp == 8:
        plan, tokens = shards, P("fsdp", ("far", "core"), None)
        mesh = Mesh(mesh.devices.reshape(fsdp, 2, 2), ("fsdp", "far", "core"))
    else:
        plan, tokens = plain_shards, P("fsdp", "seq", None)
    row, matrix = P("fsdp"), P("fsdp", None)
    return jax.shard_map(
        plan,
        mesh=mesh,
        in_specs=(
            tokens, tokens, row, row, row, matrix, row, row, matrix,
            row, row, row, row, matrix, row, matrix, row, row,
        ),
        out_specs=(
            tokens, tokens, row, row, matrix, row, row, matrix,
            row, row, row, row, matrix, row, matrix, row, row,
        ),
        check_vma=False,
    )
```
